32 devices in a mesh: rows: 4 (over y, core), tok: 8 (over z, x).
Axes of the slice: x: 2, y: 2, z: 4, core: 2. Of those that a mesh axis runs over, the one named last changes fastest.
Arguments:
- tokens_in: bfloat16 [28, 512, 64], P('rows', 'tok'), may hold values from -6 to 6
- segments: int32 [28, 512], P('rows', 'tok'), may hold values from 0 to 3, as said below
- landmark_index: int32 [28, 2, 128], P('rows'), may hold values from 0 to 1023
- ln1_gain: bfloat16 [64], replicated, may hold values from 0.5 to 1.5
- ln1_bias: bfloat16 [64], replicated, may hold values from -3 to 3
- w_query: bfloat16 [64, 64], replicated, may hold values from -0.375 to 0.375
- b_query: bfloat16 [64], replicated, may hold values from -1.5 to 1.5
- w_key: bfloat16 [64, 64], replicated, may hold values from -0.375 to 0.375
- b_key: bfloat16 [64], replicated, may hold values from -1.5 to 1.5
- w_value: bfloat16 [64, 64], replicated, may hold values from -0.75 to 0.75
- b_value: bfloat16 [64], replicated, may hold values from -3 to 3
- w_out: bfloat16 [64, 64], replicated, may hold values from -1.5 to 1.5
- b_out: bfloat16 [64], replicated, may hold values from -3 to 3
- ln2_gain: bfloat16 [64], replicated, may hold values from 0.5 to 1.5
- ln2_bias: bfloat16 [64], replicated, may hold values from -3 to 3
- w_up: bfloat16 [64, 128], replicated, may hold values from -0.75 to 0.75
- b_up: bfloat16 [128], replicated, may hold values from -3 to 3
- w_down: bfloat16 [128, 64], replicated, may hold values from -0.5 to 0.5
- b_down: bfloat16 [64], replicated, may hold values from -3 to 3
- grad_out: bfloat16 [28, 512, 64], P('rows', 'tok'), may hold values from -6 to 6
Outputs:
- layer_out: bfloat16 [28, 512, 64], P('rows', 'tok')
- grad_input: float32 [28, 512, 64], P('rows', 'tok')
- grad_ln1_gain: float32 [64], replicated
- grad_ln1_bias: float32 [64], replicated
- grad_w_query: float32 [64, 64], replicated
- grad_b_query: float32 [64], replicated
- grad_w_key: float32 [64, 64], replicated
- grad_b_key: float32 [64], replicated
- grad_w_value: float32 [64, 64], replicated
- grad_b_value: float32 [64], replicated
- grad_w_out: float32 [64, 64], replicated
- grad_b_out: float32 [64], replicated
- grad_ln2_gain: float32 [64], replicated
- grad_ln2_bias: float32 [64], replicated
- grad_w_up: float32 [64, 128], replicated
- grad_b_up: float32 [128], replicated
- grad_w_down: float32 [128, 64], replicated
- grad_b_down: float32 [64], replicated
The draws below stay inside these ranges and needn't reach their ends.
Inputs may be any that keep to these rules, and one draw needn't show every extreme that they name: Ids never fall along a row and no segment is empty. In one row of each aligned block of 7 rows the ids are 0, 1, 2, segment 1 beginning within the first 64 tokens and ending within the last 64; every other row holds segments 0 to 3, boundary k (k = 1, 2, 3) lying within 64 tokens of k * 128.
All inputs are finite; a program needn't handle non-finite values.
Results may differ from the reference program's by a relative error of at most 0.013.
Values may be sent and summed in bfloat16 or wider, within the bound.
No kernel may reach another device: no remote copies, remote signals or barrier semaphores. Data moves between devices by JAX's collectives and lax.ppermute only.
A program may use at most 64 MiB of HBM per device.

```python
import jax
import jax.numpy as jnp
from jax import lax

D = 64
HEADS = 2
FFN = 128
LMK = 128
NS_STEPS = 6
ROWS_DEV = 7
TOK_ROW = 64
ROWS = 28
ROW_LEN = 512


def draw_segments(key, part):
    key = jax.random.fold_in(key, 11)
    pick_key, begin_key, finish_key, cut_key = jax.random.split(key, 4)
    groups = ROWS // ROWS_DEV
    chosen = jax.random.randint(pick_key, (groups, 1), 0, ROWS_DEV)
    spanning = (jnp.arange(ROWS_DEV, dtype=jnp.int32)[None, :] == chosen).reshape(ROWS, 1)
    positions = jnp.arange(ROW_LEN, dtype=jnp.int32)[None, :]
    begins = jax.random.randint(begin_key, (ROWS, 1), 1, TOK_ROW)
    finishes = jax.random.randint(finish_key, (ROWS, 1), ROW_LEN - TOK_ROW + 1, ROW_LEN)
    span_ids = (positions >= begins).astype(jnp.int32) + (positions >= finishes).astype(jnp.int32)
    half_band = ROW_LEN // 8
    centres = jnp.arange(1, 4, dtype=jnp.int32)[None, :] * (ROW_LEN // 4)
    cuts = centres + jax.random.randint(cut_key, (ROWS, 3), -half_band, half_band)
    packed_ids = jnp.sum((positions[:, :, None] >= cuts[:, None, :]).astype(jnp.int32), axis=-1)
    return jnp.where(spanning, span_ids, packed_ids).astype(jnp.int32)


def set_ends(entries, rng, low, largest):
    spot = [jax.random.randint(jax.random.fold_in(rng, axis), (), 0, length) for axis, length in enumerate(entries.shape)]
    longest = entries.shape.index(max(entries.shape))
    next_to = spot[:longest] + [(spot[longest] + 1) % entries.shape[longest]] + spot[longest + 1:]
    return entries.at[tuple(spot)].set(low).at[tuple(next_to)].set(largest)


def block_scale(key, extent, shards, least, largest):
    def one(position, parts):
        steps = jax.random.uniform(jax.random.fold_in(jax.random.fold_in(key, 6), position), (parts,), jnp.float32, least / len(shards), largest / len(shards))
        return jnp.repeat(jnp.exp(steps), extent[position] // parts).reshape((-1,) + (1,) * (len(extent) - position - 1))

    factor_of = one(*shards[0])
    for cut in shards[1:]:
        factor_of = factor_of * one(*cut)
    return factor_of


def normal_values(stream_key, extent, deviation, bound, cuts=(), held_as=jnp.bfloat16):
    entries = deviation * jax.random.normal(stream_key, extent, jnp.float32)
    if cuts:
        entries = entries * block_scale(stream_key, extent, cuts, -0.22, 0.18)
    return jnp.clip(entries, -bound, bound).astype(held_as)


def setup_inputs(seed: int = 0) -> dict:
    streams_of = jax.random.split(jax.random.key(seed), 21)
    tokens_in = normal_values(streams_of[0], (ROWS, ROW_LEN, D), 1.0, 6.0, ((0, 4), (1, 8)))
    segments = draw_segments(jax.random.fold_in(streams_of[20], 71), 0)
    landmark_index = set_ends(jax.random.randint(streams_of[2], (ROWS, HEADS, LMK), 0, 2 * ROW_LEN), jax.random.fold_in(streams_of[2], 1), 0, (2 * ROW_LEN) - 1).astype(jnp.int32)
    ln1_gain = jnp.clip(1.0 + 0.1 * jax.random.normal(streams_of[3], (D,), jnp.float32), 0.5, 1.5).astype(jnp.bfloat16)
    ln1_bias = normal_values(streams_of[4], (D,), 0.3, 3.0)
    w_query = normal_values(streams_of[5], (D, D), (4 * D) ** -0.5, 0.375)
    b_query = normal_values(streams_of[6], (D,), 0.15, 1.5)
    w_key = normal_values(streams_of[7], (D, D), (4 * D) ** -0.5, 0.375)
    b_key = normal_values(streams_of[8], (D,), 0.15, 1.5)
    w_value = normal_values(streams_of[9], (D, D), D ** -0.5, 0.75)
    b_value = normal_values(streams_of[10], (D,), 0.3, 3.0)
    w_out = normal_values(streams_of[11], (D, D), (D // 4) ** -0.5, 1.5)
    b_out = normal_values(streams_of[12], (D,), 0.3, 3.0)
    ln2_gain = jnp.clip(1.0 + 0.1 * jax.random.normal(streams_of[13], (D,), jnp.float32), 0.5, 1.5).astype(jnp.bfloat16)
    ln2_bias = normal_values(streams_of[14], (D,), 0.3, 3.0)
    w_up = normal_values(streams_of[15], (D, FFN), D ** -0.5, 0.75)
    b_up = normal_values(streams_of[16], (FFN,), 0.3, 3.0)
    w_down = normal_values(streams_of[17], (FFN, D), FFN ** -0.5, 0.5)
    b_down = normal_values(streams_of[18], (D,), 0.3, 3.0)
    grad_out = normal_values(streams_of[19], (ROWS, ROW_LEN, D), 1.0, 6.0, ((0, 4), (1, 8)))
    return dict(tokens_in=tokens_in, segments=segments, landmark_index=landmark_index, ln1_gain=ln1_gain, ln1_bias=ln1_bias, w_query=w_query, b_query=b_query, w_key=w_key, b_key=b_key, w_value=w_value, b_value=b_value, w_out=w_out, b_out=b_out, ln2_gain=ln2_gain, ln2_bias=ln2_bias, w_up=w_up, b_up=b_up, w_down=w_down, b_down=b_down, grad_out=grad_out)


highest_precision = lax.Precision.HIGHEST
eps = 1e-05
ridge = 0.1

@jax.custom_vjp
def lowrank_factor(v):
    return lax.optimization_barrier(v.astype(jnp.bfloat16)).astype(jnp.float32)

@jax.custom_vjp
def lowrank_gradient(v):
    return v

def low_keep(v):
    return (lowrank_factor(v), None)

def low_pass(kept, grad):
    return (grad,)

def back_keep(v):
    return (v, None)

def back_low(kept, grad):
    return (lowrank_factor(grad),)
lowrank_factor.defvjp(low_keep, low_pass)
lowrank_gradient.defvjp(back_keep, back_low)

def norm_layer(values, gain_vec, shift_vec):
    centre = values - lax.optimization_barrier(jnp.mean(values, axis=-1, keepdims=True))
    spread = lax.optimization_barrier(jnp.mean(centre * centre, axis=-1, keepdims=True))
    return centre * lax.rsqrt(spread + eps) * gain_vec + shift_vec

def kernel_rows(points, landmarks, sharpness):
    inner_part = jnp.einsum('...td,...md->...tm', points, landmarks, precision=highest_precision)
    point_half = 0.5 * lax.optimization_barrier(jnp.sum(points * points, axis=-1))
    mark_half = 0.5 * lax.optimization_barrier(jnp.sum(landmarks * landmarks, axis=-1))
    return jnp.exp(sharpness * (inner_part - point_half[..., :, None] - mark_half[..., None, :]))

def pseudo_inverse(landmarks, same_mark, sharpness):
    mark_count = landmarks.shape[-2]
    kernel = kernel_rows(landmarks, landmarks, sharpness) * same_mark + ridge * jnp.eye(mark_count, dtype=jnp.float32)
    widest = lax.optimization_barrier(jnp.max(lax.optimization_barrier(jnp.sum(kernel, axis=-1)), axis=-1))
    approx = kernel / (widest * widest)[..., None, None]
    for repeat_idx in range(NS_STEPS):
        middle = jnp.einsum('...ij,...jk->...ik', approx, kernel, precision=highest_precision)
        approx = 2.0 * approx - jnp.einsum('...ij,...jk->...ik', middle, approx, precision=highest_precision)
    return approx

def layer_row(param_set, row_in, seg_row, index_row):
    gain1, bias1, wq_mat, bq_vec, wk_mat, bk_vec, wv_mat, bv_vec, wo_mat, bo_vec, gain2, bias2, wup_mat, bup_vec, wdown_mat, bdown_vec = param_set
    length_total = row_in.shape[0]
    head_count = index_row.shape[0]
    model_width = wq_mat.shape[0]
    head_size = model_width // head_count
    sharpness = head_size ** (-0.5)
    normed = lowrank_factor(norm_layer(row_in, gain1, bias1))

    def project(weight, shift_vec):
        made = lowrank_gradient(lowrank_factor(jnp.dot(normed, weight, precision=highest_precision) + shift_vec))
        return made.reshape(length_total, head_count, head_size).transpose(1, 0, 2)
    query = project(wq_mat, bq_vec)
    key_vec = project(wk_mat, bk_vec)
    value_rows = project(wv_mat, bv_vec)
    joined = jnp.concatenate([query, key_vec], axis=1)
    landmarks = jnp.take_along_axis(joined, index_row[:, :, None], axis=1)
    mark_seg = jnp.concatenate([seg_row, seg_row])[index_row]
    same_tok = (seg_row[None, :, None] == mark_seg[:, None, :]).astype(jnp.float32)
    same_mark = (mark_seg[:, :, None] == mark_seg[:, None, :]).astype(jnp.float32)
    nearby_query_kernel = lowrank_gradient(lowrank_factor(kernel_rows(query, landmarks, sharpness) * same_tok))
    nearby_key_kernel = lowrank_gradient(lowrank_factor(kernel_rows(key_vec, landmarks, sharpness) * same_tok))
    summed_output = lowrank_gradient(jnp.einsum('pfw,pfa->pwa', nearby_key_kernel, value_rows, precision=highest_precision))
    inverse_matrix = pseudo_inverse(landmarks, same_mark, sharpness)
    mixed_value = lowrank_gradient(lowrank_factor(jnp.einsum('woi,wil->wol', inverse_matrix, summed_output, precision=highest_precision)))
    attention_result = jnp.einsum('xog,xgk->xok', nearby_query_kernel, mixed_value, precision=highest_precision) * length_total ** (-0.5)
    attention_result = lowrank_gradient(lowrank_factor(attention_result)).transpose(1, 0, 2).reshape(length_total, model_width)
    hidden = row_in + lowrank_gradient(jnp.dot(attention_result, wo_mat, precision=highest_precision) + bo_vec)
    normed2 = lowrank_factor(norm_layer(hidden, gain2, bias2))
    inner_pre = lowrank_gradient(jnp.dot(normed2, wup_mat, precision=highest_precision) + bup_vec)
    activated = lowrank_factor(jax.nn.gelu(inner_pre))
    return hidden + lowrank_gradient(jnp.dot(activated, wdown_mat, precision=highest_precision) + bdown_vec)

def reference(tokens_in, segments, landmark_index, ln1_gain, ln1_bias, w_query, b_query, w_key, b_key, w_value, b_value, w_out, b_out, ln2_gain, ln2_bias, w_up, b_up, w_down, b_down, grad_out):
    param_set = tuple((item.astype(jnp.float32) for item in (ln1_gain, ln1_bias, w_query, b_query, w_key, b_key, w_value, b_value, w_out, b_out, ln2_gain, ln2_bias, w_up, b_up, w_down, b_down)))

    def one_row(running, row_data):
        row_in, seg_row, index_row, cot_row = row_data

        def forward(params_now, values_now):
            return layer_row(params_now, values_now, seg_row, index_row)
        row_out, pull_back = jax.vjp(forward, param_set, row_in.astype(jnp.float32))
        grad_params, grad_row = pull_back(cot_row.astype(jnp.float32))
        running = jax.tree.map(jnp.add, running, grad_params)
        return (running, (row_out.astype(jnp.bfloat16), grad_row))
    zero_set = jax.tree.map(jnp.zeros_like, param_set)
    totals, (outputs, grad_rows) = lax.scan(one_row, zero_set, (tokens_in, segments, landmark_index, grad_out))
    return (outputs, grad_rows, totals[0], totals[1], totals[2], totals[3], totals[4], totals[5], totals[6], totals[7], totals[8], totals[9], totals[10], totals[11], totals[12], totals[13], totals[14], totals[15])
```

```python
from functools import partial

import jax
import jax.numpy as jnp
from jax import lax
from jax.experimental import pallas as pl
from jax.experimental.pallas import tpu as pltpu
from jax.sharding import PartitionSpec as P


NS_STEPS = 6
EPS = 1e-05
RIDGE = 0.1
FAR = 640.0
SEG_ROWS = 16
GRAD_ROWS = 272

f32 = jnp.float32
bf16 = jnp.bfloat16


def mm(a, b):
    return lax.dot_general(a, b, (((1,), (0,)), ((), ())), preferred_element_type=f32)


def mm_nt(a, b):
    return lax.dot_general(a, b, (((1,), (1,)), ((), ())), preferred_element_type=f32)


def mm_tn(a, b):
    return lax.dot_general(a, b, (((0,), (0,)), ((), ())), preferred_element_type=f32)


def split(a):
    hi = a.astype(bf16)
    return hi, (a - hi.astype(f32)).astype(bf16)


def wide_right(b):
    hi, lo = split(b)
    return jnp.concatenate(
        [jnp.concatenate([hi, lo], 1), jnp.concatenate([hi, jnp.zeros_like(hi)], 1)], 0
    )


def mm_wide(a, wide):
    n = wide.shape[1] // 2
    both = mm(jnp.concatenate(split(a), 1), wide)
    return both[:, :n] + both[:, n:]


def row_sum(a):
    return jnp.sum(a, axis=1, keepdims=True)


def col_sum(a):
    return jnp.sum(a, axis=0, keepdims=True)


def norm_stats(values):
    centre = values - row_sum(values) * (1.0 / values.shape[1])
    spread = row_sum(centre * centre) * (1.0 / values.shape[1])
    scale = lax.rsqrt(spread + EPS)
    return centre * scale, scale


def norm_back(d_norm, xhat, scale, gain):
    scaled = d_norm * gain
    n = 1.0 / scaled.shape[1]
    return scale * (scaled - row_sum(scaled) * n - xhat * (row_sum(scaled * xhat) * n))


def iota(shape, dim):
    return lax.broadcasted_iota(jnp.int32, shape, dim)


def row_work(xg, onehot_t, idx, par):
    (gain1, bias1, wq, bq, wk, bk, wv, bv, wo, bo, gain2, bias2, wup, bup, wdown, bdown) = par
    tokens = xg.shape[0]
    width = wq.shape[0]
    heads, marks = idx.shape
    size = width // heads
    sharp = size**-0.5
    out_scale = tokens**-0.5
    hm = heads * marks
    lane = iota((tokens, 128), 1)
    low = lane < width

    def vec(v):
        return v.astype(f32)

    x = xg[:, :width].astype(f32)
    g16 = xg[:, width:]
    g = g16.astype(f32)
    xhat1, scale1 = norm_stats(x)
    normed = (xhat1 * vec(gain1) + vec(bias1)).astype(bf16)

    q2 = (mm(normed, jnp.concatenate([wq, wq], 1)) + vec(jnp.concatenate([bq, bq], 1))).astype(bf16)
    k2 = (mm(normed, jnp.concatenate([wk, wk], 1)) + vec(jnp.concatenate([bk, bk], 1))).astype(bf16)
    v = (mm(normed, wv) + vec(bv)).astype(bf16)
    q_t = q2.astype(f32).T[:width].astype(bf16)
    k_t = k2.astype(f32).T[:width].astype(bf16)
    v_t = v.astype(f32).T.astype(bf16)
    qk_t = jnp.concatenate([q_t, k_t], 1)

    place = (iota((SEG_ROWS, 128), 1) == iota((SEG_ROWS, 128), 0) + width).astype(f32).astype(bf16)
    seg_lanes = mm_tn(onehot_t, place)
    feat = jnp.where((lane >= width + 4) & (lane < width + 8), 1.0, seg_lanes)

    def features(p2):
        p = p2.astype(f32)
        sq = p * p
        hi = sq.astype(bf16).astype(f32)
        return jnp.concatenate(
            [jnp.where(low, p, hi).astype(bf16), jnp.where(low, sq - hi, feat).astype(bf16)], 1
        )

    feats = jnp.concatenate([features(q2), features(k2)], 0)

    idx_row = jnp.concatenate([idx[h : h + 1] for h in range(heads)], 1)
    pick_t = (iota((2 * tokens, hm), 0) == idx_row).astype(f32).astype(bf16)
    seg2 = jnp.concatenate([onehot_t, onehot_t], 1)
    picked = mm(jnp.concatenate([qk_t, seg2], 0), pick_t)
    own = ((iota((width, hm), 0) // size) == (iota((width, hm), 1) // marks)).astype(f32)
    mark_t = picked[:width] * own
    mark_seg = picked[width : width + 8]
    sq = mark_t * mark_t
    half = -0.5 * col_sum(sq)
    half_hi = half.astype(bf16).astype(f32)
    half_mid = (half - half_hi).astype(bf16).astype(f32)
    half_lo = half - half_hi - half_mid
    row8 = iota((8, hm), 0)
    extra = jnp.where(row8 < 4, mark_seg * FAR, 0.0)
    extra = jnp.where(row8 == 4, half_hi, extra)
    extra = jnp.where(row8 == 5, half_mid, extra)
    extra = jnp.where(row8 == 6, half_lo, extra)
    extra = jnp.where(row8 == 7, -FAR, extra)
    pad = jnp.zeros((width - 8, hm), f32)
    right = jnp.concatenate([mark_t, -0.5 * own, -0.5 * own, extra, pad], 0).astype(bf16)
    near = jnp.exp(sharp * mm(feats, right)).astype(bf16)
    near_q, near_k = near[:tokens], near[tokens:]

    sq_hi = sq.astype(bf16).astype(f32)
    left = jnp.concatenate(
        [mark_t, sq_hi, sq - sq_hi, jnp.where(row8 < 4, mark_seg, 1.0), pad], 0
    ).astype(bf16)
    mark16 = mark_t.astype(bf16)

    eye = (iota((marks, marks), 0) == iota((marks, marks), 1)).astype(f32)
    heads_now = []
    for h in range(heads):
        at = slice(h * marks, (h + 1) * marks)
        kernel = jnp.exp(sharp * mm_tn(left[:, at], right[:, at]))
        gram = kernel + RIDGE * eye
        sums = col_sum(gram)
        widest = jnp.max(sums, axis=1, keepdims=True)
        inv2 = 1.0 / (widest * widest)
        approx = gram * inv2
        rest = eye - mm_wide(approx, wide_right(gram))
        steps = []
        for step in range(NS_STEPS):
            steps.append((approx, rest))
            wide = wide_right(rest)
            if step < NS_STEPS - 1:
                both = mm_wide(jnp.concatenate([rest, approx], 0), wide)
                rest, approx = both[:marks], approx + both[marks:]
            else:
                approx = approx + mm_wide(approx, wide)
        heads_now.append((kernel, gram, sums, widest, inv2, steps, approx))

    summed_t = mm(v_t, near_k) * own
    mixed_t = jnp.concatenate(
        [
            mm_wide(summed_t[:, h * marks : (h + 1) * marks], wide_right(heads_now[h][6]))
            for h in range(heads)
        ],
        1,
    ).astype(bf16)
    att = (mm_nt(near_q, mixed_t) * out_scale).astype(bf16)
    hidden = x + mm(att, wo) + vec(bo)
    xhat2, scale2 = norm_stats(hidden)
    normed2 = (xhat2 * vec(gain2) + vec(bias2)).astype(bf16)
    inner = mm(normed2, wup) + vec(bup)
    c = (2.0 / jnp.pi) ** 0.5
    inner2 = inner * inner
    th = jnp.tanh(c * inner * (1.0 + 0.044715 * inner2))
    act = (0.5 * inner * (1.0 + th)).astype(bf16)
    layer_out = hidden + mm(act, wdown) + vec(bdown)

    d_act = mm_nt(g16, wdown)
    slope = 0.5 * (1.0 + th) + 0.5 * inner * (1.0 - th * th) * (
        c * (1.0 + (3.0 * 0.044715) * inner2)
    )
    d_inner = (d_act * slope).astype(bf16)
    g_wdown_t = mm_tn(g16, act)
    g_bdown = col_sum(g)
    g_wup = mm_tn(normed2, d_inner)
    g_bup = col_sum(d_inner.astype(f32))
    d_norm2 = mm_nt(d_inner, wup)
    g_gain2 = col_sum(d_norm2 * xhat2)
    g_bias2 = col_sum(d_norm2)
    d_hidden = g + norm_back(d_norm2, xhat2, scale2, vec(gain2))
    d_branch = d_hidden.astype(bf16)
    g_wo = mm_tn(att, d_branch)
    g_bo = col_sum(d_branch.astype(f32))
    d_att = mm_nt(d_branch, wo).astype(bf16)
    d_att_t = mm_nt(wo, d_branch).astype(bf16)
    d_mixed_t = (mm(d_att_t, near_q) * (own * out_scale)).astype(bf16)
    pull_q = ((mm(d_att, mixed_t) * out_scale) * near_q.astype(f32)).astype(bf16)
    d_summed = []
    gram_parts = []
    for h in range(heads):
        kernel, gram, sums, widest, inv2, steps, approx = heads_now[h]
        at = slice(h * marks, (h + 1) * marks)
        rows = slice(h * size, (h + 1) * size)
        hi, lo = split(approx)
        both = mm(d_mixed_t[:, at], jnp.concatenate([hi, lo], 1))
        d_summed.append((both[:, :marks] + both[:, marks:]).astype(bf16))
        dm = d_mixed_t[rows, at]
        s_hi, s_lo = split(summed_t[rows, at])
        d_now = 0.5 * mm_tn(
            jnp.concatenate([dm, dm, s_hi, s_lo], 0), jnp.concatenate([s_hi, s_lo, dm, dm], 0)
        )
        d_gram = jnp.zeros((marks, marks), f32)
        for step in reversed(range(NS_STEPS)):
            before, rest = steps[step]
            both = mm_wide(jnp.concatenate([rest, before], 0), wide_right(d_now))
            d_gram = d_gram - mm_wide(both[marks:], wide_right(before))
            turned = both[:marks]
            d_now = turned + turned.T
        d_gram = d_gram + inv2 * d_now
        d_widest = -2.0 * jnp.sum(row_sum(d_now * gram), axis=0, keepdims=True) * (inv2 / widest)
        top = (sums == widest).astype(f32)
        top = top * (d_widest / row_sum(top))
        d_gram = d_gram + top
        weighted = d_gram * kernel
        weighted = (0.5 * (weighted + weighted.T)).astype(bf16)
        lhs = jnp.concatenate([mark16[:, at], jnp.ones((16, marks), bf16)], 0)
        gram_parts.append(2.0 * mm(lhs, weighted))
    gram_part = jnp.concatenate(gram_parts, 1)
    d_summed_t = jnp.concatenate(d_summed, 1)
    pull_k = (mm(v, d_summed_t) * near_k.astype(f32)).astype(bf16)
    dv = mm_nt(near_k, d_summed_t).astype(bf16)
    pulls = jnp.concatenate([pull_q, pull_k], 0)
    tok_part = mm(jnp.concatenate([qk_t, jnp.ones((16, 2 * tokens), bf16)], 0), pulls)
    both_part = tok_part + gram_part
    d_mark_t = (both_part[:width] - mark_t * both_part[width : width + 1]) * own
    onto = jnp.concatenate([mark16, d_mark_t.astype(bf16)], 1)
    moved = mm_nt(jnp.concatenate([pulls, pick_t], 1), onto)
    weight = mm_nt(pulls, own.astype(bf16))
    dq = (sharp * (moved[:tokens] - weight[:tokens] * q2[:, :width].astype(f32))).astype(bf16)
    dk = (sharp * (moved[tokens:] - weight[tokens:] * k2[:, :width].astype(f32))).astype(bf16)
    d_normed = mm_nt(dq, wq) + mm_nt(dk, wk) + mm_nt(dv, wv)
    g_wq = mm_tn(normed, dq)
    g_wk = mm_tn(normed, dk)
    g_wv = mm_tn(normed, dv)
    g_bq = col_sum(dq.astype(f32))
    g_bk = col_sum(dk.astype(f32))
    g_bv = col_sum(dv.astype(f32))
    g_gain1 = col_sum(d_normed * xhat1)
    g_bias1 = col_sum(d_normed)
    grad_in = d_hidden + norm_back(d_normed, xhat1, scale1, vec(gain1))

    def pair(a, b):
        return jnp.concatenate([a, b], 1)

    vecs = [
        g_bup,
        pair(g_bdown, g_bq),
        pair(g_bk, g_bv),
        pair(g_bo, g_gain1),
        pair(g_bias1, g_gain2),
        pair(g_bias2, jnp.zeros_like(g_bias2)),
        jnp.zeros((GRAD_ROWS - 262, 128), f32),
    ]
    grads = jnp.concatenate([g_wup, g_wdown_t, pair(g_wq, g_wk), pair(g_wv, g_wo)] + vecs, 0)
    return pair(layer_out, grad_in).astype(bf16), grads


def read_params(refs):
    return tuple(r[...] if len(r.shape) == 2 else r[...].reshape(1, -1) for r in refs)


def main_kernel(tok_block, blk_ref, idx_ref, *refs):
    params, (out_ref, keep_ref, send_ref) = refs[:16], refs[16:]
    blocks = blk_ref.shape[0]
    tokens = blocks * tok_block
    row = jnp.minimum(lax.axis_index("tok"), idx_ref.shape[0] - 1)
    xg = blk_ref[:, :tok_block, :].reshape(tokens, 128)
    ids = blk_ref[:, tok_block:, :].astype(f32)
    half = iota((SEG_ROWS, 128), 1) < tok_block
    onehot_t = jnp.concatenate(
        [jnp.where(half, ids[2 * j], ids[2 * j + 1]) for j in range(blocks // 2)], 1
    ).astype(bf16)
    out, grads = row_work(xg, onehot_t, idx_ref[row], read_params(params))
    out_ref[...] = out.reshape(blocks, tok_block, 128)
    first = lax.rem(lax.axis_index("rows"), 2) == 0
    h = GRAD_ROWS // 2
    keep_ref[...] = jnp.where(first, grads[:h], grads[h:])
    send_ref[...] = jnp.where(first, grads[h:], grads[:h])


def pack_kernel(x_ref, g_ref, s_ref, out_ref):
    rows, tok, width = x_ref.shape
    out_ref[...] = jnp.zeros(out_ref.shape, out_ref.dtype)
    out_ref[:rows, :tok, :width] = x_ref[...]
    out_ref[:rows, :tok, width:] = g_ref[...]
    seg = s_ref[...]
    for r in range(rows):
        ids = jnp.broadcast_to(seg[r : r + 1], (SEG_ROWS, tok))
        onehot = (ids == iota((SEG_ROWS, tok), 0)).astype(f32).astype(bf16)
        out_ref[r, tok:, :width] = onehot
        out_ref[r, tok:, width:] = onehot


def sum_kernel(got_ref, out_ref, grad_ref, sum_ref):
    rows, tok, width = out_ref.shape
    out_ref[...] = got_ref[:rows, :tok, :width]
    grad_ref[...] = got_ref[:rows, :tok, width:].astype(f32)
    total = got_ref[0, tok:, :].astype(f32)
    for j in range(1, got_ref.shape[0]):
        total = total + got_ref[j, tok:, :].astype(f32)
    sum_ref[...] = total


def unpack_kernel(mine_ref, other_ref, *outs):
    first = lax.rem(lax.axis_index("rows"), 2) == 0
    mine, other = mine_ref[...], other_ref[...]
    a = jnp.where(first, mine, other)
    b = jnp.where(first, other, mine)
    whole = jnp.concatenate([a, b], 0)
    (gain1, bias1, wq, bq, wk, bk, wv, bv, wo, bo, gain2, bias2, wup, bup, wdown, bdown) = outs
    wup[...] = whole[0:64]
    wdown[...] = whole[64:128].T
    wq[...] = whole[128:192, :64]
    wk[...] = whole[128:192, 64:]
    wv[...] = whole[192:256, :64]
    wo[...] = whole[192:256, 64:]
    bup[...] = whole[256]
    bdown[...] = whole[257, :64]
    bq[...] = whole[257, 64:]
    bk[...] = whole[258, :64]
    bv[...] = whole[258, 64:]
    bo[...] = whole[259, :64]
    gain1[...] = whole[259, 64:]
    bias1[...] = whole[260, :64]
    gain2[...] = whole[260, 64:]
    bias2[...] = whole[261, :64]


def call(kernel, outs, *args):
    vmem = pl.BlockSpec(memory_space=pltpu.VMEM)
    return pl.pallas_call(
        kernel,
        out_shape=outs,
        in_specs=[vmem] * len(args),
        out_specs=jax.tree.map(lambda _: vmem, outs),
        compiler_params=pltpu.CompilerParams(vmem_limit_bytes=56 * 1024 * 1024),
    )(*args)


def shards(tokens_in, segments, landmark_index, *rest):
    params, grad_out = rest[:16], rest[16]
    rows, tok, width = tokens_in.shape
    n_tok = lax.axis_size("tok")
    n_rows = lax.axis_size("rows")
    sds = jax.ShapeDtypeStruct
    sent = call(
        pack_kernel, sds((n_tok, tok + SEG_ROWS, 128), bf16), tokens_in, grad_out, segments
    )
    got = lax.all_to_all(sent, "tok", 0, 0, tiled=True)
    h = GRAD_ROWS // 2
    out, keep, send = call(
        partial(main_kernel, tok),
        (sds((n_tok, tok, 128), bf16), sds((h, 128), f32), sds((h, 128), f32)),
        got,
        landmark_index,
        *params,
    )
    total = keep + lax.ppermute(send, "rows", [(i, i ^ 1) for i in range(n_rows)])
    step = 2
    while step < n_rows:
        total = total + lax.ppermute(total, "rows", [(i, i ^ step) for i in range(n_rows)])
        step *= 2
    back = jnp.concatenate([out, jnp.broadcast_to(total.astype(bf16), (n_tok, h, 128))], 1)
    got = lax.all_to_all(back, "tok", 0, 0, tiled=True)
    layer_out, grad_input, mine = call(
        sum_kernel,
        (sds((rows, tok, width), bf16), sds((rows, tok, width), f32), sds((h, 128), f32)),
        got,
    )
    other = lax.ppermute(mine, "rows", [(i, i ^ 1) for i in range(n_rows)])
    sums = call(unpack_kernel, tuple(sds(p.shape, f32) for p in params), mine, other)
    return (layer_out, grad_input) + tuple(sums)


def solution(mesh):
    split3 = P("rows", "tok", None)
    return jax.shard_map(
        shards,
        mesh=mesh,
        in_specs=(split3, P("rows", "tok"), P("rows", None, None)) + (P(),) * 16 + (split3,),
        out_specs=(split3, split3) + (P(),) * 16,
        check_vma=False,
    )
```

```python
from functools import partial

import jax
import jax.numpy as jnp
from jax import lax
from jax.experimental import pallas as pl
from jax.experimental.pallas import tpu as pltpu
from jax.sharding import PartitionSpec as P


NS_STEPS = 6
EPS = 1e-05
RIDGE = 0.1
FAR = 640.0
SEG_ROWS = 16
GRAD_ROWS = 272

f32 = jnp.float32
bf16 = jnp.bfloat16


def mm(a, b):
    return lax.dot_general(a, b, (((1,), (0,)), ((), ())), preferred_element_type=f32)


def mm_nt(a, b):
    return lax.dot_general(a, b, (((1,), (1,)), ((), ())), preferred_element_type=f32)


def mm_tn(a, b):
    return lax.dot_general(a, b, (((0,), (0,)), ((), ())), preferred_element_type=f32)


def split(a):
    hi = a.astype(bf16)
    return hi, (a - hi.astype(f32)).astype(bf16)


def wide_right(b):
    hi, lo = split(b)
    return jnp.concatenate(
        [jnp.concatenate([hi, lo], 1), jnp.concatenate([hi, jnp.zeros_like(hi)], 1)], 0
    )


def mm_wide(a, wide):
    n = wide.shape[1] // 2
    both = mm(jnp.concatenate(split(a), 1), wide)
    return both[:, :n] + both[:, n:]


def row_sum(a):
    return jnp.sum(a, axis=1, keepdims=True)


def col_sum(a):
    return jnp.sum(a, axis=0, keepdims=True)


def total_of(a):
    return col_sum(row_sum(a))


def sym_outer(a, b):
    a_hi, a_lo = split(a)
    b_hi, b_lo = split(b)
    return 0.5 * mm_tn(
        jnp.concatenate([a_hi, a_hi, a_lo, b_hi, b_lo, b_hi], 0),
        jnp.concatenate([b_hi, b_lo, b_hi, a_hi, a_hi, a_lo], 0),
    )


def both_sides(a, wide):
    one = mm_wide(a, wide)
    return one + one.T


def norm_stats(values):
    centre = values - row_sum(values) * (1.0 / values.shape[1])
    spread = row_sum(centre * centre) * (1.0 / values.shape[1])
    scale = lax.rsqrt(spread + EPS)
    return centre * scale, scale


def norm_back(d_norm, xhat, scale, gain):
    scaled = d_norm * gain
    n = 1.0 / scaled.shape[1]
    return scale * (scaled - row_sum(scaled) * n - xhat * (row_sum(scaled * xhat) * n))


def iota(shape, dim):
    return lax.broadcasted_iota(jnp.int32, shape, dim)


def row_work(xg, onehot_t, idx, par):
    (gain1, bias1, wq, bq, wk, bk, wv, bv, wo, bo, gain2, bias2, wup, bup, wdown_t, bdown) = par
    tokens = xg.shape[0]
    width = wq.shape[0]
    heads, marks = idx.shape
    size = width // heads
    sharp = size**-0.5
    out_scale = tokens**-0.5
    hm = heads * marks
    lane = iota((tokens, 128), 1)
    low = lane < width

    def vec(v):
        return v.astype(f32)

    x = xg[:, :width].astype(f32)
    g16 = xg[:, width:]
    g = g16.astype(f32)
    xhat1, scale1 = norm_stats(x)
    normed = (xhat1 * vec(gain1) + vec(bias1)).astype(bf16)

    q2 = (mm(normed, jnp.concatenate([wq, wq], 1)) + vec(jnp.concatenate([bq, bq], 1))).astype(bf16)
    k2 = (mm(normed, jnp.concatenate([wk, wk], 1)) + vec(jnp.concatenate([bk, bk], 1))).astype(bf16)
    v = (mm(normed, wv) + vec(bv)).astype(bf16)
    q_t = q2.astype(f32).T[:width].astype(bf16)
    k_t = k2.astype(f32).T[:width].astype(bf16)
    v_t = v.astype(f32).T.astype(bf16)
    qk_t = jnp.concatenate([q_t, k_t], 1)

    place = (iota((SEG_ROWS, 128), 1) == iota((SEG_ROWS, 128), 0) + width).astype(f32).astype(bf16)
    seg_lanes = mm_tn(onehot_t, place)
    feat = jnp.where((lane >= width + 4) & (lane < width + 8), 1.0, seg_lanes)

    def features(p2):
        p = p2.astype(f32)
        sq = p * p
        hi = sq.astype(bf16).astype(f32)
        return jnp.concatenate(
            [jnp.where(low, p, hi).astype(bf16), jnp.where(low, sq - hi, feat).astype(bf16)], 1
        )

    feats = jnp.concatenate([features(q2), features(k2)], 0)

    idx_row = jnp.concatenate([idx[h : h + 1] for h in range(heads)], 1)
    pick_t = (iota((2 * tokens, hm), 0) == idx_row).astype(f32).astype(bf16)
    seg2 = jnp.concatenate([onehot_t, onehot_t], 1)
    picked = mm(jnp.concatenate([qk_t, seg2], 0), pick_t)
    own = ((iota((width, hm), 0) // size) == (iota((width, hm), 1) // marks)).astype(f32)
    mark_t = picked[:width] * own
    mark_seg = picked[width : width + 8]
    sq = mark_t * mark_t
    half = -0.5 * col_sum(sq)
    half_hi = half.astype(bf16).astype(f32)
    half_mid = (half - half_hi).astype(bf16).astype(f32)
    half_lo = half - half_hi - half_mid
    row8 = iota((8, hm), 0)
    extra = jnp.where(row8 < 4, mark_seg * FAR, 0.0)
    extra = jnp.where(row8 == 4, half_hi, extra)
    extra = jnp.where(row8 == 5, half_mid, extra)
    extra = jnp.where(row8 == 6, half_lo, extra)
    extra = jnp.where(row8 == 7, -FAR, extra)
    pad = jnp.zeros((width - 8, hm), f32)
    right = jnp.concatenate([mark_t, -0.5 * own, -0.5 * own, extra, pad], 0).astype(bf16)
    near = jnp.exp(sharp * mm(feats, right)).astype(bf16)
    near_q, near_k = near[:tokens], near[tokens:]

    sq_hi = sq.astype(bf16).astype(f32)
    left = jnp.concatenate(
        [mark_t, sq_hi, sq - sq_hi, jnp.where(row8 < 4, mark_seg, 1.0), pad], 0
    ).astype(bf16)
    mark16 = mark_t.astype(bf16)

    eye = (iota((marks, marks), 0) == iota((marks, marks), 1)).astype(f32)
    hs = range(heads)
    at = [slice(h * marks, (h + 1) * marks) for h in hs]
    rows_of = [slice(h * size, (h + 1) * size) for h in hs]
    kernel = [jnp.exp(sharp * mm_tn(left[:, at[h]], right[:, at[h]])) for h in hs]
    gram = [kernel[h] + RIDGE * eye for h in hs]
    sums = [col_sum(gram[h]) for h in hs]
    widest = [jnp.max(sums[h], axis=1, keepdims=True) for h in hs]
    inv2 = [1.0 / (widest[h] * widest[h]) for h in hs]
    gram_wide = [wide_right(gram[h]) for h in hs]
    summed_t = [mm(v_t[rows_of[h]], near_k[:, at[h]]) for h in hs]
    rests, wides, grown = [], [], []
    rest = [eye - mm_wide(gram[h] * inv2[h], gram_wide[h]) for h in hs]
    now = [mm_wide(summed_t[h], gram_wide[h]) * inv2[h] for h in hs]
    for step in range(NS_STEPS):
        wide = [wide_right(rest[h]) for h in hs]
        rests.append(rest)
        wides.append(wide)
        grown.append(now)
        if step < NS_STEPS - 1:
            rest = [mm_wide(rest[h], wide[h]) for h in hs]
        now = [now[h] + mm_wide(now[h], wide[h]) for h in hs]

    def spread_heads(parts):
        zero = jnp.zeros_like(parts[0])
        return jnp.concatenate(
            [jnp.concatenate([parts[h] if g == h else zero for g in hs], 1) for h in hs], 0
        )

    mixed_t = spread_heads(now).astype(bf16)
    att = (mm_nt(near_q, mixed_t) * out_scale).astype(bf16)
    hidden = x + mm(att, wo) + vec(bo)
    xhat2, scale2 = norm_stats(hidden)
    normed2 = (xhat2 * vec(gain2) + vec(bias2)).astype(bf16)
    inner = mm(normed2, wup) + vec(bup)
    c = (2.0 / jnp.pi) ** 0.5
    inner2 = inner * inner
    th = jnp.tanh(c * inner * (1.0 + 0.044715 * inner2))
    act = (0.5 * inner * (1.0 + th)).astype(bf16)
    layer_out = hidden + mm_nt(act, wdown_t) + vec(bdown)

    d_act = mm(g16, wdown_t)
    slope = 0.5 * (1.0 + th) + 0.5 * inner * (1.0 - th * th) * (
        c * (1.0 + (3.0 * 0.044715) * inner2)
    )
    d_inner = (d_act * slope).astype(bf16)
    g_wdown_t = mm_tn(g16, act)
    g_bdown = col_sum(g)
    g_wup = mm_tn(normed2, d_inner)
    g_bup = col_sum(d_inner.astype(f32))
    d_norm2 = mm_nt(d_inner, wup)
    g_gain2 = col_sum(d_norm2 * xhat2)
    g_bias2 = col_sum(d_norm2)
    d_hidden = g + norm_back(d_norm2, xhat2, scale2, vec(gain2))
    d_branch = d_hidden.astype(bf16)
    g_wo = mm_tn(att, d_branch)
    g_bo = col_sum(d_branch.astype(f32))
    d_att = mm_nt(d_branch, wo).astype(bf16)
    d_att_t = mm_nt(wo, d_branch).astype(bf16)
    d_mixed_t = (mm(d_att_t, near_q) * (own * out_scale)).astype(bf16)
    pull_q = ((mm(d_att, mixed_t) * out_scale) * near_q.astype(f32)).astype(bf16)
    back = [d_mixed_t[rows_of[h], at[h]].astype(f32) for h in hs]
    d_rest = None
    for step in reversed(range(NS_STEPS)):
        outer = [sym_outer(back[h], grown[step][h]) for h in hs]
        if d_rest is None:
            d_rest = outer
        else:
            d_rest = [outer[h] + both_sides(d_rest[h], wides[step][h]) for h in hs]
        back = [back[h] + mm_wide(back[h], wides[step][h]) for h in hs]
    d_summed_t = spread_heads([mm_wide(back[h], gram_wide[h]) * inv2[h] for h in hs]).astype(bf16)
    gram_parts = []
    for h in hs:
        d_gram = inv2[h] * (
            sym_outer(back[h], summed_t[h]) - both_sides(d_rest[h], gram_wide[h])
        )
        d_widest = (2.0 / widest[h]) * (
            total_of(d_rest[h] * (eye - rests[0][h])) - total_of(back[h] * grown[0][h])
        )
        top = (sums[h] == widest[h]).astype(f32)
        weighted = (d_gram + top * (d_widest / row_sum(top))) * kernel[h]
        weighted = (0.5 * (weighted + weighted.T)).astype(bf16)
        lhs = jnp.concatenate([mark16[:, at[h]], jnp.ones((16, marks), bf16)], 0)
        gram_parts.append(2.0 * mm(lhs, weighted))
    gram_part = jnp.concatenate(gram_parts, 1)
    pull_k = (mm(v, d_summed_t) * near_k.astype(f32)).astype(bf16)
    dv = mm_nt(near_k, d_summed_t).astype(bf16)
    pulls = jnp.concatenate([pull_q, pull_k], 0)
    tok_part = mm(jnp.concatenate([qk_t, jnp.ones((16, 2 * tokens), bf16)], 0), pulls)
    both_part = tok_part + gram_part
    d_mark_t = (both_part[:width] - mark_t * both_part[width : width + 1]) * own
    onto = jnp.concatenate([mark16, d_mark_t.astype(bf16)], 1)
    moved = mm_nt(jnp.concatenate([pulls, pick_t], 1), onto)
    weight = mm_nt(pulls, own.astype(bf16))
    dq = (sharp * (moved[:tokens] - weight[:tokens] * q2[:, :width].astype(f32))).astype(bf16)
    dk = (sharp * (moved[tokens:] - weight[tokens:] * k2[:, :width].astype(f32))).astype(bf16)
    d_normed = mm_nt(dq, wq) + mm_nt(dk, wk) + mm_nt(dv, wv)
    g_wq = mm_tn(normed, dq)
    g_wk = mm_tn(normed, dk)
    g_wv = mm_tn(normed, dv)
    g_bq = col_sum(dq.astype(f32))
    g_bk = col_sum(dk.astype(f32))
    g_bv = col_sum(dv.astype(f32))
    g_gain1 = col_sum(d_normed * xhat1)
    g_bias1 = col_sum(d_normed)
    grad_in = d_hidden + norm_back(d_normed, xhat1, scale1, vec(gain1))

    def pair(a, b):
        return jnp.concatenate([a, b], 1)

    vecs = [
        g_bup,
        pair(g_bdown, g_bq),
        pair(g_bk, g_bv),
        pair(g_bo, g_gain1),
        pair(g_bias1, g_gain2),
        pair(g_bias2, jnp.zeros_like(g_bias2)),
        jnp.zeros((GRAD_ROWS - 262, 128), f32),
    ]
    grads = jnp.concatenate([g_wup, g_wdown_t, pair(g_wq, g_wk), pair(g_wv, g_wo)] + vecs, 0)
    return pair(layer_out, grad_in).astype(bf16), grads


def read_params(refs):
    return tuple(r[...] if len(r.shape) == 2 else r[...].reshape(1, -1) for r in refs)


def main_kernel(tok_block, blk_ref, idx_ref, *refs):
    params, (out_ref, keep_ref, send_ref) = refs[:16], refs[16:]
    blocks = blk_ref.shape[0]
    tokens = blocks * tok_block
    row = jnp.minimum(lax.axis_index("tok"), idx_ref.shape[0] - 1)
    xg = blk_ref[:, :tok_block, :].reshape(tokens, 128)
    ids = blk_ref[:, tok_block:, :].astype(f32)
    half = iota((SEG_ROWS, 128), 1) < tok_block
    onehot_t = jnp.concatenate(
        [jnp.where(half, ids[2 * j], ids[2 * j + 1]) for j in range(blocks // 2)], 1
    ).astype(bf16)
    out, grads = row_work(xg, onehot_t, idx_ref[row], read_params(params))
    out_ref[...] = out.reshape(blocks, tok_block, 128)
    first = lax.rem(lax.axis_index("rows"), 2) == 0
    h = GRAD_ROWS // 2
    keep_ref[...] = jnp.where(first, grads[:h], grads[h:])
    send_ref[...] = jnp.where(first, grads[h:], grads[:h])


def pack_kernel(x_ref, g_ref, s_ref, out_ref):
    rows, tok, width = x_ref.shape
    out_ref[...] = jnp.zeros(out_ref.shape, out_ref.dtype)
    out_ref[:rows, :tok, :width] = x_ref[...]
    out_ref[:rows, :tok, width:] = g_ref[...]
    seg = s_ref[...]
    for r in range(rows):
        ids = jnp.broadcast_to(seg[r : r + 1], (SEG_ROWS, tok))
        onehot = (ids == iota((SEG_ROWS, tok), 0)).astype(f32).astype(bf16)
        out_ref[r, tok:, :width] = onehot
        out_ref[r, tok:, width:] = onehot


def sum_kernel(got_ref, out_ref, grad_ref, sum_ref):
    rows, tok, width = out_ref.shape
    total = got_ref[0, tok:, :].astype(f32)
    for j in range(1, got_ref.shape[0]):
        total = total + got_ref[j, tok:, :].astype(f32)
    sum_ref[...] = total.astype(bf16)
    out_ref[...] = got_ref[:rows, :tok, :width]
    grad_ref[...] = got_ref[:rows, :tok, width:].astype(f32)


def unpack_kernel(n_parts, *refs):
    parts, outs = refs[:n_parts], refs[n_parts:]
    halves = [
        sum([p[...].astype(f32) for p in parts[core + 2 :: 2]], parts[core][...].astype(f32))
        for core in range(2)
    ]
    first = lax.rem(lax.axis_index("rows"), 2) == 0
    a = jnp.where(first, halves[0], halves[1])
    b = jnp.where(first, halves[1], halves[0])
    whole = jnp.concatenate([a, b], 0)
    (gain1, bias1, wq, bq, wk, bk, wv, bv, wo, bo, gain2, bias2, wup, bup, wdown_t, bdown) = outs
    wup[...] = whole[0:64]
    wdown_t[...] = whole[64:128]
    wq[...] = whole[128:192, :64]
    wk[...] = whole[128:192, 64:]
    wv[...] = whole[192:256, :64]
    wo[...] = whole[192:256, 64:]
    bup[...] = whole[256]
    bdown[...] = whole[257, :64]
    bq[...] = whole[257, 64:]
    bk[...] = whole[258, :64]
    bv[...] = whole[258, 64:]
    bo[...] = whole[259, :64]
    gain1[...] = whole[259, 64:]
    bias1[...] = whole[260, :64]
    gain2[...] = whole[260, 64:]
    bias2[...] = whole[261, :64]


def call(kernel, outs, *args, mib=12):
    vmem = pl.BlockSpec(memory_space=pltpu.VMEM)
    return pl.pallas_call(
        kernel,
        out_shape=outs,
        in_specs=[vmem] * len(args),
        out_specs=jax.tree.map(lambda _: vmem, outs),
        compiler_params=pltpu.CompilerParams(vmem_limit_bytes=mib * 1024 * 1024),
    )(*args)


def shards(tokens_in, segments, landmark_index, *rest):
    params, grad_out = rest[:14] + (rest[14].T, rest[15]), rest[16]
    rows, tok, width = tokens_in.shape
    n_tok = lax.axis_size("tok")
    n_rows = lax.axis_size("rows")
    sds = jax.ShapeDtypeStruct
    sent = call(
        pack_kernel, sds((n_tok, tok + SEG_ROWS, 128), bf16), tokens_in, grad_out, segments, mib=56
    )
    got = lax.all_to_all(sent, "tok", 0, 0, tiled=True)
    h = GRAD_ROWS // 2
    out, keep, send = call(
        partial(main_kernel, tok),
        (sds((n_tok, tok, 128), bf16), sds((h, 128), f32), sds((h, 128), f32)),
        got,
        landmark_index,
        *params,
        mib=12 * max(1, n_tok * tok // 512),
    )
    def from_xor(array, m):
        return lax.ppermute(array, "rows", [(i, i ^ m) for i in range(n_rows)])

    total = (keep + from_xor(send, 1)).astype(bf16)
    back = jnp.concatenate([out, jnp.broadcast_to(total, (n_tok, h, 128))], 1)
    got = lax.all_to_all(back, "tok", 0, 0, tiled=True)
    layer_out, grad_input, mine = call(
        sum_kernel,
        (sds((rows, tok, width), bf16), sds((rows, tok, width), f32), sds((h, 128), bf16)),
        got,
    )
    parts = [mine] + [from_xor(mine, m) for m in range(1, n_rows)]
    sums = call(
        partial(unpack_kernel, n_rows), tuple(sds(p.shape, f32) for p in params), *parts
    )
    sums = sums[:14] + (sums[14].T,) + sums[15:]
    return (layer_out, grad_input) + tuple(sums)


def solution(mesh):
    split3 = P("rows", "tok", None)
    return jax.shard_map(
        shards,
        mesh=mesh,
        in_specs=(split3, P("rows", "tok"), P("rows", None, None)) + (P(),) * 16 + (split3,),
        out_specs=(split3, split3) + (P(),) * 16,
        check_vma=False,
    )
```

```python
from functools import partial

import jax
import jax.numpy as jnp
from jax import lax
from jax.experimental import pallas as pl
from jax.experimental.pallas import tpu as pltpu
from jax.sharding import PartitionSpec as P


NS_STEPS = 6
EPS = 1e-05
RIDGE = 0.1
FAR = 640.0
SEG_ROWS = 16
GRAD_ROWS = 272

f32 = jnp.float32
bf16 = jnp.bfloat16


def mm(a, b):
    return lax.dot_general(a, b, (((1,), (0,)), ((), ())), preferred_element_type=f32)


def mm_nt(a, b):
    return lax.dot_general(a, b, (((1,), (1,)), ((), ())), preferred_element_type=f32)


def mm_tn(a, b):
    return lax.dot_general(a, b, (((0,), (0,)), ((), ())), preferred_element_type=f32)


def split(a):
    hi = a.astype(bf16)
    return hi, (a - hi.astype(f32)).astype(bf16)


def wide_right(b):
    hi, lo = split(b)
    return jnp.concatenate(
        [jnp.concatenate([hi, lo], 1), jnp.concatenate([hi, jnp.zeros_like(hi)], 1)], 0
    )


def mm_wide(a, wide):
    n = wide.shape[1] // 2
    both = mm(jnp.concatenate(split(a), 1), wide)
    return both[:, :n] + both[:, n:]


def row_sum(a):
    return jnp.sum(a, axis=1, keepdims=True)


def col_sum(a):
    return jnp.sum(a, axis=0, keepdims=True)


def total_of(a):
    return col_sum(row_sum(a))


def both_parts(product, a, b):
    n = b.shape[1]
    both = product(a, jnp.concatenate(split(b), 1))
    return both[:, :n] + both[:, n:]


def pair(a, b):
    return jnp.concatenate([a, b], 1)


def wide_mm(a_pair, wide):
    n = wide.shape[1] // 2
    both = mm(a_pair, wide)
    return both[:, :n] + both[:, n:]


def norm_stats(values):
    centre = values - row_sum(values) * (1.0 / values.shape[1])
    spread = row_sum(centre * centre) * (1.0 / values.shape[1])
    scale = lax.rsqrt(spread + EPS)
    return centre * scale, scale


def norm_back(d_norm, xhat, scale, gain):
    scaled = d_norm * gain
    n = 1.0 / scaled.shape[1]
    return scale * (scaled - row_sum(scaled) * n - xhat * (row_sum(scaled * xhat) * n))


def iota(shape, dim):
    return lax.broadcasted_iota(jnp.int32, shape, dim)


def row_work(xg, onehot_t, idx, par):
    (gain1, bias1, wq, bq, wk, bk, wv, bv, wo, bo, gain2, bias2, wup, bup, wdown_t, bdown) = par
    tokens = xg.shape[0]
    width = wq.shape[0]
    heads, marks = idx.shape
    size = width // heads
    sharp = size**-0.5
    out_scale = tokens**-0.5
    hm = heads * marks
    lane = iota((tokens, 128), 1)
    low = lane < width

    def vec(v):
        return v.astype(f32)

    x = xg[:, :width].astype(f32)
    g16 = xg[:, width:]
    g = g16.astype(f32)
    xhat1, scale1 = norm_stats(x)
    normed = (xhat1 * vec(gain1) + vec(bias1)).astype(bf16)

    q2 = (mm(normed, jnp.concatenate([wq, wq], 1)) + vec(jnp.concatenate([bq, bq], 1))).astype(bf16)
    k2 = (mm(normed, jnp.concatenate([wk, wk], 1)) + vec(jnp.concatenate([bk, bk], 1))).astype(bf16)
    v = (mm(normed, wv) + vec(bv)).astype(bf16)
    q_t = q2.astype(f32).T[:width].astype(bf16)
    k_t = k2.astype(f32).T[:width].astype(bf16)
    v_t = v.astype(f32).T.astype(bf16)
    qk_t = jnp.concatenate([q_t, k_t], 1)

    place = (iota((SEG_ROWS, 128), 1) == iota((SEG_ROWS, 128), 0) + width).astype(f32).astype(bf16)
    seg_lanes = mm_tn(onehot_t, place)
    feat = jnp.where((lane >= width + 4) & (lane < width + 8), 1.0, seg_lanes)

    def features(p2):
        p = p2.astype(f32)
        sq = p * p
        hi = sq.astype(bf16).astype(f32)
        return jnp.concatenate(
            [jnp.where(low, p, hi).astype(bf16), jnp.where(low, sq - hi, feat).astype(bf16)], 1
        )

    feats_q, feats_k = features(q2), features(k2)

    idx_row = jnp.concatenate([idx[h : h + 1] for h in range(heads)], 1)
    pick_t = (iota((2 * tokens, hm), 0) == idx_row).astype(f32).astype(bf16)
    seg2 = jnp.concatenate([onehot_t, onehot_t], 1)
    picked = mm(jnp.concatenate([qk_t, seg2], 0), pick_t)
    own = ((iota((width, hm), 0) // size) == (iota((width, hm), 1) // marks)).astype(f32)
    mark_t = picked[:width] * own
    mark_seg = picked[width : width + 8]
    sq = mark_t * mark_t
    half = -0.5 * col_sum(sq)
    half_hi = half.astype(bf16).astype(f32)
    half_mid = (half - half_hi).astype(bf16).astype(f32)
    half_lo = half - half_hi - half_mid
    row8 = iota((8, hm), 0)
    extra = jnp.where(row8 < 4, mark_seg * FAR, 0.0)
    extra = jnp.where(row8 == 4, half_hi, extra)
    extra = jnp.where(row8 == 5, half_mid, extra)
    extra = jnp.where(row8 == 6, half_lo, extra)
    extra = jnp.where(row8 == 7, -FAR, extra)
    pad = jnp.zeros((width - 8, hm), f32)
    right = jnp.concatenate([mark_t, -0.5 * own, -0.5 * own, extra, pad], 0).astype(bf16)
    sq_hi = sq.astype(bf16).astype(f32)
    left = jnp.concatenate(
        [mark_t, sq_hi, sq - sq_hi, jnp.where(row8 < 4, mark_seg, 1.0), pad], 0
    ).astype(bf16)
    mark16 = mark_t.astype(bf16)

    eye = (iota((marks, marks), 0) == iota((marks, marks), 1)).astype(f32)
    hs = range(heads)
    at = [slice(h * marks, (h + 1) * marks) for h in hs]
    rows_of = [slice(h * size, (h + 1) * size) for h in hs]
    kernel = [jnp.exp(sharp * mm_tn(left[:, at[h]], right[:, at[h]])) for h in hs]
    gram = [kernel[h] + RIDGE * eye for h in hs]
    sums = [col_sum(gram[h]) for h in hs]
    widest = [jnp.max(sums[h], axis=1, keepdims=True) for h in hs]
    inv2 = [1.0 / (widest[h] * widest[h]) for h in hs]
    gram_wide = [wide_right(gram[h]) for h in hs]

    def near_of(points):
        return jnp.exp(sharp * mm(points, right)).astype(bf16)

    chunk = tokens // 4
    near_q_parts = []
    rest_pair, grown_pair = [], []
    wo_of = [wo[rows_of[h]] for h in hs]
    rest = [eye - mm_wide(gram[h] * inv2[h], gram_wide[h]) for h in hs]
    near_k = near_of(feats_k)
    summed_t = [mm(v_t[rows_of[h]], near_k[:, at[h]]) for h in hs]
    sent_t = [both_parts(mm_tn, wo_of[h], summed_t[h]) for h in hs]
    now = [mm_wide(sent_t[h], gram_wide[h]) * inv2[h] for h in hs]
    rests, wides, grown = [], [], []
    for step in range(NS_STEPS):
        wide = [wide_right(rest[h]) for h in hs]
        rests.append(rest)
        wides.append(wide)
        grown.append(now)
        if step < NS_STEPS - 1:
            rest = [mm_wide(rest[h], wide[h]) for h in hs]
        now = [now[h] + mm_wide(now[h], wide[h]) for h in hs]
        if len(near_q_parts) < 4:
            lo = len(near_q_parts) * chunk
            near_q_parts.append(near_of(feats_q[lo : lo + chunk]))
        rest_pair.append([pair(*split(rests[step][h])) for h in hs])
        grown_pair.append([grown[step][h].T.astype(bf16) for h in hs])
    near_q = jnp.concatenate(near_q_parts, 0)
    mixed_t = jnp.concatenate(now, 1).astype(bf16)
    hidden = x + (mm_nt(near_q, mixed_t) * out_scale + vec(bo))
    xhat2, scale2 = norm_stats(hidden)
    normed2 = (xhat2 * vec(gain2) + vec(bias2)).astype(bf16)
    inner = mm(normed2, wup) + vec(bup)
    c = (2.0 / jnp.pi) ** 0.5
    inner2 = inner * inner
    th = jnp.tanh(c * inner * (1.0 + 0.044715 * inner2))
    act = (0.5 * inner * (1.0 + th)).astype(bf16)
    layer_out = hidden + mm_nt(act, wdown_t) + vec(bdown)

    gram_pair = [pair(*split(gram[h])) for h in hs]
    sent_pair = [pair(*split(sent_t[h].T)) for h in hs]
    kernel_inv = [kernel[h] * inv2[h] for h in hs]
    widest_a = [(2.0 / widest[h]) * (eye - rests[0][h]) for h in hs]
    widest_b = [(2.0 / widest[h]) * grown[0][h] for h in hs]
    mark_ones = [
        jnp.concatenate([mark16[:, at[h]], jnp.ones((16, marks), bf16)], 0) for h in hs
    ]
    top_part = []
    for h in hs:
        top = (sums[h] == widest[h]).astype(f32)
        top = top * (1.0 / row_sum(top))
        seen = kernel[h].astype(bf16)
        along = jnp.broadcast_to(top, (16, marks)).astype(bf16)
        top_part.append(
            top * mm(mark_ones[h], seen)
            + mm_nt(mark_ones[h], along)[:, :1] * mm(along, seen)[:1]
        )
    d_act = mm(g16, wdown_t)
    slope = 0.5 * (1.0 + th) + 0.5 * inner * (1.0 - th * th) * (
        c * (1.0 + (3.0 * 0.044715) * inner2)
    )
    d_inner = (d_act * slope).astype(bf16)
    g_wdown_t = mm_tn(g16, act)
    g_bdown = col_sum(g)
    g_wup = mm_tn(normed2, d_inner)
    g_bup = col_sum(d_inner.astype(f32))
    d_norm2 = mm_nt(d_inner, wup)
    g_gain2 = col_sum(d_norm2 * xhat2)
    g_bias2 = col_sum(d_norm2)
    d_hidden = g + norm_back(d_norm2, xhat2, scale2, vec(gain2))
    d_branch = d_hidden.astype(bf16)
    g_bo = col_sum(d_branch.astype(f32))
    d_sent_t = mm_tn(d_branch, near_q) * out_scale
    back = [d_sent_t[:, at[h]] for h in hs]

    def pulled(rows):
        pull = ((mm(d_branch[rows], mixed_t) * out_scale) * near_q[rows].astype(f32)).astype(bf16)
        return pull, stays(pull, q2[rows])

    def stays(pull, p2):
        both = mm(pull, both_m)
        return sharp * (both[:, :width] - both[:, width:] * p2[:, :width].astype(f32))

    both_m = jnp.concatenate([mark_t, own], 0).T.astype(bf16)
    q_parts = []
    d_rest = None
    for step in reversed(range(NS_STEPS)):
        outer = [mm(grown_pair[step][h], back[h].astype(bf16)) for h in hs]
        back = [back[h] + mm_wide(back[h], wides[step][h]) for h in hs]
        if d_rest is None:
            d_rest = outer
        else:
            d_rest = [
                mm_wide(d_rest[h], wides[step][h])
                + wide_mm(rest_pair[step][h], wide_right(d_rest[h]))
                + outer[h]
                for h in hs
            ]
        if len(q_parts) < 4:
            lo = len(q_parts) * chunk
            q_parts.append(pulled(slice(lo, lo + chunk)))
    pull_q = jnp.concatenate([p for p, _ in q_parts], 0)
    stay_q = [s for _, s in q_parts]
    left_now = [mm_wide(jnp.concatenate([back[h], d_rest[h]], 0), gram_wide[h]) for h in hs]
    d_start = [left_now[h][:width] * inv2[h] for h in hs]
    d_summed = [both_parts(mm, wo_of[h], d_start[h]).astype(bf16) for h in hs]
    none = jnp.zeros((size, marks), bf16)
    d_summed_t = jnp.concatenate(
        [jnp.concatenate([d_summed[h] if g == h else none for g in hs], 1) for h in hs], 0
    )
    d_gram = [
        wide_mm(
            pair(sent_pair[h], -gram_pair[h]),
            jnp.concatenate([wide_right(back[h]), wide_right(d_rest[h])], 0),
        )
        - left_now[h][width:]
        for h in hs
    ]
    pull_k = (mm(v, d_summed_t) * near_k.astype(f32)).astype(bf16)
    gram_parts = []
    for h in hs:
        d_widest = total_of(d_rest[h] * widest_a[h]) - total_of(back[h] * widest_b[h])
        weighted = ((d_gram[h] + d_gram[h].T) * kernel_inv[h]).astype(bf16)
        gram_parts.append(mm(mark_ones[h], weighted) + d_widest * top_part[h])
    gram_part = jnp.concatenate(gram_parts, 1)
    pulls = jnp.concatenate([pull_q, pull_k], 0)
    tok_part = mm(jnp.concatenate([qk_t, jnp.ones((16, 2 * tokens), bf16)], 0), pulls)
    both_part = tok_part + gram_part
    d_mark_t = (both_part[:width] - mark_t * both_part[width : width + 1]) * own
    stay_k = [stays(pull_k[lo : lo + chunk], k2[lo : lo + chunk]) for lo in range(0, tokens, chunk)]
    stay = jnp.concatenate(stay_q + stay_k, 0)
    g_wo = jnp.concatenate(
        [mm_nt(summed_t[h].astype(bf16), d_start[h].astype(bf16)) for h in hs], 0
    )
    dv = mm_nt(near_k, d_summed_t).astype(bf16)
    moved = mm_nt(pick_t, d_mark_t.astype(bf16))
    dq = (stay[:tokens] + sharp * moved[:tokens]).astype(bf16)
    dk = (stay[tokens:] + sharp * moved[tokens:]).astype(bf16)
    d_normed = mm_nt(dq, wq) + mm_nt(dk, wk) + mm_nt(dv, wv)
    g_wq = mm_tn(normed, dq)
    g_wk = mm_tn(normed, dk)
    g_wv = mm_tn(normed, dv)
    g_bq = col_sum(dq.astype(f32))
    g_bk = col_sum(dk.astype(f32))
    g_bv = col_sum(dv.astype(f32))
    g_gain1 = col_sum(d_normed * xhat1)
    g_bias1 = col_sum(d_normed)
    grad_in = d_hidden + norm_back(d_normed, xhat1, scale1, vec(gain1))

    vecs = [
        g_bup,
        pair(g_bdown, g_bq),
        pair(g_bk, g_bv),
        pair(g_bo, g_gain1),
        pair(g_bias1, g_gain2),
        pair(g_bias2, jnp.zeros_like(g_bias2)),
        jnp.zeros((GRAD_ROWS - 262, 128), f32),
    ]
    grads = jnp.concatenate([g_wup, g_wdown_t, pair(g_wq, g_wk), pair(g_wv, g_wo)] + vecs, 0)
    return pair(layer_out, grad_in).astype(bf16), grads


MATRICES = (2, 4, 6, 8, 12, 14)
VECTORS = (0, 1, 3, 5, 7, 9, 10, 11, 13, 15)


def read_params(mats, vec_ref):
    par = [None] * 16
    for i, ref in zip(MATRICES, mats):
        par[i] = ref[...]
    for row, i in enumerate(VECTORS):
        wide = par[12].shape[1] if i == 13 else par[2].shape[0]
        par[i] = vec_ref[row : row + 1, :wide]
    return tuple(par)


def main_kernel(tok_block, blk_ref, idx_ref, vec_ref, *refs):
    mats, (out_ref, keep_ref, send_ref) = refs[:6], refs[6:]
    blocks = blk_ref.shape[0]
    tokens = blocks * tok_block
    row = jnp.minimum(lax.axis_index("tok"), idx_ref.shape[0] - 1)
    xg = blk_ref[:, :tok_block, :].reshape(tokens, 128)
    ids = blk_ref[:, tok_block:, :].astype(f32)
    half = iota((SEG_ROWS, 128), 1) < tok_block
    onehot_t = jnp.concatenate(
        [jnp.where(half, ids[2 * j], ids[2 * j + 1]) for j in range(blocks // 2)], 1
    ).astype(bf16)
    out, grads = row_work(xg, onehot_t, idx_ref[row], read_params(mats, vec_ref))
    out_ref[...] = out.reshape(blocks, tok_block, 128)
    first = lax.rem(lax.axis_index("rows"), 2) == 0
    h = GRAD_ROWS // 2
    keep_ref[...] = jnp.where(first, grads[:h], grads[h:])
    send_ref[...] = jnp.where(first, grads[h:], grads[:h])


def pack_kernel(x_ref, g_ref, s_ref, *refs):
    vecs, (out_ref, vec_ref) = refs[:-2], refs[-2:]
    rows, tok, width = x_ref.shape
    for i, ref in enumerate(vecs):
        vec_ref[i : i + 1, : ref.shape[0]] = ref[...].astype(f32).reshape(1, -1)
    out_ref[...] = jnp.zeros(out_ref.shape, out_ref.dtype)
    out_ref[:rows, :tok, :width] = x_ref[...]
    out_ref[:rows, :tok, width:] = g_ref[...]
    seg = s_ref[...]
    for r in range(rows):
        ids = jnp.broadcast_to(seg[r : r + 1], (SEG_ROWS, tok))
        onehot = (ids == iota((SEG_ROWS, tok), 0)).astype(f32).astype(bf16)
        out_ref[r, tok:, :width] = onehot
        out_ref[r, tok:, width:] = onehot


def sum_kernel(got_ref, out_ref, grad_ref, sum_ref):
    rows, tok, width = out_ref.shape
    total = got_ref[0, tok:, :].astype(f32)
    for j in range(1, got_ref.shape[0]):
        total = total + got_ref[j, tok:, :].astype(f32)
    sum_ref[...] = total.astype(bf16)
    out_ref[...] = got_ref[:rows, :tok, :width]
    grad_ref[...] = got_ref[:rows, :tok, width:].astype(f32)


def unpack_kernel(n_parts, *refs):
    parts, outs = refs[:n_parts], refs[n_parts:]
    halves = [
        sum([p[...].astype(f32) for p in parts[core + 2 :: 2]], parts[core][...].astype(f32))
        for core in range(2)
    ]
    first = lax.rem(lax.axis_index("rows"), 2) == 0
    a = jnp.where(first, halves[0], halves[1])
    b = jnp.where(first, halves[1], halves[0])
    whole = jnp.concatenate([a, b], 0)
    (gain1, bias1, wq, bq, wk, bk, wv, bv, wo, bo, gain2, bias2, wup, bup, wdown_t, bdown) = outs
    wup[...] = whole[0:64]
    wdown_t[...] = whole[64:128]
    wq[...] = whole[128:192, :64]
    wk[...] = whole[128:192, 64:]
    wv[...] = whole[192:256, :64]
    wo[...] = whole[192:256, 64:]
    bup[...] = whole[256]
    bdown[...] = whole[257, :64]
    bq[...] = whole[257, 64:]
    bk[...] = whole[258, :64]
    bv[...] = whole[258, 64:]
    bo[...] = whole[259, :64]
    gain1[...] = whole[259, 64:]
    bias1[...] = whole[260, :64]
    gain2[...] = whole[260, 64:]
    bias2[...] = whole[261, :64]


def call(kernel, outs, *args, mib=12):
    vmem = pl.BlockSpec(memory_space=pltpu.VMEM)
    return pl.pallas_call(
        kernel,
        out_shape=outs,
        in_specs=[vmem] * len(args),
        out_specs=jax.tree.map(lambda _: vmem, outs),
        compiler_params=pltpu.CompilerParams(vmem_limit_bytes=mib * 1024 * 1024),
    )(*args)


def shards(tokens_in, segments, landmark_index, *rest):
    params, grad_out = rest[:14] + (rest[14].T, rest[15]), rest[16]
    rows, tok, width = tokens_in.shape
    n_tok = lax.axis_size("tok")
    n_rows = lax.axis_size("rows")
    sds = jax.ShapeDtypeStruct
    sent, vecs = call(
        pack_kernel,
        (sds((n_tok, tok + SEG_ROWS, 128), bf16), sds((16, 128), f32)),
        tokens_in,
        grad_out,
        segments,
        *[params[i] for i in VECTORS],
        mib=56,
    )
    got = lax.all_to_all(sent, "tok", 0, 0, tiled=True)
    h = GRAD_ROWS // 2
    out, keep, send = call(
        partial(main_kernel, tok),
        (sds((n_tok, tok, 128), bf16), sds((h, 128), f32), sds((h, 128), f32)),
        got,
        landmark_index,
        vecs,
        *[params[i] for i in MATRICES],
        mib=12 * max(1, n_tok * tok // 512),
    )
    def from_xor(array, m):
        return lax.ppermute(array, "rows", [(i, i ^ m) for i in range(n_rows)])

    total = (keep + from_xor(send, 1)).astype(bf16)
    back = jnp.concatenate([out, jnp.broadcast_to(total, (n_tok, h, 128))], 1)
    got = lax.all_to_all(back, "tok", 0, 0, tiled=True)
    layer_out, grad_input, mine = call(
        sum_kernel,
        (sds((rows, tok, width), bf16), sds((rows, tok, width), f32), sds((h, 128), bf16)),
        got,
    )
    parts = [mine] + [from_xor(mine, m) for m in range(1, n_rows)]
    sums = call(
        partial(unpack_kernel, n_rows), tuple(sds(p.shape, f32) for p in params), *parts
    )
    sums = sums[:14] + (sums[14].T,) + sums[15:]
    return (layer_out, grad_input) + tuple(sums)


def solution(mesh):
    split3 = P("rows", "tok", None)
    return jax.shard_map(
        shards,
        mesh=mesh,
        in_specs=(split3, P("rows", "tok"), P("rows", None, None)) + (P(),) * 16 + (split3,),
        out_specs=(split3, split3) + (P(),) * 16,
        check_vma=False,
    )
```

```python
from functools import partial

import jax
import jax.numpy as jnp
from jax import lax
from jax.experimental import pallas as pl
from jax.experimental.pallas import tpu as pltpu
from jax.sharding import PartitionSpec as P


NS_STEPS = 6
EPS = 1e-05
RIDGE = 0.1
FAR = 640.0
SEG_ROWS = 16
GRAD_ROWS = 272

f32 = jnp.float32
bf16 = jnp.bfloat16


def mm(a, b):
    return lax.dot_general(a, b, (((1,), (0,)), ((), ())), preferred_element_type=f32)


def mm_nt(a, b):
    return lax.dot_general(a, b, (((1,), (1,)), ((), ())), preferred_element_type=f32)


def mm_tn(a, b):
    return lax.dot_general(a, b, (((0,), (0,)), ((), ())), preferred_element_type=f32)


def split(a):
    hi = a.astype(bf16)
    return hi, (a - hi.astype(f32)).astype(bf16)


def wide_right(b):
    hi, lo = split(b)
    return jnp.concatenate(
        [jnp.concatenate([hi, lo], 1), jnp.concatenate([hi, jnp.zeros_like(hi)], 1)], 0
    )


def mm_wide(a, wide):
    n = wide.shape[1] // 2
    both = mm(jnp.concatenate(split(a), 1), wide)
    return both[:, :n] + both[:, n:]


def row_sum(a):
    return jnp.sum(a, axis=1, keepdims=True)


def col_sum(a):
    return jnp.sum(a, axis=0, keepdims=True)


def total_of(a):
    return col_sum(row_sum(a))


def both_parts(product, a, b):
    n = b.shape[1]
    both = product(a, jnp.concatenate(split(b), 1))
    return both[:, :n] + both[:, n:]


def pair(a, b):
    return jnp.concatenate([a, b], 1)


def wide_mm(a_pair, wide):
    n = wide.shape[1] // 2
    both = mm(a_pair, wide)
    return both[:, :n] + both[:, n:]


def norm_stats(values):
    n = 1.0 / values.shape[0]
    centre = values - col_sum(values) * n
    scale = lax.rsqrt(col_sum(centre * centre) * n + EPS)
    return centre * scale, scale


def norm_back(d_norm, xhat, scale, gain):
    scaled = d_norm * gain
    n = 1.0 / scaled.shape[0]
    return scale * (scaled - col_sum(scaled) * n - xhat * (col_sum(scaled * xhat) * n))


def iota(shape, dim):
    return lax.broadcasted_iota(jnp.int32, shape, dim)


def row_work(xg, onehot_t, idx, par):
    (gain1, bias1, wq, bq, wk, bk, wv, bv, wo, bo, gain2, bias2, wup, bup, wdown_t, bdown) = par
    tokens = xg.shape[0]
    width = wq.shape[0]
    heads, marks = idx.shape
    size = width // heads
    sharp = size**-0.5
    out_scale = tokens**-0.5
    hm = heads * marks
    hs = range(heads)
    at = [slice(h * marks, (h + 1) * marks) for h in hs]
    rows_of = [slice(h * size, (h + 1) * size) for h in hs]
    chunk = tokens // 4
    chunks = [slice(lo, lo + chunk) for lo in range(0, tokens, chunk)]

    xg_t = xg.astype(f32).T
    x_t, g_t = xg_t[:width], xg_t[width:]
    g16_t = g_t.astype(bf16)
    wqkv = jnp.concatenate([wq, wk, wv], 1)
    wqkv_t = wqkv.astype(f32).T.astype(bf16)
    xhat1, scale1 = norm_stats(x_t)
    normed_t = (xhat1 * gain1 + bias1).astype(bf16)
    qkv_t = mm(wqkv_t, normed_t) + jnp.concatenate([bq, bk, bv], 0)
    qkv16_t = qkv_t.astype(bf16)
    q_t, k_t, v_t = (qkv16_t[i * width : (i + 1) * width] for i in range(3))
    seg_rows = jnp.where(
        (iota(onehot_t.shape, 0) >= 4) & (iota(onehot_t.shape, 0) < 8), 1.0, onehot_t.astype(f32)
    )
    seg_rows = jnp.concatenate(
        [seg_rows, jnp.zeros((width - SEG_ROWS, tokens), f32)], 0
    ).astype(bf16)

    def features(p_t):
        p = p_t.astype(f32)
        sq = p * p
        hi = sq.astype(bf16)
        return jnp.concatenate([p_t, hi, (sq - hi.astype(f32)).astype(bf16), seg_rows], 0)

    feats_q, feats_k = features(q_t), features(k_t)

    idx_row = jnp.concatenate([idx[h : h + 1] for h in hs], 1)
    pick_t = (iota((2 * tokens, hm), 0) == idx_row).astype(f32).astype(bf16)
    qk_t = jnp.concatenate([q_t, k_t], 1)
    seg2 = jnp.concatenate([onehot_t, onehot_t], 1)
    picked = mm(jnp.concatenate([qk_t, seg2], 0), pick_t)
    own = ((iota((width, hm), 0) // size) == (iota((width, hm), 1) // marks)).astype(f32)
    mark_t = picked[:width] * own
    mark_seg = picked[width : width + 8]
    sq = mark_t * mark_t
    half = -0.5 * col_sum(sq)
    half_hi = half.astype(bf16).astype(f32)
    half_mid = (half - half_hi).astype(bf16).astype(f32)
    half_lo = half - half_hi - half_mid
    row8 = iota((8, hm), 0)
    extra = jnp.where(row8 < 4, mark_seg * FAR, 0.0)
    extra = jnp.where(row8 == 4, half_hi, extra)
    extra = jnp.where(row8 == 5, half_mid, extra)
    extra = jnp.where(row8 == 6, half_lo, extra)
    extra = jnp.where(row8 == 7, -FAR, extra)
    pad = jnp.zeros((width - 8, hm), f32)
    right_m = jnp.concatenate([mark_t, -0.5 * own, -0.5 * own, extra, pad], 0).T.astype(bf16)
    sq_hi = sq.astype(bf16).astype(f32)
    left = jnp.concatenate(
        [mark_t, sq_hi, sq - sq_hi, jnp.where(row8 < 4, mark_seg, 1.0), pad], 0
    ).astype(bf16)
    mark16 = mark_t.astype(bf16)

    def near_of(points):
        return jnp.exp(sharp * mm(right_m, points)).astype(bf16)

    eye = (iota((marks, marks), 0) == iota((marks, marks), 1)).astype(f32)
    kernel = [jnp.exp(sharp * mm(right_m[at[h]], left[:, at[h]])) for h in hs]
    gram = [kernel[h] + RIDGE * eye for h in hs]
    sums = [col_sum(gram[h]) for h in hs]
    widest = [jnp.max(sums[h], axis=1, keepdims=True) for h in hs]
    inv2 = [1.0 / (widest[h] * widest[h]) for h in hs]
    gram_wide = [wide_right(gram[h]) for h in hs]
    wo_of = [wo[rows_of[h]] for h in hs]
    rest = [eye - mm_wide(gram[h] * inv2[h], gram_wide[h]) for h in hs]
    v_tok = v_t.astype(f32).T.astype(bf16)
    rests, wides = [rest], []
    near_k, near_q, near_q_tok, summed_t, sent_t, grown = [], [], [], [], [], []
    rest_pair, grown_pair = [], []

    def add_near_k(i):
        half = tokens // 2
        near_k.append(near_of(feats_k[:, i * half : (i + 1) * half]))

    def add_near_q(i):
        near_q.append(near_of(feats_q[:, chunks[i]]))
        near_q_tok.append(near_q[-1].T)

    def add_sums():
        near_k[:] = [jnp.concatenate(near_k, 1)]
        both = mm(near_k[0], v_tok).T
        summed_t.extend(both[rows_of[h], at[h]] for h in hs)

    def add_sent():
        sent_t.extend(both_parts(mm_tn, wo_of[h], summed_t[h]) for h in hs)
        grown.append([mm_wide(sent_t[h], gram_wide[h]) * inv2[h] for h in hs])

    def two_steps(step):
        nxt = rests[step + 1]
        return [rests[step][h] + nxt[h] + mm_wide(rests[step][h], wides[step + 1][h]) for h in hs]

    def grown_by(now, wide):
        return [now[h] + mm_wide(now[h], wide[h]) for h in hs]

    def widen(both):
        return [wide_right(both[h]) for h in hs]

    def add_pairs(step):
        rest_pair.append([pair(*split(rests[step][h])) for h in hs])

    def next_rest():
        wides.append(widen(rests[-1]))
        if len(rests) < NS_STEPS:
            rests.append([mm_wide(rests[-1][h], wides[-1][h]) for h in hs])

    add_near_k(0)
    next_rest()
    add_near_k(1)
    next_rest()
    twice = [widen(two_steps(0))]
    add_sums()
    next_rest()
    add_pairs(0)
    add_near_q(0)
    add_sent()
    next_rest()
    twice.append(widen(two_steps(2)))
    add_pairs(1)
    add_near_q(1)
    grown.extend([None] * NS_STEPS)
    grown[2] = grown_by(grown[0], twice[0])
    next_rest()
    add_near_q(2)
    grown[4] = grown_by(grown[2], twice[1])
    next_rest()
    grown[5] = grown_by(grown[4], wides[4])
    add_near_q(3)
    grown[6] = grown_by(grown[5], wides[5])
    near_k, now = near_k[0], grown[-1]
    near_q = jnp.concatenate(near_q, 1)
    near_q_tok = jnp.concatenate(near_q_tok, 0)
    mixed_t = jnp.concatenate(now, 1).astype(bf16)
    hidden = x_t + (mm(mixed_t, near_q) * out_scale + bo)
    twice.append(widen(two_steps(4)))
    inverse = [gram[h] * inv2[h] for h in hs]
    for wide in twice:
        inverse = grown_by(inverse, wide)
    inverse_wide = widen(inverse)
    grown[1] = grown_by(grown[0], wides[0])
    grown[3] = grown_by(grown[2], wides[2])
    for step in range(2, NS_STEPS):
        add_pairs(step)
    grown_pair = [[grown[step][h].T.astype(bf16) for h in hs] for step in range(NS_STEPS)]
    wup_t = wup.astype(f32).T.astype(bf16)
    d_act = mm_tn(wdown_t, g16_t)
    xhat2, scale2 = norm_stats(hidden)
    normed2_t = (xhat2 * gain2 + bias2).astype(bf16)
    inner = mm(wup_t, normed2_t) + bup
    c = (2.0 / jnp.pi) ** 0.5
    inner2 = inner * inner
    th = jnp.tanh(c * inner * (1.0 + 0.044715 * inner2))
    act = (0.5 * inner * (1.0 + th)).astype(bf16)

    slope = 0.5 * (1.0 + th) + 0.5 * inner * (1.0 - th * th) * (
        c * (1.0 + (3.0 * 0.044715) * inner2)
    )
    d_inner = (d_act * slope).astype(bf16)
    d_norm2 = mm(wup, d_inner)
    layer_out = hidden + (mm(wdown_t, act) + bdown)
    d_hidden = g_t + norm_back(d_norm2, xhat2, scale2, gain2)
    d_branch = d_hidden.astype(bf16)
    d_sent_t = mm(d_branch, near_q_tok) * out_scale
    back = [d_sent_t[:, at[h]] for h in hs]

    gram_pair = [pair(*split(gram[h])) for h in hs]
    sent_pair = [pair(*split(sent_t[h].T)) for h in hs]
    kernel_inv = [kernel[h] * inv2[h] for h in hs]
    widest_a = [(2.0 / widest[h]) * (eye - rests[0][h]) for h in hs]
    widest_b = [(2.0 / widest[h]) * grown[0][h] for h in hs]
    mark_both = jnp.concatenate([mark16, own.astype(bf16)], 0)
    mark_ones = [
        jnp.concatenate([mark16[:, at[h]], jnp.ones((16, marks), bf16)], 0) for h in hs
    ]
    top_part = []
    for h in hs:
        top = (sums[h] == widest[h]).astype(f32)
        top = top * (1.0 / row_sum(top))
        seen = kernel[h].astype(bf16)
        along = jnp.broadcast_to(top, (16, marks)).astype(bf16)
        top_part.append(
            top * mm(mark_ones[h], seen)
            + mm_nt(mark_ones[h], along)[:, :1] * mm(along, seen)[:1]
        )
    mixed_m = mixed_t.astype(f32).T.astype(bf16)
    q_tok = q_t.astype(f32).T.astype(bf16)
    k_tok = k_t.astype(f32).T.astype(bf16)
    ones_tok = jnp.ones((tokens, width), bf16)
    d_start = [mm_wide(back[h], inverse_wide[h]) for h in hs]
    d_summed = [both_parts(mm, wo_of[h], d_start[h]) for h in hs]
    none = jnp.zeros((size, marks), f32)
    d_summed_t = jnp.concatenate(
        [jnp.concatenate([d_summed[h] if g == h else none for g in hs], 1) for h in hs], 0
    )
    d_summed_m = d_summed_t.T.astype(bf16)
    def stays(pull, p_t):
        both = mm(mark_both, pull)
        return sharp * (both[:width] - both[width:] * p_t.astype(f32))

    pulls_q, toks = [], []

    def pull_some(i):
        now_at = chunks[i]
        pull = mm(mixed_m, d_branch[:, now_at]) * out_scale
        pulls_q.append((pull * near_q[:, now_at].astype(f32)).astype(bf16))

    def pull_rest():
        pull = mm(d_summed_m, v_t)
        pulls_q.append((pull * near_k.astype(f32)).astype(bf16))

    def add_tok(pull, tok):
        toks.append(mm(pull, pair(tok, ones_tok)))

    def add_tok_q():
        pulls_q[:4] = [jnp.concatenate(pulls_q[:4], 1)]
        add_tok(pulls_q[0], q_tok)

    def add_tok_k():
        add_tok(pulls_q[1], k_tok)

    beside = [
        [partial(pull_some, 0), partial(pull_some, 1)],
        [partial(pull_some, 2), partial(pull_some, 3)],
        [add_tok_q],
        [pull_rest],
        [add_tok_k],
        [],
    ]
    d_rest = None
    for step in reversed(range(NS_STEPS)):
        outer = [mm(grown_pair[step][h], back[h].astype(bf16)) for h in hs]
        back = [back[h] + mm_wide(back[h], wides[step][h]) for h in hs]
        if d_rest is None:
            d_rest = outer
        else:
            d_rest = [
                mm_wide(d_rest[h], wides[step][h])
                + wide_mm(rest_pair[step][h], wide_right(d_rest[h]))
                + outer[h]
                for h in hs
            ]
        for work in beside[NS_STEPS - 1 - step]:
            work()
    pull_q, pull_k = pulls_q
    d_gram = [
        wide_mm(sent_pair[h], wide_right(back[h]))
        - mm_wide(d_rest[h], gram_wide[h])
        - wide_mm(gram_pair[h], wide_right(d_rest[h]))
        for h in hs
    ]
    tok_both = (toks[0] + toks[1]).T
    tok_t, tok_sum = tok_both[:width], tok_both[width : width + 1]
    stay_q, stay_k = stays(pull_q, q_t), stays(pull_k, k_t)
    gram_part = []
    for h in hs:
        d_widest = total_of(d_rest[h] * widest_a[h]) - total_of(back[h] * widest_b[h])
        weighted = ((d_gram[h] + d_gram[h].T) * kernel_inv[h]).astype(bf16)
        gram_part.append(mm(mark_ones[h], weighted) + d_widest * top_part[h])
    gram_part = jnp.concatenate(gram_part, 1)
    d_mark_t = (
        (tok_t + gram_part[:width] - mark_t * (tok_sum + gram_part[width : width + 1])) * own
    ).astype(bf16)
    idx_col = jnp.broadcast_to(idx_row.astype(f32), (8, hm)).T[:, :1].astype(jnp.int32)
    pick_m = (iota((hm, 2 * tokens), 1) == idx_col).astype(f32).astype(bf16)
    moved = mm(d_mark_t, pick_m)
    dq = (stay_q + sharp * moved[:, :tokens]).astype(bf16)
    dk = (stay_k + sharp * moved[:, tokens:]).astype(bf16)
    dv = mm(d_summed_t.astype(bf16), near_k).astype(bf16)
    dqkv = jnp.concatenate([dq, dk, dv], 0)
    d_normed = mm(wqkv, dqkv)
    grad_in = d_hidden + norm_back(d_normed, xhat1, scale1, gain1)
    out = jnp.concatenate([layer_out, grad_in], 0).T.astype(bf16)

    ones16 = jnp.ones((16, tokens), bf16)
    g_down = mm_nt(g16_t, act)
    g_up = mm_nt(jnp.concatenate([normed2_t, ones16], 0), d_inner)
    g_qkv = mm_nt(jnp.concatenate([normed_t, ones16], 0), dqkv)
    g_bias = mm_nt(ones16, jnp.concatenate([g16_t, d_branch], 0))
    g_wo = jnp.concatenate(
        [mm_nt(summed_t[h].astype(bf16), d_start[h].astype(bf16)) for h in hs], 0
    )
    columns = [
        row_sum(d_normed * xhat1),
        row_sum(d_normed),
        row_sum(d_norm2 * xhat2),
        row_sum(d_norm2),
    ]
    lane = iota((width, 128), 1)
    norms = sum(jnp.where(lane == i, col, 0.0) for i, col in enumerate(columns)).T[:8]
    g_bqkv = g_qkv[width : width + 1]
    vecs = [
        g_up[width : width + 1],
        pair(g_bias[:1, :width], g_bqkv[:, :width]),
        g_bqkv[:, width:],
        pair(g_bias[:1, width:], norms[0:1]),
        pair(norms[1:2], norms[2:3]),
        pair(norms[3:4], jnp.zeros((1, width), f32)),
        jnp.zeros((GRAD_ROWS - 262, 128), f32),
    ]
    grads = jnp.concatenate(
        [
            g_up[:width],
            g_down[:width],
            g_qkv[:width, : 2 * width],
            pair(g_qkv[:width, 2 * width :], g_wo),
        ]
        + vecs,
        0,
    )
    return out, grads


MATRICES = (2, 4, 6, 8, 12, 14)
VECTORS = (0, 1, 3, 5, 7, 9, 10, 11, 13, 15)


def read_params(mats, vec_cols):
    par = [None] * 16
    for i, ref in zip(MATRICES, mats):
        par[i] = ref[...]
    for row, i in enumerate(VECTORS):
        wide = par[12].shape[1] if i == 13 else par[2].shape[0]
        par[i] = vec_cols[:wide, row : row + 1]
    return tuple(par)


def main_kernel(tok_block, blk_ref, idx_ref, vec_ref, *refs):
    mats, (out_ref, keep_ref, send_ref) = refs[:6], refs[6:]
    vec_cols = vec_ref[...].T
    blocks = blk_ref.shape[0]
    tokens = blocks * tok_block
    row = jnp.minimum(lax.axis_index("tok"), idx_ref.shape[0] - 1)
    xg = blk_ref[:, :tok_block, :].reshape(tokens, 128)
    ids = blk_ref[:, tok_block:, :].astype(f32)
    half = iota((SEG_ROWS, 128), 1) < tok_block
    onehot_t = jnp.concatenate(
        [jnp.where(half, ids[2 * j], ids[2 * j + 1]) for j in range(blocks // 2)], 1
    ).astype(bf16)
    out, grads = row_work(xg, onehot_t, idx_ref[row], read_params(mats, vec_cols))
    out_ref[...] = out.reshape(blocks, tok_block, 128)
    first = lax.rem(lax.axis_index("rows"), 2) == 0
    h = GRAD_ROWS // 2
    keep_ref[...] = jnp.where(first, grads[:h], grads[h:])
    send_ref[...] = jnp.where(first, grads[h:], grads[:h])


def pack_kernel(xg_ref, s_ref, *refs):
    vecs, (out_ref, vec_ref) = refs[:-2], refs[-2:]
    rows, tok, width = xg_ref.shape
    out_ref[:rows, :tok, :] = xg_ref[...]
    out_ref[rows:] = jnp.zeros((out_ref.shape[0] - rows,) + out_ref.shape[1:], bf16)
    seg = s_ref[...]
    seg = jnp.concatenate([seg, seg], 1)
    for r in range(rows):
        ids = jnp.broadcast_to(seg[r : r + 1], (SEG_ROWS, width))
        out_ref[r, tok:, :] = (ids == iota((SEG_ROWS, width), 0)).astype(f32).astype(bf16)
    for i, ref in enumerate(vecs):
        vec_ref[i : i + 1, : ref.shape[0]] = ref[...].astype(f32).reshape(1, -1)


def sum_kernel(tok, got_ref, sum_ref):
    total = got_ref[0, tok:, :].astype(f32)
    for j in range(1, got_ref.shape[0]):
        total = total + got_ref[j, tok:, :].astype(f32)
    sum_ref[...] = total.astype(bf16)


def rows_kernel(got_ref, out_ref, grad_ref):
    rows, tok, width = out_ref.shape
    out_ref[...] = got_ref[:rows, :tok, :width]
    grad_ref[...] = got_ref[:rows, :tok, width:].astype(f32)


def unpack_kernel(n_parts, *refs):
    parts, outs = refs[:n_parts], refs[n_parts:]
    halves = [
        sum([p[...].astype(f32) for p in parts[core + 2 :: 2]], parts[core][...].astype(f32))
        for core in range(2)
    ]
    first = lax.rem(lax.axis_index("rows"), 2) == 0
    a = jnp.where(first, halves[0], halves[1])
    b = jnp.where(first, halves[1], halves[0])
    whole = jnp.concatenate([a, b], 0)
    (gain1, bias1, wq, bq, wk, bk, wv, bv, wo, bo, gain2, bias2, wup, bup, wdown_t, bdown) = outs
    wup[...] = whole[0:64]
    wdown_t[...] = whole[64:128]
    wq[...] = whole[128:192, :64]
    wk[...] = whole[128:192, 64:]
    wv[...] = whole[192:256, :64]
    wo[...] = whole[192:256, 64:]
    bup[...] = whole[256]
    bdown[...] = whole[257, :64]
    bq[...] = whole[257, 64:]
    bk[...] = whole[258, :64]
    bv[...] = whole[258, 64:]
    bo[...] = whole[259, :64]
    gain1[...] = whole[259, 64:]
    bias1[...] = whole[260, :64]
    gain2[...] = whole[260, 64:]
    bias2[...] = whole[261, :64]


def call(kernel, outs, *args, mib=12):
    vmem = pl.BlockSpec(memory_space=pltpu.VMEM)
    return pl.pallas_call(
        kernel,
        out_shape=outs,
        in_specs=[vmem] * len(args),
        out_specs=jax.tree.map(lambda _: vmem, outs),
        compiler_params=pltpu.CompilerParams(vmem_limit_bytes=mib * 1024 * 1024),
    )(*args)


def shards(tokens_in, segments, landmark_index, *rest):
    params, grad_out = rest[:14] + (rest[14].T, rest[15]), rest[16]
    rows, tok, width = tokens_in.shape
    n_tok = lax.axis_size("tok")
    n_rows = lax.axis_size("rows")
    sds = jax.ShapeDtypeStruct
    sent, vecs = call(
        pack_kernel,
        (sds((n_tok, tok + SEG_ROWS, 128), bf16), sds((16, 128), f32)),
        jnp.concatenate([tokens_in, grad_out], 2),
        segments,
        *[params[i] for i in VECTORS],
        mib=4,
    )
    got = lax.all_to_all(sent, "tok", 0, 0, tiled=True)
    h = GRAD_ROWS // 2
    out, keep, send = call(
        partial(main_kernel, tok),
        (sds((n_tok, tok, 128), bf16), sds((h, 128), f32), sds((h, 128), f32)),
        got,
        landmark_index,
        vecs,
        *[params[i] for i in MATRICES],
        mib=12 * max(1, n_tok * tok // 512),
    )
    def from_xor(array, m):
        return lax.ppermute(array, "rows", [(i, i ^ m) for i in range(n_rows)])

    total = (keep + from_xor(send, 1)).astype(bf16)
    back = jnp.concatenate([out, jnp.broadcast_to(total, (n_tok, h, 128))], 1)
    got = lax.all_to_all(back, "tok", 0, 0, tiled=True)
    mine = call(partial(sum_kernel, tok), sds((h, 128), bf16), got)
    parts = [mine] + [from_xor(mine, m) for m in range(1, n_rows)]
    layer_out, grad_input = call(
        rows_kernel, (sds((rows, tok, width), bf16), sds((rows, tok, width), f32)), got
    )
    sums = call(
        partial(unpack_kernel, n_rows), tuple(sds(p.shape, f32) for p in params), *parts
    )
    sums = sums[:14] + (sums[14].T,) + sums[15:]
    return (layer_out, grad_input) + tuple(sums)


def solution(mesh):
    split3 = P("rows", "tok", None)
    return jax.shard_map(
        shards,
        mesh=mesh,
        in_specs=(split3, P("rows", "tok"), P("rows", None, None)) + (P(),) * 16 + (split3,),
        out_specs=(split3, split3) + (P(),) * 16,
        check_vma=False,
    )
```

```python
from functools import partial

import jax
import jax.numpy as jnp
from jax import lax
from jax.experimental import pallas as pl
from jax.experimental.pallas import tpu as pltpu
from jax.sharding import PartitionSpec as P


NS_STEPS = 6
EPS = 1e-05
RIDGE = 0.1
FAR = 640.0
SEG_ROWS = 8
GRAD_ROWS = 272
NORM_ROW = 131

LOG2_E = 1.4426950408889634

f32 = jnp.float32
bf16 = jnp.bfloat16


def mm(a, b):
    return lax.dot_general(a, b, (((1,), (0,)), ((), ())), preferred_element_type=f32)


def mm_nt(a, b):
    return lax.dot_general(a, b, (((1,), (1,)), ((), ())), preferred_element_type=f32)


def mm_tn(a, b):
    return lax.dot_general(a, b, (((0,), (0,)), ((), ())), preferred_element_type=f32)


def split(a):
    hi = a.astype(bf16)
    return hi, (a - hi.astype(f32)).astype(bf16)


def wide_right(b):
    hi, lo = split(b)
    return jnp.concatenate(
        [jnp.concatenate([hi, lo], 1), jnp.concatenate([hi, jnp.zeros_like(hi)], 1)], 0
    )


def mm_wide(a, wide):
    n = wide.shape[1] // 2
    both = mm(jnp.concatenate(split(a), 1), wide)
    return both[:, :n] + both[:, n:]


def row_sum(a):
    return jnp.sum(a, axis=1, keepdims=True)


def col_sum(a):
    return jnp.sum(a, axis=0, keepdims=True)


def total_of(a):
    return col_sum(row_sum(a))


def both_parts(product, a, b):
    n = b.shape[1]
    both = product(a, jnp.concatenate(split(b), 1))
    return both[:, :n] + both[:, n:]


def pair(a, b):
    return jnp.concatenate([a, b], 1)


def wide_mm(a_pair, wide):
    n = wide.shape[1] // 2
    both = mm(a_pair, wide)
    return both[:, :n] + both[:, n:]


def norm_stats(values):
    n = 1.0 / values.shape[0]
    centre = values - col_sum(values) * n
    scale = lax.rsqrt(col_sum(centre * centre) * n + EPS)
    return centre * scale, scale


def norm_back(d_norm, xhat, scale, gain):
    scaled = d_norm * gain
    n = 1.0 / scaled.shape[0]
    return scale * (scaled - col_sum(scaled) * n - xhat * (col_sum(scaled * xhat) * n))


def iota(shape, dim):
    return lax.broadcasted_iota(jnp.int32, shape, dim)


def row_work(xg, onehot_t, idx, par):
    (gain1, bias1, wq, bq, wk, bk, wv, bv, wo, bo, gain2, bias2, wup, bup, wdown_t, bdown) = par
    tokens = xg.shape[0]
    width = wq.shape[0]
    heads, marks = idx.shape
    size = width // heads
    sharp = size**-0.5
    sharp2 = sharp * LOG2_E
    out_scale = tokens**-0.5
    hm = heads * marks
    hs = range(heads)
    at = [slice(h * marks, (h + 1) * marks) for h in hs]
    rows_of = [slice(h * size, (h + 1) * size) for h in hs]
    chunk = tokens // 4
    chunks = [slice(lo, lo + chunk) for lo in range(0, tokens, chunk)]

    xg_t = xg.astype(f32).T
    x_t, g_t = xg_t[:width], xg_t[width:]
    g16_t = g_t.astype(bf16)
    wqkv = jnp.concatenate([wq, wk, wv], 1)
    wqkv_t = wqkv.astype(f32).T.astype(bf16)
    xhat1, scale1 = norm_stats(x_t)
    normed_t = (xhat1 * gain1 + bias1).astype(bf16)
    qkv_t = mm(wqkv_t, normed_t) + jnp.concatenate([bq, bk, bv], 0)
    qkv16_t = qkv_t.astype(bf16)
    q_t, k_t, v_t = (qkv16_t[i * width : (i + 1) * width] for i in range(3))
    seg_rows = jnp.where(
        (iota(onehot_t.shape, 0) >= 4) & (iota(onehot_t.shape, 0) < 8), 1.0, onehot_t.astype(f32)
    )
    seg_rows = jnp.concatenate(
        [seg_rows, jnp.zeros((width - SEG_ROWS, tokens), f32)], 0
    ).astype(bf16)

    def features(p_t):
        p = p_t.astype(f32)
        sq = p * p
        hi = sq.astype(bf16)
        return jnp.concatenate([p_t, seg_rows, hi, (sq - hi.astype(f32)).astype(bf16)], 0)

    feats_q, feats_k = features(q_t), features(k_t)

    idx_row = jnp.concatenate([idx[h : h + 1] for h in hs], 1)
    pick_t = (iota((2 * tokens, hm), 0) == idx_row).astype(f32).astype(bf16)
    qk_t = jnp.concatenate([q_t, k_t], 1)
    ones16 = jnp.ones((16, tokens), bf16)
    normed_ones = jnp.concatenate([normed_t, ones16], 0)
    seg2 = jnp.concatenate([onehot_t, onehot_t], 1)
    picked = mm(jnp.concatenate([qk_t, seg2], 0), pick_t)
    own = ((iota((width, hm), 0) // size) == (iota((width, hm), 1) // marks)).astype(f32)
    mark_t = picked[:width] * own
    mark_seg = picked[width : width + 8]
    sq = mark_t * mark_t
    half = -0.5 * col_sum(sq)
    half_hi = half.astype(bf16).astype(f32)
    half_mid = (half - half_hi).astype(bf16).astype(f32)
    half_lo = half - half_hi - half_mid
    row8 = iota((8, hm), 0)
    extra = jnp.where(row8 < 4, mark_seg * FAR, 0.0)
    extra = jnp.where(row8 == 4, half_hi, extra)
    extra = jnp.where(row8 == 5, half_mid, extra)
    extra = jnp.where(row8 == 6, half_lo, extra)
    extra = jnp.where(row8 == 7, -FAR, extra)
    pad = jnp.zeros((width - 8, hm), f32)
    squares = iota((hm, 2 * width), 1) % width // size == iota((hm, 2 * width), 0) // marks
    right_m = pair(
        jnp.concatenate([mark_t, extra, pad], 0).T.astype(bf16),
        jnp.where(squares, -0.5, 0.0).astype(bf16),
    )
    sq_hi = sq.astype(bf16).astype(f32)
    left = jnp.concatenate(
        [mark_t, jnp.where(row8 < 4, mark_seg, 1.0), pad, sq_hi, sq - sq_hi], 0
    ).astype(bf16)
    mark16 = mark_t.astype(bf16)

    def near_of(points):
        return jnp.exp2(sharp2 * mm(right_m, points)).astype(bf16)

    eye = (iota((marks, marks), 0) == iota((marks, marks), 1)).astype(f32)
    kernel = [jnp.exp2(sharp2 * mm(right_m[at[h]], left[:, at[h]])) for h in hs]
    gram = [kernel[h] + RIDGE * eye for h in hs]
    sums = [col_sum(gram[h]) for h in hs]
    widest = [jnp.max(sums[h], axis=1, keepdims=True) for h in hs]
    inv2 = [1.0 / (widest[h] * widest[h]) for h in hs]
    gram_wide = [wide_right(gram[h]) for h in hs]
    wo_of = [wo[rows_of[h]] for h in hs]
    rest = [eye - mm_wide(gram[h] * inv2[h], gram_wide[h]) for h in hs]
    v_tok = v_t.astype(f32).T.astype(bf16)
    rests, wides = [rest], []
    near_k, near_q, near_q_tok, summed_t, sent_t, grown = [], [], [], [], [], []

    def add_near_k(i):
        half = tokens // 2
        near_k.append(near_of(feats_k[:, i * half : (i + 1) * half]))

    def add_near_q(i):
        near_q.append(near_of(feats_q[:, chunks[i]]))
        near_q_tok.append(near_q[-1].T)

    def add_sums():
        near_k[:] = [jnp.concatenate(near_k, 1)]
        both = mm(near_k[0], v_tok).T
        summed_t.extend(both[rows_of[h], at[h]] for h in hs)

    def add_sent():
        sent_t.extend(both_parts(mm_tn, wo_of[h], summed_t[h]) for h in hs)
        grown.append([mm_wide(sent_t[h], gram_wide[h]) * inv2[h] for h in hs])

    def two_steps(step):
        nxt = rests[step + 1]
        return [rests[step][h] + nxt[h] + mm_wide(rests[step][h], wides[step + 1][h]) for h in hs]

    def grown_by(now, wide):
        return [now[h] + mm_wide(now[h], wide[h]) for h in hs]

    def widen(both):
        return [wide_right(both[h]) for h in hs]

    def next_rest():
        wides.append(widen(rests[-1]))
        if len(rests) < NS_STEPS:
            rests.append([mm_wide(rests[-1][h], wides[-1][h]) for h in hs])

    add_near_k(0)
    next_rest()
    add_near_k(1)
    next_rest()
    twice = [widen(two_steps(0))]
    add_sums()
    next_rest()
    add_near_q(0)
    add_sent()
    next_rest()
    twice.append(widen(two_steps(2)))
    add_near_q(1)
    grown.extend([None] * NS_STEPS)
    grown[2] = grown_by(grown[0], twice[0])
    next_rest()
    add_near_q(2)
    grown[4] = grown_by(grown[2], twice[1])
    next_rest()
    grown[5] = grown_by(grown[4], wides[4])
    add_near_q(3)
    grown[6] = grown_by(grown[5], wides[5])
    near_k, now = near_k[0], grown[-1]
    near_q = jnp.concatenate(near_q, 1)
    near_q_tok = jnp.concatenate(near_q_tok, 0)
    mixed_t = jnp.concatenate(now, 1).astype(bf16)
    hidden = x_t + (mm(mixed_t, near_q) * out_scale + bo)
    twice.append(widen(two_steps(4)))
    inverse = [gram[h] * inv2[h] for h in hs]
    for wide in twice:
        inverse = grown_by(inverse, wide)
    inverse_wide = widen(inverse)
    grown[1] = grown_by(grown[0], wides[0])
    grown[3] = grown_by(grown[2], wides[2])
    beside_rest = [
        [pair(rests[step][h], grown[step][h].T).astype(bf16) for h in hs]
        for step in range(NS_STEPS)
    ]
    normed_mark = pair(mm(normed_ones, pick_t[:tokens]), mm(normed_ones, pick_t[tokens:])).astype(bf16)
    wup_t = wup.astype(f32).T.astype(bf16)
    d_act = mm_tn(wdown_t, g16_t)
    xhat2, scale2 = norm_stats(hidden)
    normed2_t = (xhat2 * gain2 + bias2).astype(bf16)
    inner = mm(wup_t, normed2_t) + bup
    c = (2.0 / jnp.pi) ** 0.5
    inner2 = inner * inner
    th = jnp.tanh(c * inner * (1.0 + 0.044715 * inner2))
    act = (0.5 * inner * (1.0 + th)).astype(bf16)

    slope = 0.5 * (1.0 + th) + 0.5 * inner * (1.0 - th * th) * (
        c * (1.0 + (3.0 * 0.044715) * inner2)
    )
    d_inner = (d_act * slope).astype(bf16)
    d_norm2 = mm(wup, d_inner)
    layer_out = hidden + (mm(wdown_t, act) + bdown)
    d_hidden = g_t + norm_back(d_norm2, xhat2, scale2, gain2)
    d_branch = d_hidden.astype(bf16)
    d_sent_t = mm(d_branch, near_q_tok) * out_scale
    back = [d_sent_t[:, at[h]] for h in hs]

    beside_gram = [pair(sent_t[h].T, -gram[h]).astype(bf16) for h in hs]
    kernel_inv = [kernel[h] * inv2[h] for h in hs]
    widest_a = [(2.0 / widest[h]) * (eye - rests[0][h]) for h in hs]
    widest_b = [(2.0 / widest[h]) * grown[0][h] for h in hs]
    mark_both = jnp.concatenate([mark16, own.astype(bf16)], 0)
    mark_ones = [
        jnp.concatenate([mark16[:, at[h]], jnp.ones((16, marks), bf16)], 0) for h in hs
    ]
    top_part = []
    for h in hs:
        top = (sums[h] == widest[h]).astype(f32)
        top = top * (1.0 / row_sum(top))
        seen = kernel[h].astype(bf16)
        along = jnp.broadcast_to(top, (16, marks)).astype(bf16)
        top_part.append(
            top * mm(mark_ones[h], seen)
            + mm_nt(mark_ones[h], along)[:, :1] * mm(along, seen)[:1]
        )
    mixed_m = (jnp.concatenate(now, 1) * out_scale).T.astype(bf16)
    q_tok = q_t.astype(f32).T.astype(bf16)
    k_tok = k_t.astype(f32).T.astype(bf16)
    ones_tok = jnp.ones((tokens, width), bf16)
    d_start = [mm_wide(back[h], inverse_wide[h]) for h in hs]
    d_summed = [both_parts(mm, wo_of[h], d_start[h]) for h in hs]
    none = jnp.zeros((size, marks), f32)
    d_summed_t = jnp.concatenate(
        [jnp.concatenate([d_summed[h] if g == h else none for g in hs], 1) for h in hs], 0
    )
    d_summed_m = d_summed_t.T.astype(bf16)
    def stays(pull, p_t):
        both = mm(mark_both, pull)
        return sharp * (both[:width] - both[width:] * p_t.astype(f32))

    pulls_q, toks = [], []

    def pull_some(i):
        now_at = chunks[i]
        pulls_q.append(mm(mixed_m, d_branch[:, now_at]).astype(bf16) * near_q[:, now_at])

    def pull_rest():
        pulls_q.append(mm(d_summed_m, v_t).astype(bf16) * near_k)

    def add_tok(pull, tok):
        toks.append(mm(pull, pair(tok, ones_tok)))

    def add_tok_q():
        pulls_q[:4] = [jnp.concatenate(pulls_q[:4], 1)]
        add_tok(pulls_q[0], q_tok)

    def add_tok_k():
        add_tok(pulls_q[1], k_tok)

    early = {}

    def add_down():
        early["down"] = mm_nt(g16_t, act)

    def add_up():
        early["up"] = mm_nt(jnp.concatenate([normed2_t, ones16], 0), d_inner)

    def add_bias():
        early["bias"] = mm_nt(ones16, jnp.concatenate([g16_t, d_branch], 0))

    def add_wo():
        early["wo"] = jnp.concatenate(
            [mm_nt(summed_t[h].astype(bf16), d_start[h].astype(bf16)) for h in hs], 0
        )

    def add_stay():
        stay_q, stay_k = stays(pulls_q[0], q_t), stays(pulls_q[1], k_t)
        dv = mm(d_summed_t.astype(bf16), near_k)
        early["stay"] = jnp.concatenate([stay_q, stay_k, dv], 0).astype(bf16)

    def add_qkv():
        early["qkv"] = mm_nt(normed_ones, early["stay"])

    def add_normed():
        early["normed"] = mm(wqkv, early["stay"])

    beside = [
        [partial(pull_some, 0), partial(pull_some, 1), partial(pull_some, 2), partial(pull_some, 3)],
        [add_tok_q, pull_rest],
        [add_tok_k],
        [add_stay],
        [add_up, add_down],
        [add_qkv, add_normed, add_bias, add_wo],
    ]
    b16 = [back[h].astype(bf16) for h in hs]
    last = NS_STEPS - 1
    d_rest = [mm(beside_rest[last][h][:, marks:], b16[h]) for h in hs]
    back = [back[h] + wide_mm(b16[h], wides[last][h][:marks]) for h in hs]
    for step in reversed(range(NS_STEPS)):
        if step < last:
            both16 = [
                jnp.concatenate([d_rest[h].astype(bf16), back[h].astype(bf16)], 0) for h in hs
            ]
            turned = [wide_mm(both16[h], wides[step][h][:marks]) for h in hs]
            back = [back[h] + turned[h][marks:] for h in hs]
            d_rest = [turned[h][:marks] + mm(beside_rest[step][h], both16[h]) for h in hs]
        for work in beside[last - step]:
            work()
    d16 = [d_rest[h].astype(bf16) for h in hs]
    d_gram = [
        mm(beside_gram[h], jnp.concatenate([back[h].astype(bf16), d16[h]], 0))
        - wide_mm(d16[h], gram_wide[h][:marks])
        for h in hs
    ]
    tok_both = (toks[0] + toks[1]).T
    tok_t, tok_sum = tok_both[:width], tok_both[width : width + 1]
    stay, d_normed_tok = early["stay"], early["normed"]
    gram_part = []
    for h in hs:
        d_widest = total_of(d_rest[h] * widest_a[h]) - total_of(back[h] * widest_b[h])
        weighted = ((d_gram[h] + d_gram[h].T) * kernel_inv[h]).astype(bf16)
        gram_part.append(mm(mark_ones[h], weighted) + d_widest * top_part[h])
    gram_part = jnp.concatenate(gram_part, 1)
    d_mark_t = (
        (tok_t + gram_part[:width] - mark_t * (tok_sum + gram_part[width : width + 1])) * own
    ).astype(bf16)
    g_bias, g_wo = early["bias"], early["wo"]
    g_down, g_up = early["down"], early["up"]
    by_mark = sharp * pair(
        mm_nt(normed_mark[:, :hm], d_mark_t), mm_nt(normed_mark[:, hm:], d_mark_t)
    )
    g_qkv = early["qkv"] + pair(by_mark, jnp.zeros((width + 16, width), f32))
    columns = [
        row_sum(d_norm2 * xhat2),
        row_sum(d_norm2),
    ]
    lane = iota((width, 128), 1)
    norms = sum(jnp.where(lane == i, col, 0.0) for i, col in enumerate(columns)).T[:8]
    g_bqkv = g_qkv[width : width + 1]
    blank = jnp.zeros((1, 2 * width), f32)
    grads = jnp.concatenate(
        [
            g_up[:width],
            g_down[:width],
            g_up[width : width + 1],
            pair(g_bias[:1, :width], g_bqkv[:, :width]),
            g_bqkv[:, width:],
        ]
        + [blank] * 5
        + [
            g_qkv[:width, : 2 * width],
            pair(g_qkv[:width, 2 * width :], g_wo),
            pair(g_bias[:1, width:], norms[0:1]),
            pair(norms[1:2], blank[:, :width]),
        ]
        + [blank] * 6,
        0,
    )
    later = (d_mark_t, d_normed_tok, d_hidden, xhat1, scale1, layer_out)
    return later, grads


def row_end(later, idx, par):
    gain1, wq, wk = par
    d_mark_t, d_normed_tok, d_hidden, xhat1, scale1, layer_out = later
    width, tokens = xhat1.shape
    heads, marks = idx.shape
    hm = heads * marks
    idx_row = jnp.concatenate([idx[h : h + 1] for h in range(heads)], 1)
    idx_col = jnp.broadcast_to(idx_row.astype(f32), (8, hm)).T[:, :1].astype(jnp.int32)
    tok_lane = iota((hm, tokens), 1)
    pick_m = jnp.concatenate([tok_lane == idx_col, tok_lane + tokens == idx_col], 0)
    pick_m = pick_m.astype(f32).astype(bf16)
    onto = mm(jnp.concatenate([wq, wk], 0), d_mark_t).astype(bf16)
    moved = mm(pair(onto[:width], onto[width:]), pick_m)
    d_normed = d_normed_tok + (width // heads) ** -0.5 * moved
    grad_in = d_hidden + norm_back(d_normed, xhat1, scale1, gain1)
    lane = iota((width, 128), 1)
    sums = jnp.where(lane == 0, row_sum(d_normed * xhat1), 0.0) + jnp.where(
        lane == 1, row_sum(d_normed), 0.0
    )
    sums = sums.T
    return jnp.concatenate([layer_out, grad_in], 0).T.astype(bf16), pair(sums[:1], sums[1:2])


MATRICES = (2, 4, 6, 8, 12, 14)
VECTORS = (0, 1, 3, 5, 7, 9, 10, 11, 13, 15)


def read_params(mats, vec_cols):
    par = [None] * 16
    for i, ref in zip(MATRICES, mats):
        par[i] = ref[...]
    for row, i in enumerate(VECTORS):
        wide = par[12].shape[1] if i == 13 else par[2].shape[0]
        par[i] = vec_cols[:wide, row : row + 1]
    return tuple(par)


def own_row(idx_ref):
    return idx_ref[jnp.minimum(lax.axis_index("tok"), idx_ref.shape[0] - 1)]


def main_kernel(tok_block, blk_ref, idx_ref, vec_ref, *refs):
    mats, later_refs, (keep_ref, send_ref) = refs[:6], refs[6:-2], refs[-2:]
    blocks = blk_ref.shape[0]
    tokens = blocks * tok_block
    xg = blk_ref[:, :tok_block, :].reshape(tokens, 128)
    ids = blk_ref[:, tok_block:, :].astype(f32)
    half = iota((SEG_ROWS, 128), 1) < tok_block
    onehot_t = jnp.concatenate(
        [jnp.where(half, ids[2 * j], ids[2 * j + 1]) for j in range(blocks // 2)], 1
    ).astype(bf16)
    later, grads = row_work(xg, onehot_t, own_row(idx_ref), read_params(mats, vec_ref[...].T))
    for ref, value in zip(later_refs, later):
        ref[...] = value
    first = lax.rem(lax.axis_index("rows"), 2) == 0
    h = GRAD_ROWS // 2
    keep_ref[...] = jnp.where(first, grads[:h], grads[h:])
    send_ref[...] = jnp.where(first, grads[h:], grads[:h])


def end_kernel(idx_ref, vec_ref, wq_ref, wk_ref, *refs):
    later, out_ref, norm_ref = [ref[...] for ref in refs[:-2]], refs[-2], refs[-1]
    gain1 = vec_ref[...].T[: wq_ref.shape[0], :1]
    out, sums = row_end(later, own_row(idx_ref), (gain1, wq_ref[...], wk_ref[...]))
    out_ref[...] = out.reshape(out_ref.shape)
    norm_ref[...] = jnp.where(iota(norm_ref.shape, 0) == NORM_ROW, sums, 0.0)


def pack_kernel(xg_ref, s_ref, *refs):
    vecs, (out_ref, vec_ref) = refs[:-2], refs[-2:]
    rows, tok, width = xg_ref.shape
    out_ref[:rows, :tok, :] = xg_ref[...]
    out_ref[rows:] = jnp.zeros((out_ref.shape[0] - rows,) + out_ref.shape[1:], bf16)
    seg = s_ref[...]
    seg = jnp.concatenate([seg, seg], 1)
    for r in range(rows):
        ids = jnp.broadcast_to(seg[r : r + 1], (SEG_ROWS, width))
        out_ref[r, tok:, :] = (ids == iota((SEG_ROWS, width), 0)).astype(f32).astype(bf16)
    for i, ref in enumerate(vecs):
        vec_ref[i : i + 1, : ref.shape[0]] = ref[...].astype(f32).reshape(1, -1)


def sum_kernel(tok, got_ref, sum_ref):
    total = got_ref[0, tok:, :].astype(f32)
    for j in range(1, got_ref.shape[0]):
        total = total + got_ref[j, tok:, :].astype(f32)
    sum_ref[...] = total.astype(bf16)


def rows_kernel(got_ref, out_ref, grad_ref):
    rows, tok, width = out_ref.shape
    out_ref[...] = got_ref[:rows, :tok, :width]
    grad_ref[...] = got_ref[:rows, :tok, width:].astype(f32)


def unpack_kernel(n_parts, *refs):
    parts, outs = refs[:n_parts], refs[n_parts:]
    parts = [p[...].astype(f32) for p in parts]
    halves = [sum(parts[core + 2 :: 2], parts[core]) for core in range(2)]
    norms = halves[0][NORM_ROW] + halves[1][NORM_ROW]
    first = lax.rem(lax.axis_index("rows"), 2) == 0
    a = jnp.where(first, halves[0], halves[1])
    b = jnp.where(first, halves[1], halves[0])
    whole = jnp.concatenate([a, b], 0)
    (gain1, bias1, wq, bq, wk, bk, wv, bv, wo, bo, gain2, bias2, wup, bup, wdown_t, bdown) = outs
    wup[...] = whole[0:64]
    wdown_t[...] = whole[64:128]
    bup[...] = whole[128]
    bdown[...] = whole[129, :64]
    bq[...] = whole[129, 64:]
    bk[...] = whole[130, :64]
    bv[...] = whole[130, 64:]
    wq[...] = whole[136:200, :64]
    wk[...] = whole[136:200, 64:]
    wv[...] = whole[200:264, :64]
    wo[...] = whole[200:264, 64:]
    bo[...] = whole[264, :64]
    gain2[...] = whole[264, 64:]
    bias2[...] = whole[265, :64]
    gain1[...] = norms[:64]
    bias1[...] = norms[64:]


def call(kernel, outs, *args, mib=12):
    vmem = pl.BlockSpec(memory_space=pltpu.VMEM)
    return pl.pallas_call(
        kernel,
        out_shape=outs,
        in_specs=[vmem] * len(args),
        out_specs=jax.tree.map(lambda _: vmem, outs),
        compiler_params=pltpu.CompilerParams(vmem_limit_bytes=mib * 1024 * 1024),
    )(*args)


def shards(tokens_in, segments, landmark_index, *rest):
    params, grad_out = rest[:14] + (rest[14].T, rest[15]), rest[16]
    rows, tok, width = tokens_in.shape
    n_tok = lax.axis_size("tok")
    n_rows = lax.axis_size("rows")
    sds = jax.ShapeDtypeStruct
    sent, vecs = call(
        pack_kernel,
        (sds((n_tok, tok + SEG_ROWS, 128), bf16), sds((16, 128), f32)),
        jnp.concatenate([tokens_in, grad_out], 2),
        segments,
        *[params[i] for i in VECTORS],
        mib=4,
    )
    got = lax.all_to_all(sent, "tok", 0, 0, tiled=True)
    h = GRAD_ROWS // 2
    tokens = n_tok * tok
    mib = 12 * max(1, tokens // 512)
    by_token = sds((width, tokens), f32)
    marks = landmark_index.shape[1] * landmark_index.shape[2]
    *later, keep, send = call(
        partial(main_kernel, tok),
        (sds((width, marks), bf16),)
        + (by_token,) * 3
        + (sds((1, tokens), f32), by_token)
        + (sds((h, 128), f32),) * 2,
        got,
        landmark_index,
        vecs,
        *[params[i] for i in MATRICES],
        mib=mib,
    )
    send = lax.ppermute(send, "rows", [(i, i ^ 1) for i in range(n_rows)])
    out, norms = call(
        end_kernel,
        (sds((n_tok, tok, 128), bf16), sds((h, 128), f32)),
        landmark_index,
        vecs,
        params[2],
        params[4],
        *later,
        mib=mib,
    )
    def from_xor(array, m):
        return lax.ppermute(array, "rows", [(i, i ^ m) for i in range(n_rows)])

    total = (keep + send + norms).astype(bf16)
    back = jnp.concatenate([out, jnp.broadcast_to(total, (n_tok, h, 128))], 1)
    got = lax.all_to_all(back, "tok", 0, 0, tiled=True)
    mine = call(partial(sum_kernel, tok), sds((h, 128), bf16), got)
    parts = [mine] + [from_xor(mine, m) for m in range(1, n_rows)]
    layer_out, grad_input = call(
        rows_kernel, (sds((rows, tok, width), bf16), sds((rows, tok, width), f32)), got
    )
    sums = call(
        partial(unpack_kernel, n_rows), tuple(sds(p.shape, f32) for p in params), *parts
    )
    sums = sums[:14] + (sums[14].T,) + sums[15:]
    return (layer_out, grad_input) + tuple(sums)


def solution(mesh):
    split3 = P("rows", "tok", None)
    return jax.shard_map(
        shards,
        mesh=mesh,
        in_specs=(split3, P("rows", "tok"), P("rows", None, None)) + (P(),) * 16 + (split3,),
        out_specs=(split3, split3) + (P(),) * 16,
        check_vma=False,
    )
```

```python
from functools import partial

import jax
import jax.numpy as jnp
from jax import lax
from jax.experimental import pallas as pl
from jax.experimental.pallas import tpu as pltpu
from jax.sharding import PartitionSpec as P


NS_STEPS = 6
EPS = 1e-05
RIDGE = 0.1
FAR = 640.0
SEG_ROWS = 8
FIRST = 1
GRAD_ROWS = 272
NORM_ROW = 131

LOG2_E = 1.4426950408889634

f32 = jnp.float32
bf16 = jnp.bfloat16


def mm(a, b):
    return lax.dot_general(a, b, (((1,), (0,)), ((), ())), preferred_element_type=f32)


def mm_nt(a, b):
    return lax.dot_general(a, b, (((1,), (1,)), ((), ())), preferred_element_type=f32)


def mm_tn(a, b):
    return lax.dot_general(a, b, (((0,), (0,)), ((), ())), preferred_element_type=f32)


def split(a):
    hi = a.astype(bf16)
    return hi, (a - hi.astype(f32)).astype(bf16)


def wide_right(b):
    hi, lo = split(b)
    return jnp.concatenate(
        [jnp.concatenate([hi, lo], 1), jnp.concatenate([hi, jnp.zeros_like(hi)], 1)], 0
    )


def mm_wide(a, wide):
    n = wide.shape[1] // 2
    both = mm(jnp.concatenate(split(a), 1), wide)
    return both[:, :n] + both[:, n:]


def row_sum(a):
    return jnp.sum(a, axis=1, keepdims=True)


def col_sum(a):
    return jnp.sum(a, axis=0, keepdims=True)


def total_of(a):
    return col_sum(row_sum(a))


def both_parts(product, a, b):
    n = b.shape[1]
    both = product(a, jnp.concatenate(split(b), 1))
    return both[:, :n] + both[:, n:]


def pair(a, b):
    return jnp.concatenate([a, b], 1)


def wide_mm(a_pair, wide):
    n = wide.shape[1] // 2
    both = mm(a_pair, wide)
    return both[:, :n] + both[:, n:]


def norm_stats(values):
    n = 1.0 / values.shape[0]
    centre = values - col_sum(values) * n
    scale = lax.rsqrt(col_sum(centre * centre) * n + EPS)
    return centre * scale, scale


def norm_back(d_norm, xhat, scale, gain):
    scaled = d_norm * gain
    n = 1.0 / scaled.shape[0]
    return scale * (scaled - col_sum(scaled) * n - xhat * (col_sum(scaled * xhat) * n))


def iota(shape, dim):
    return lax.broadcasted_iota(jnp.int32, shape, dim)


def row_work(xg, onehot_t, idx, par):
    (gain1, bias1, wq, bq, wk, bk, wv, bv, wo, bo, gain2, bias2, wup, bup, wdown_t, bdown) = par
    tokens = xg.shape[0]
    width = wq.shape[0]
    heads, marks = idx.shape
    size = width // heads
    sharp = size**-0.5
    sharp2 = sharp * LOG2_E
    out_scale = tokens**-0.5
    hm = heads * marks
    hs = range(heads)
    at = [slice(h * marks, (h + 1) * marks) for h in hs]
    rows_of = [slice(h * size, (h + 1) * size) for h in hs]
    chunk = tokens // 4
    chunks = [slice(lo, lo + chunk) for lo in range(0, tokens, chunk)]

    xg_t = xg.astype(f32).T
    x_t, g_t = xg_t[:width], xg_t[width:]
    g16_t = g_t.astype(bf16)
    wqkv = jnp.concatenate([wq, wk, wv], 1)
    wqkv_t = wqkv.astype(f32).T.astype(bf16)
    xhat1, scale1 = norm_stats(x_t)
    normed_t = (xhat1 * gain1 + bias1).astype(bf16)
    qkv_t = mm(wqkv_t, normed_t) + jnp.concatenate([bq, bk, bv], 0)
    qkv16_t = qkv_t.astype(bf16)
    q_t, k_t, v_t = (qkv16_t[i * width : (i + 1) * width] for i in range(3))
    seg_rows = jnp.where(
        (iota(onehot_t.shape, 0) >= 4) & (iota(onehot_t.shape, 0) < 8), 1.0, onehot_t.astype(f32)
    )
    seg_rows = jnp.concatenate(
        [seg_rows, jnp.zeros((width - SEG_ROWS, tokens), f32)], 0
    ).astype(bf16)

    def features(p_t):
        p = p_t.astype(f32)
        sq = p * p
        hi = sq.astype(bf16)
        return jnp.concatenate([p_t, seg_rows, hi, (sq - hi.astype(f32)).astype(bf16)], 0)

    feats_q, feats_k = features(q_t), features(k_t)

    idx_row = jnp.concatenate([idx[h : h + 1] for h in hs], 1)
    pick_t = (iota((2 * tokens, hm), 0) == idx_row).astype(f32).astype(bf16)
    qk_t = jnp.concatenate([q_t, k_t], 1)
    ones16 = jnp.ones((16, tokens), bf16)
    normed_ones = jnp.concatenate([normed_t, ones16], 0)
    seg2 = jnp.concatenate([onehot_t, onehot_t], 1)
    picked = mm(jnp.concatenate([qk_t, seg2], 0), pick_t)
    own = ((iota((width, hm), 0) // size) == (iota((width, hm), 1) // marks)).astype(f32)
    mark_t = picked[:width] * own
    mark_seg = picked[width : width + 8]
    sq = mark_t * mark_t
    half = -0.5 * col_sum(sq)
    half_hi = half.astype(bf16).astype(f32)
    half_mid = (half - half_hi).astype(bf16).astype(f32)
    half_lo = half - half_hi - half_mid
    row8 = iota((8, hm), 0)
    extra = jnp.where(row8 < 4, mark_seg * FAR, 0.0)
    extra = jnp.where(row8 == 4, half_hi, extra)
    extra = jnp.where(row8 == 5, half_mid, extra)
    extra = jnp.where(row8 == 6, half_lo, extra)
    extra = jnp.where(row8 == 7, -FAR, extra)
    pad = jnp.zeros((width - 8, hm), f32)
    squares = iota((hm, 2 * width), 1) % width // size == iota((hm, 2 * width), 0) // marks
    right_m = pair(
        jnp.concatenate([mark_t, extra, pad], 0).T.astype(bf16),
        jnp.where(squares, -0.5, 0.0).astype(bf16),
    )
    sq_hi = sq.astype(bf16).astype(f32)
    left = jnp.concatenate(
        [mark_t, jnp.where(row8 < 4, mark_seg, 1.0), pad, sq_hi, sq - sq_hi], 0
    ).astype(bf16)
    mark16 = mark_t.astype(bf16)

    def near_of(points):
        return jnp.exp2(sharp2 * mm(right_m, points)).astype(bf16)

    eye = (iota((marks, marks), 0) == iota((marks, marks), 1)).astype(f32)
    kernel = [jnp.exp2(sharp2 * mm(right_m[at[h]], left[:, at[h]])) for h in hs]
    gram = [kernel[h] + RIDGE * eye for h in hs]
    sums = [col_sum(gram[h]) for h in hs]
    widest = [jnp.max(sums[h], axis=1, keepdims=True) for h in hs]
    inv2 = [1.0 / (widest[h] * widest[h]) for h in hs]
    gram_wide = [wide_right(gram[h]) for h in hs]
    wo_of = [wo[rows_of[h]] for h in hs]
    rest = [eye - mm_wide(gram[h] * inv2[h], gram_wide[h]) for h in hs]
    v_tok = v_t.astype(f32).T.astype(bf16)
    rests, wides = [rest], []
    near_k, near_q, near_q_tok, summed_t, sent_t, grown = [], [], [], [], [], []

    def add_near_k(i):
        half = tokens // 2
        near_k.append(near_of(feats_k[:, i * half : (i + 1) * half]))

    def add_near_q(i):
        near_q.append(near_of(feats_q[:, chunks[i]]))
        near_q_tok.append(near_q[-1].T)

    def add_sums():
        near_k[:] = [jnp.concatenate(near_k, 1)]
        both = mm(near_k[0], v_tok).T
        summed_t.extend(both[rows_of[h], at[h]] for h in hs)

    def add_sent():
        sent_t.extend(both_parts(mm_tn, wo_of[h], summed_t[h]) for h in hs)
        grown.append([mm_wide(sent_t[h], gram_wide[h]) * inv2[h] for h in hs])

    def two_steps(step):
        nxt = rests[step + 1]
        return [rests[step][h] + nxt[h] + mm_wide(rests[step][h], wides[step + 1][h]) for h in hs]

    def grown_by(now, wide):
        return [now[h] + mm_wide(now[h], wide[h]) for h in hs]

    def widen(both):
        return [wide_right(both[h]) for h in hs]

    def next_rest():
        wides.append(widen(rests[-1]))
        if len(rests) < NS_STEPS:
            rests.append([mm_wide(rests[-1][h], wides[-1][h]) for h in hs])

    add_near_k(0)
    next_rest()
    add_near_k(1)
    next_rest()
    twice = [widen(two_steps(0))]
    add_sums()
    next_rest()
    add_near_q(0)
    add_sent()
    next_rest()
    twice.append(widen(two_steps(2)))
    add_near_q(1)
    grown.extend([None] * NS_STEPS)
    grown[2] = grown_by(grown[0], twice[0])
    next_rest()
    add_near_q(2)
    grown[4] = grown_by(grown[2], twice[1])
    next_rest()
    grown[5] = grown_by(grown[4], wides[4])
    add_near_q(3)
    grown[6] = grown_by(grown[5], wides[5])
    near_k, now = near_k[0], grown[-1]
    near_q = jnp.concatenate(near_q, 1)
    near_q_tok = jnp.concatenate(near_q_tok, 0)
    mixed_t = jnp.concatenate(now, 1).astype(bf16)
    hidden = x_t + (mm(mixed_t, near_q) * out_scale + bo)
    twice.append(widen(two_steps(4)))
    inverse = [gram[h] * inv2[h] for h in hs]
    for wide in twice:
        inverse = grown_by(inverse, wide)
    inverse_wide = widen(inverse)
    grown[1] = grown_by(grown[0], wides[0])
    grown[3] = grown_by(grown[2], wides[2])
    beside_rest = [
        [pair(rests[step][h], grown[step][h].T).astype(bf16) for h in hs]
        for step in range(NS_STEPS)
    ]
    normed_mark = pair(mm(normed_ones, pick_t[:tokens]), mm(normed_ones, pick_t[tokens:])).astype(bf16)
    wup_t = wup.astype(f32).T.astype(bf16)
    d_act = mm_tn(wdown_t, g16_t)
    xhat2, scale2 = norm_stats(hidden)
    normed2_t = (xhat2 * gain2 + bias2).astype(bf16)
    inner = mm(wup_t, normed2_t) + bup
    c = (2.0 / jnp.pi) ** 0.5
    inner2 = inner * inner
    th = jnp.tanh(c * inner * (1.0 + 0.044715 * inner2))
    act = (0.5 * inner * (1.0 + th)).astype(bf16)

    slope = 0.5 * (1.0 + th) + 0.5 * inner * (1.0 - th * th) * (
        c * (1.0 + (3.0 * 0.044715) * inner2)
    )
    d_inner = (d_act * slope).astype(bf16)
    d_norm2 = mm(wup, d_inner)
    layer_out = hidden + (mm(wdown_t, act) + bdown)
    d_hidden = g_t + norm_back(d_norm2, xhat2, scale2, gain2)
    d_branch = d_hidden.astype(bf16)
    d_sent_t = mm(d_branch, near_q_tok) * out_scale
    back = [d_sent_t[:, at[h]] for h in hs]

    beside_gram = [pair(sent_t[h].T, -gram[h]).astype(bf16) for h in hs]
    kernel_inv = [kernel[h] * inv2[h] for h in hs]
    widest_a = [(2.0 / widest[h]) * (eye - rests[0][h]) for h in hs]
    widest_b = [(2.0 / widest[h]) * grown[0][h] for h in hs]
    mark_both = jnp.concatenate([mark16, own.astype(bf16)], 0)
    mark_ones = [
        jnp.concatenate([mark16[:, at[h]], jnp.ones((16, marks), bf16)], 0) for h in hs
    ]
    top_part = []
    for h in hs:
        top = (sums[h] == widest[h]).astype(f32)
        top = top * (1.0 / row_sum(top))
        seen = kernel[h].astype(bf16)
        along = jnp.broadcast_to(top, (16, marks)).astype(bf16)
        top_part.append(
            top * mm(mark_ones[h], seen)
            + mm_nt(mark_ones[h], along)[:, :1] * mm(along, seen)[:1]
        )
    mixed_m = (jnp.concatenate(now, 1) * out_scale).T.astype(bf16)
    q_tok = q_t.astype(f32).T.astype(bf16)
    k_tok = k_t.astype(f32).T.astype(bf16)
    ones_tok = jnp.ones((tokens, width), bf16)
    d_start = [mm_wide(back[h], inverse_wide[h]) for h in hs]
    d_summed = [both_parts(mm, wo_of[h], d_start[h]) for h in hs]
    none = jnp.zeros((size, marks), f32)
    d_summed_t = jnp.concatenate(
        [jnp.concatenate([d_summed[h] if g == h else none for g in hs], 1) for h in hs], 0
    )
    d_summed_m = d_summed_t.T.astype(bf16)
    def stays(pull, p_t):
        both = mm(mark_both, pull)
        return sharp * (both[:width] - both[width:] * p_t.astype(f32))

    pulls_q, toks = [], []

    def pull_some(i):
        now_at = chunks[i]
        pulls_q.append(mm(mixed_m, d_branch[:, now_at]).astype(bf16) * near_q[:, now_at])

    def pull_rest():
        pulls_q.append(mm(d_summed_m, v_t).astype(bf16) * near_k)

    def add_tok(pull, tok):
        toks.append(mm(pull, pair(tok, ones_tok)))

    def add_tok_q():
        pulls_q[:4] = [jnp.concatenate(pulls_q[:4], 1)]
        add_tok(pulls_q[0], q_tok)

    def add_tok_k():
        add_tok(pulls_q[1], k_tok)

    early = {}

    def add_down():
        early["down"] = mm_nt(g16_t, act)

    def add_up():
        early["up"] = mm_nt(jnp.concatenate([normed2_t, ones16], 0), d_inner)

    def add_bias():
        early["bias"] = mm_nt(ones16, jnp.concatenate([g16_t, d_branch], 0))

    def add_wo():
        early["wo"] = jnp.concatenate(
            [mm_nt(summed_t[h].astype(bf16), d_start[h].astype(bf16)) for h in hs], 0
        )

    def add_stay():
        stay_q, stay_k = stays(pulls_q[0], q_t), stays(pulls_q[1], k_t)
        dv = mm(d_summed_t.astype(bf16), near_k)
        early["stay"] = jnp.concatenate([stay_q, stay_k, dv], 0).astype(bf16)

    def add_qkv():
        early["qkv"] = mm_nt(normed_ones, early["stay"])

    def add_normed():
        early["normed"] = mm(wqkv, early["stay"])

    beside = [
        [partial(pull_some, 0), partial(pull_some, 1), partial(pull_some, 2), partial(pull_some, 3)],
        [add_tok_q, pull_rest],
        [add_tok_k],
        [add_stay],
        [add_up, add_down],
        [add_qkv, add_normed, add_bias, add_wo],
    ]
    b16 = [back[h].astype(bf16) for h in hs]
    last = NS_STEPS - 1
    d_rest = [mm(beside_rest[last][h][:, marks:], b16[h]) for h in hs]
    back = [back[h] + wide_mm(b16[h], wides[last][h][:marks]) for h in hs]
    for step in reversed(range(NS_STEPS)):
        if step < last:
            both16 = [
                jnp.concatenate([d_rest[h].astype(bf16), back[h].astype(bf16)], 0) for h in hs
            ]
            turned = [wide_mm(both16[h], wides[step][h][:marks]) for h in hs]
            back = [back[h] + turned[h][marks:] for h in hs]
            d_rest = [turned[h][:marks] + mm(beside_rest[step][h], both16[h]) for h in hs]
        for work in beside[last - step]:
            work()
    d16 = [d_rest[h].astype(bf16) for h in hs]
    d_gram = [
        mm(beside_gram[h], jnp.concatenate([back[h].astype(bf16), d16[h]], 0))
        - wide_mm(d16[h], gram_wide[h][:marks])
        for h in hs
    ]
    tok_both = (toks[0] + toks[1]).T
    tok_t, tok_sum = tok_both[:width], tok_both[width : width + 1]
    stay, d_normed_tok = early["stay"], early["normed"]
    gram_part = []
    for h in hs:
        d_widest = total_of(d_rest[h] * widest_a[h]) - total_of(back[h] * widest_b[h])
        weighted = ((d_gram[h] + d_gram[h].T) * kernel_inv[h]).astype(bf16)
        gram_part.append(mm(mark_ones[h], weighted) + d_widest * top_part[h])
    gram_part = jnp.concatenate(gram_part, 1)
    d_mark_t = (
        (tok_t + gram_part[:width] - mark_t * (tok_sum + gram_part[width : width + 1])) * own
    ).astype(bf16)
    g_bias, g_wo = early["bias"], early["wo"]
    g_down, g_up = early["down"], early["up"]
    by_mark = sharp * pair(
        mm_nt(normed_mark[:, :hm], d_mark_t), mm_nt(normed_mark[:, hm:], d_mark_t)
    )
    g_qkv = early["qkv"] + pair(by_mark, jnp.zeros((width + 16, width), f32))
    columns = [
        row_sum(d_norm2 * xhat2),
        row_sum(d_norm2),
    ]
    lane = iota((width, 128), 1)
    norms = sum(jnp.where(lane == i, col, 0.0) for i, col in enumerate(columns)).T[:8]
    g_bqkv = g_qkv[width : width + 1]
    blank = jnp.zeros((1, 2 * width), f32)
    grads = jnp.concatenate(
        [
            g_up[:width],
            g_down[:width],
            g_up[width : width + 1],
            pair(g_bias[:1, :width], g_bqkv[:, :width]),
            g_bqkv[:, width:],
        ]
        + [blank] * 5
        + [
            g_qkv[:width, : 2 * width],
            pair(g_qkv[:width, 2 * width :], g_wo),
            pair(g_bias[:1, width:], norms[0:1]),
            pair(norms[1:2], blank[:, :width]),
        ]
        + [blank] * 6,
        0,
    )
    later = (d_mark_t, d_normed_tok, d_hidden, xhat1, scale1, layer_out)
    return later, grads


def row_end(later, idx, par):
    gain1, wq, wk = par
    d_mark_t, d_normed_tok, d_hidden, xhat1, scale1, layer_out = later
    width, tokens = xhat1.shape
    heads, marks = idx.shape
    hm = heads * marks
    idx_row = jnp.concatenate([idx[h : h + 1] for h in range(heads)], 1)
    idx_col = jnp.broadcast_to(idx_row.astype(f32), (8, hm)).T[:, :1].astype(jnp.int32)
    tok_lane = iota((hm, tokens), 1)
    pick_m = jnp.concatenate([tok_lane == idx_col, tok_lane + tokens == idx_col], 0)
    pick_m = pick_m.astype(f32).astype(bf16)
    onto = mm(jnp.concatenate([wq, wk], 0), d_mark_t).astype(bf16)
    moved = mm(pair(onto[:width], onto[width:]), pick_m)
    d_normed = d_normed_tok + (width // heads) ** -0.5 * moved
    grad_in = d_hidden + norm_back(d_normed, xhat1, scale1, gain1)
    lane = iota((width, 128), 1)
    sums = jnp.where(lane == 0, row_sum(d_normed * xhat1), 0.0) + jnp.where(
        lane == 1, row_sum(d_normed), 0.0
    )
    sums = sums.T
    return jnp.concatenate([layer_out, grad_in], 0).T.astype(bf16), pair(sums[:1], sums[1:2])


MATRICES = (2, 4, 6, 8, 12, 14)
VECTORS = (0, 1, 3, 5, 7, 9, 10, 11, 13, 15)


def read_params(mats, vec_cols):
    par = [None] * 16
    for i, ref in zip(MATRICES, mats):
        par[i] = ref[...]
    for row, i in enumerate(VECTORS):
        wide = par[12].shape[1] if i == 13 else par[2].shape[0]
        par[i] = vec_cols[:wide, row : row + 1]
    return tuple(par)


def own_row(idx_ref):
    return idx_ref[jnp.clip(lax.axis_index("tok") - FIRST, 0, idx_ref.shape[0] - 1)]


def for_owners(idx_ref, work, zeroed):
    row = lax.axis_index("tok") - FIRST
    has_row = (row >= 0) & (row < idx_ref.shape[0])
    pl.when(has_row)(work)

    @pl.when(jnp.logical_not(has_row))
    def _():
        for ref in zeroed:
            ref[...] = jnp.zeros(ref.shape, ref.dtype)


def main_kernel(tok_block, blk_ref, idx_ref, vec_ref, *refs):
    mats, later_refs, (keep_ref, send_ref) = refs[:6], refs[6:-2], refs[-2:]

    def work():
        blocks = blk_ref.shape[0]
        tokens = blocks * tok_block
        xg = blk_ref[:, :tok_block, :].reshape(tokens, 128)
        ids = blk_ref[:, tok_block:, :].astype(f32)
        half = iota((SEG_ROWS, 128), 1) < tok_block
        onehot_t = jnp.concatenate(
            [jnp.where(half, ids[2 * j], ids[2 * j + 1]) for j in range(blocks // 2)], 1
        ).astype(bf16)
        later, grads = row_work(xg, onehot_t, own_row(idx_ref), read_params(mats, vec_ref[...].T))
        for ref, value in zip(later_refs, later):
            ref[...] = value
        first = lax.rem(lax.axis_index("rows"), 2) == 0
        h = GRAD_ROWS // 2
        keep_ref[...] = jnp.where(first, grads[:h], grads[h:])
        send_ref[...] = jnp.where(first, grads[h:], grads[:h])

    for_owners(idx_ref, work, (keep_ref, send_ref))


def end_kernel(idx_ref, vec_ref, wq_ref, wk_ref, *refs):
    later_refs, out_ref, norm_ref = refs[:-2], refs[-2], refs[-1]

    def work():
        later = [ref[...] for ref in later_refs]
        gain1 = vec_ref[...].T[: wq_ref.shape[0], :1]
        out, sums = row_end(later, own_row(idx_ref), (gain1, wq_ref[...], wk_ref[...]))
        out_ref[...] = out.reshape(out_ref.shape)
        norm_ref[...] = jnp.where(iota(norm_ref.shape, 0) == NORM_ROW, sums, 0.0)

    for_owners(idx_ref, work, (out_ref, norm_ref))


def pack_kernel(xg_ref, s_ref, *refs):
    vecs, (out_ref, vec_ref) = refs[:-2], refs[-2:]
    rows, tok, width = xg_ref.shape
    out_ref[:FIRST] = jnp.zeros((FIRST,) + out_ref.shape[1:], bf16)
    out_ref[FIRST : rows + FIRST, :tok, :] = xg_ref[...]
    unused = out_ref.shape[0] - rows - FIRST
    if unused:
        out_ref[rows + FIRST :] = jnp.zeros((unused,) + out_ref.shape[1:], bf16)
    seg = s_ref[...]
    seg = jnp.concatenate([seg, seg], 1)
    for r in range(rows):
        ids = jnp.broadcast_to(seg[r : r + 1], (SEG_ROWS, width))
        out_ref[FIRST + r, tok:, :] = (ids == iota((SEG_ROWS, width), 0)).astype(f32).astype(bf16)
    for i, ref in enumerate(vecs):
        vec_ref[i : i + 1, : ref.shape[0]] = ref[...].astype(f32).reshape(1, -1)


def sum_kernel(tok, got_ref, sum_ref):
    total = got_ref[0, tok:, :].astype(f32)
    for j in range(1, got_ref.shape[0]):
        total = total + got_ref[j, tok:, :].astype(f32)
    sum_ref[...] = total.astype(bf16)


def rows_kernel(got_ref, out_ref, grad_ref):
    rows, tok, width = out_ref.shape
    out_ref[...] = got_ref[FIRST : rows + FIRST, :tok, :width]
    grad_ref[...] = got_ref[FIRST : rows + FIRST, :tok, width:].astype(f32)


def unpack_kernel(n_parts, *refs):
    parts, outs = refs[:n_parts], refs[n_parts:]
    parts = [p[...].astype(f32) for p in parts]
    halves = [sum(parts[core + 2 :: 2], parts[core]) for core in range(2)]
    norms = halves[0][NORM_ROW] + halves[1][NORM_ROW]
    first = lax.rem(lax.axis_index("rows"), 2) == 0
    a = jnp.where(first, halves[0], halves[1])
    b = jnp.where(first, halves[1], halves[0])
    whole = jnp.concatenate([a, b], 0)
    (gain1, bias1, wq, bq, wk, bk, wv, bv, wo, bo, gain2, bias2, wup, bup, wdown_t, bdown) = outs
    wup[...] = whole[0:64]
    wdown_t[...] = whole[64:128]
    bup[...] = whole[128]
    bdown[...] = whole[129, :64]
    bq[...] = whole[129, 64:]
    bk[...] = whole[130, :64]
    bv[...] = whole[130, 64:]
    wq[...] = whole[136:200, :64]
    wk[...] = whole[136:200, 64:]
    wv[...] = whole[200:264, :64]
    wo[...] = whole[200:264, 64:]
    bo[...] = whole[264, :64]
    gain2[...] = whole[264, 64:]
    bias2[...] = whole[265, :64]
    gain1[...] = norms[:64]
    bias1[...] = norms[64:]


def call(kernel, outs, *args, mib=12):
    vmem = pl.BlockSpec(memory_space=pltpu.VMEM)
    return pl.pallas_call(
        kernel,
        out_shape=outs,
        in_specs=[vmem] * len(args),
        out_specs=jax.tree.map(lambda _: vmem, outs),
        compiler_params=pltpu.CompilerParams(vmem_limit_bytes=mib * 1024 * 1024),
    )(*args)


def shards(tokens_in, segments, landmark_index, *rest):
    params, grad_out = rest[:14] + (rest[14].T, rest[15]), rest[16]
    rows, tok, width = tokens_in.shape
    n_tok = lax.axis_size("tok")
    n_rows = lax.axis_size("rows")
    sds = jax.ShapeDtypeStruct
    sent, vecs = call(
        pack_kernel,
        (sds((n_tok, tok + SEG_ROWS, 128), bf16), sds((16, 128), f32)),
        jnp.concatenate([tokens_in, grad_out], 2),
        segments,
        *[params[i] for i in VECTORS],
        mib=4,
    )
    got = lax.all_to_all(sent, "tok", 0, 0, tiled=True)
    h = GRAD_ROWS // 2
    tokens = n_tok * tok
    mib = 12 * max(1, tokens // 512)
    by_token = sds((width, tokens), f32)
    marks = landmark_index.shape[1] * landmark_index.shape[2]
    *later, keep, send = call(
        partial(main_kernel, tok),
        (sds((width, marks), bf16),)
        + (by_token,) * 3
        + (sds((1, tokens), f32), by_token)
        + (sds((h, 128), f32),) * 2,
        got,
        landmark_index,
        vecs,
        *[params[i] for i in MATRICES],
        mib=mib,
    )
    send = lax.ppermute(send, "rows", [(i, i ^ 1) for i in range(n_rows)])
    out, norms = call(
        end_kernel,
        (sds((n_tok, tok, 128), bf16), sds((h, 128), f32)),
        landmark_index,
        vecs,
        params[2],
        params[4],
        *later,
        mib=mib,
    )
    def from_xor(array, m):
        return lax.ppermute(array, "rows", [(i, i ^ m) for i in range(n_rows)])

    total = (keep + send + norms).astype(bf16)
    back = jnp.concatenate([out, jnp.broadcast_to(total, (n_tok, h, 128))], 1)
    got = lax.all_to_all(back, "tok", 0, 0, tiled=True)
    mine = call(partial(sum_kernel, tok), sds((h, 128), bf16), got)
    parts = [mine] + [from_xor(mine, m) for m in range(1, n_rows)]
    layer_out, grad_input = call(
        rows_kernel, (sds((rows, tok, width), bf16), sds((rows, tok, width), f32)), got
    )
    sums = call(
        partial(unpack_kernel, n_rows), tuple(sds(p.shape, f32) for p in params), *parts
    )
    sums = sums[:14] + (sums[14].T,) + sums[15:]
    return (layer_out, grad_input) + tuple(sums)


def solution(mesh):
    split3 = P("rows", "tok", None)
    return jax.shard_map(
        shards,
        mesh=mesh,
        in_specs=(split3, P("rows", "tok"), P("rows", None, None)) + (P(),) * 16 + (split3,),
        out_specs=(split3, split3) + (P(),) * 16,
        check_vma=False,
    )
```

```python
from functools import partial

import jax
import jax.numpy as jnp
from jax import lax
from jax.experimental import pallas as pl
from jax.experimental.pallas import tpu as pltpu
from jax.sharding import PartitionSpec as P


NS_STEPS = 6
EPS = 1e-05
RIDGE = 0.1
FAR = 640.0
SEG_ROWS = 8
FIRST = 1
GRAD_ROWS = 272
NORM_ROW = 131

LOG2_E = 1.4426950408889634

f32 = jnp.float32
bf16 = jnp.bfloat16


def mm(a, b):
    return lax.dot_general(a, b, (((1,), (0,)), ((), ())), preferred_element_type=f32)


def mm_nt(a, b):
    return lax.dot_general(a, b, (((1,), (1,)), ((), ())), preferred_element_type=f32)


def mm_tn(a, b):
    return lax.dot_general(a, b, (((0,), (0,)), ((), ())), preferred_element_type=f32)


def split(a):
    hi = a.astype(bf16)
    return hi, (a - hi.astype(f32)).astype(bf16)


def wide_right(b):
    hi, lo = split(b)
    return jnp.concatenate(
        [jnp.concatenate([hi, lo], 1), jnp.concatenate([hi, jnp.zeros_like(hi)], 1)], 0
    )


def mm_wide(a, wide):
    n = wide.shape[1] // 2
    both = mm(jnp.concatenate(split(a), 1), wide)
    return both[:, :n] + both[:, n:]


def row_sum(a):
    return jnp.sum(a, axis=1, keepdims=True)


def col_sum(a):
    return jnp.sum(a, axis=0, keepdims=True)


def total_of(a):
    return col_sum(row_sum(a))


def both_parts(product, a, b):
    n = b.shape[1]
    both = product(a, jnp.concatenate(split(b), 1))
    return both[:, :n] + both[:, n:]


def pair(a, b):
    return jnp.concatenate([a, b], 1)


def wide_mm(a_pair, wide):
    n = wide.shape[1] // 2
    both = mm(a_pair, wide)
    return both[:, :n] + both[:, n:]


def both_parts_left(a, wide):
    n = wide.shape[1] // 2
    return wide_mm(a, wide[:n])


def norm_stats(values):
    n = 1.0 / values.shape[0]
    centre = values - col_sum(values) * n
    scale = lax.rsqrt(col_sum(centre * centre) * n + EPS)
    return centre * scale, scale


def norm_back(d_norm, xhat, scale, gain):
    scaled = d_norm * gain
    n = 1.0 / scaled.shape[0]
    return scale * (scaled - col_sum(scaled) * n - xhat * (col_sum(scaled * xhat) * n))


def iota(shape, dim):
    return lax.broadcasted_iota(jnp.int32, shape, dim)


def row_work(xg, onehot_t, idx, par):
    (gain1, bias1, wq, bq, wk, bk, wv, bv, wo, bo, gain2, bias2, wup, bup, wdown_t, bdown) = par
    tokens = xg.shape[0]
    width = wq.shape[0]
    heads, marks = idx.shape
    size = width // heads
    sharp = size**-0.5
    sharp2 = sharp * LOG2_E
    out_scale = tokens**-0.5
    hm = heads * marks
    hs = range(heads)
    at = [slice(h * marks, (h + 1) * marks) for h in hs]
    rows_of = [slice(h * size, (h + 1) * size) for h in hs]
    chunk = tokens // 4
    chunks = [slice(lo, lo + chunk) for lo in range(0, tokens, chunk)]

    xg_t = xg.astype(f32).T
    x_t, g_t = xg_t[:width], xg_t[width:]
    g16_t = g_t.astype(bf16)
    wqkv = jnp.concatenate([wq, wk, wv], 1)
    wqkv_t = wqkv.astype(f32).T.astype(bf16)
    xhat1, scale1 = norm_stats(x_t)
    normed_t = (xhat1 * gain1 + bias1).astype(bf16)
    qkv_t = mm(wqkv_t, normed_t) + jnp.concatenate([bq, bk, bv], 0)
    qkv16_t = qkv_t.astype(bf16)
    q_t, k_t, v_t = (qkv16_t[i * width : (i + 1) * width] for i in range(3))
    seg_rows = jnp.where(
        (iota(onehot_t.shape, 0) >= 4) & (iota(onehot_t.shape, 0) < 8), 1.0, onehot_t.astype(f32)
    )
    seg_rows = jnp.concatenate(
        [seg_rows, jnp.zeros((width - SEG_ROWS, tokens), f32)], 0
    ).astype(bf16)

    def features(p_t):
        p = p_t.astype(f32)
        sq = p * p
        hi = sq.astype(bf16)
        return jnp.concatenate([p_t, seg_rows, hi, (sq - hi.astype(f32)).astype(bf16)], 0)

    feats_q, feats_k = features(q_t), features(k_t)

    idx_row = jnp.concatenate([idx[h : h + 1] for h in hs], 1)
    pick_t = (iota((2 * tokens, hm), 0) == idx_row).astype(f32).astype(bf16)
    qk_t = jnp.concatenate([q_t, k_t], 1)
    ones16 = jnp.ones((16, tokens), bf16)
    normed_ones = jnp.concatenate([normed_t, ones16], 0)
    seg2 = jnp.concatenate([onehot_t, onehot_t], 1)
    picked = mm(jnp.concatenate([qk_t, seg2], 0), pick_t)
    own = ((iota((width, hm), 0) // size) == (iota((width, hm), 1) // marks)).astype(f32)
    mark_t = picked[:width] * own
    mark_seg = picked[width : width + 8]
    sq = mark_t * mark_t
    half = -0.5 * col_sum(sq)
    half_hi = half.astype(bf16).astype(f32)
    half_mid = (half - half_hi).astype(bf16).astype(f32)
    half_lo = half - half_hi - half_mid
    row8 = iota((8, hm), 0)
    extra = jnp.where(row8 < 4, mark_seg * FAR, 0.0)
    extra = jnp.where(row8 == 4, half_hi, extra)
    extra = jnp.where(row8 == 5, half_mid, extra)
    extra = jnp.where(row8 == 6, half_lo, extra)
    extra = jnp.where(row8 == 7, -FAR, extra)
    pad = jnp.zeros((width - 8, hm), f32)
    squares = iota((hm, 2 * width), 1) % width // size == iota((hm, 2 * width), 0) // marks
    right_m = pair(
        jnp.concatenate([mark_t, extra, pad], 0).T.astype(bf16),
        jnp.where(squares, -0.5, 0.0).astype(bf16),
    )
    sq_hi = sq.astype(bf16).astype(f32)
    left = jnp.concatenate(
        [mark_t, jnp.where(row8 < 4, mark_seg, 1.0), pad, sq_hi, sq - sq_hi], 0
    ).astype(bf16)
    mark16 = mark_t.astype(bf16)

    def near_of(points):
        return jnp.exp2(sharp2 * mm(right_m, points)).astype(bf16)

    eye = (iota((marks, marks), 0) == iota((marks, marks), 1)).astype(f32)
    kernel = [jnp.exp2(sharp2 * mm(right_m[at[h]], left[:, at[h]])) for h in hs]
    gram = [kernel[h] + RIDGE * eye for h in hs]
    sums = [col_sum(gram[h]) for h in hs]
    widest = [jnp.max(sums[h], axis=1, keepdims=True) for h in hs]
    inv2 = [1.0 / (widest[h] * widest[h]) for h in hs]
    gram_wide = [wide_right(gram[h]) for h in hs]
    wo_of = [wo[rows_of[h]] for h in hs]
    rest = [eye - mm_wide(gram[h] * inv2[h], gram_wide[h]) for h in hs]
    v_tok = v_t.astype(f32).T.astype(bf16)
    rests, wides = [rest], []
    near_k, near_q, near_q_tok, summed_t, sent_t, grown = [], [], [], [], [], []

    def add_near_k(i):
        half = tokens // 2
        near_k.append(near_of(feats_k[:, i * half : (i + 1) * half]))

    def add_near_q(i):
        near_q.append(near_of(feats_q[:, chunks[i]]))
        near_q_tok.append(near_q[-1].T)

    def add_sums():
        near_k[:] = [jnp.concatenate(near_k, 1)]
        both = mm(near_k[0], v_tok).T
        summed_t.extend(both[rows_of[h], at[h]] for h in hs)

    def add_sent():
        sent_t.extend(both_parts(mm_tn, wo_of[h], summed_t[h]) for h in hs)
        grown.append([mm_wide(sent_t[h], gram_wide[h]) * inv2[h] for h in hs])

    def two_steps(step):
        nxt = rests[step + 1]
        return [rests[step][h] + nxt[h] + mm_wide(rests[step][h], wides[step + 1][h]) for h in hs]

    def grown_by(now, wide):
        return [now[h] + mm_wide(now[h], wide[h]) for h in hs]

    def widen(both):
        return [wide_right(both[h]) for h in hs]

    def next_rest():
        wides.append(widen(rests[-1]))
        if len(rests) < NS_STEPS:
            rests.append([mm_wide(rests[-1][h], wides[-1][h]) for h in hs])

    add_near_k(0)
    next_rest()
    add_near_k(1)
    next_rest()
    twice = [widen(two_steps(0))]
    add_sums()
    next_rest()
    add_near_q(0)
    add_sent()
    next_rest()
    twice.append(widen(two_steps(2)))
    add_near_q(1)
    grown.extend([None] * NS_STEPS)
    grown[2] = grown_by(grown[0], twice[0])
    next_rest()
    add_near_q(2)
    grown[4] = grown_by(grown[2], twice[1])
    next_rest()
    grown[5] = grown_by(grown[4], wides[4])
    add_near_q(3)
    grown[6] = grown_by(grown[5], wides[5])
    near_k, now = near_k[0], grown[-1]
    near_q = jnp.concatenate(near_q, 1)
    near_q_tok = jnp.concatenate(near_q_tok, 0)
    mixed_t = jnp.concatenate(now, 1).astype(bf16)
    hidden = x_t + (mm(mixed_t, near_q) * out_scale + bo)
    twice.append(widen(two_steps(4)))
    inverse = [gram[h] * inv2[h] for h in hs]
    for wide in twice:
        inverse = grown_by(inverse, wide)
    inverse_wide = widen(inverse)
    grown[1] = grown_by(grown[0], wides[0])
    grown[3] = grown_by(grown[2], wides[2])
    beside_rest = [
        [pair(rests[step][h], grown[step][h].T).astype(bf16) for h in hs]
        for step in range(NS_STEPS)
    ]
    normed_mark = pair(mm(normed_ones, pick_t[:tokens]), mm(normed_ones, pick_t[tokens:])).astype(bf16)
    wup_t = wup.astype(f32).T.astype(bf16)
    d_act = mm_tn(wdown_t, g16_t)
    xhat2, scale2 = norm_stats(hidden)
    normed2_t = (xhat2 * gain2 + bias2).astype(bf16)
    inner = mm(wup_t, normed2_t) + bup
    c = (2.0 / jnp.pi) ** 0.5
    inner2 = inner * inner
    th = jnp.tanh(c * inner * (1.0 + 0.044715 * inner2))
    act = (0.5 * inner * (1.0 + th)).astype(bf16)

    slope = 0.5 * (1.0 + th) + 0.5 * inner * (1.0 - th * th) * (
        c * (1.0 + (3.0 * 0.044715) * inner2)
    )
    d_inner = (d_act * slope).astype(bf16)
    d_norm2 = mm(wup, d_inner)
    layer_out = hidden + (mm(wdown_t, act) + bdown)
    d_hidden = g_t + norm_back(d_norm2, xhat2, scale2, gain2)
    d_branch = d_hidden.astype(bf16)
    d_sent_t = mm(d_branch, near_q_tok) * out_scale
    back = [d_sent_t[:, at[h]] for h in hs]

    beside_gram = [pair(sent_t[h].T, -gram[h]).astype(bf16) for h in hs]
    kernel_inv = [kernel[h] * inv2[h] for h in hs]
    widest_a = [(2.0 / widest[h]) * (eye - rests[0][h]) for h in hs]
    widest_b = [(2.0 / widest[h]) * grown[0][h] for h in hs]
    mark_both = jnp.concatenate([mark16, own.astype(bf16)], 0)
    mark_ones = [
        jnp.concatenate([mark16[:, at[h]], jnp.ones((16, marks), bf16)], 0) for h in hs
    ]
    top_part = []
    for h in hs:
        top = (sums[h] == widest[h]).astype(f32)
        top = top * (1.0 / row_sum(top))
        seen = kernel[h].astype(bf16)
        along = jnp.broadcast_to(top, (16, marks)).astype(bf16)
        top_part.append(
            top * mm(mark_ones[h], seen)
            + mm_nt(mark_ones[h], along)[:, :1] * mm(along, seen)[:1]
        )
    mixed = [mm_wide(summed_t[h], inverse_wide[h]) for h in hs]
    blank_h = jnp.zeros((size, marks), f32)
    mixed_m = jnp.concatenate(
        [jnp.concatenate([mixed[h] if g == h else blank_h for g in hs], 1) for h in hs], 0
    ).T.astype(bf16)
    d_att = mm(wo, d_branch).astype(bf16)
    q_tok = q_t.astype(f32).T.astype(bf16)
    k_tok = k_t.astype(f32).T.astype(bf16)
    ones_tok = jnp.ones((tokens, width), bf16)
    d_start = [mm_wide(back[h], inverse_wide[h]) for h in hs]
    d_att_early = mm(wo, d_branch).astype(bf16)
    d_mixed = mm(d_att_early, near_q_tok) * out_scale
    d_mixed = [d_mixed[rows_of[h], at[h]].astype(bf16) for h in hs]
    d_summed = [both_parts_left(d_mixed[h], inverse_wide[h]) for h in hs]
    none = jnp.zeros((size, marks), f32)
    d_summed_t = jnp.concatenate(
        [jnp.concatenate([d_summed[h] if g == h else none for g in hs], 1) for h in hs], 0
    )
    d_summed_m = d_summed_t.T.astype(bf16)
    def stays(pull, p_t):
        both = mm(mark_both, pull)
        return sharp * (both[:width] - both[width:] * p_t.astype(f32))

    pulls_q, toks = [], []

    def pull_some(i):
        now_at = chunks[i]
        pull = (mm(mixed_m, d_att[:, now_at]) * out_scale).astype(bf16)
        pulls_q.append((pull.astype(f32) * near_q[:, now_at].astype(f32)).astype(bf16))

    def pull_rest():
        pull = mm(d_summed_m, v_t).astype(bf16)
        pulls_q.append((pull.astype(f32) * near_k.astype(f32)).astype(bf16))

    def add_tok(pull, tok):
        toks.append(mm(pull, pair(tok, ones_tok)))

    def add_tok_q():
        pulls_q[:4] = [jnp.concatenate(pulls_q[:4], 1)]
        add_tok(pulls_q[0], q_tok)

    def add_tok_k():
        add_tok(pulls_q[1], k_tok)

    early = {}

    def add_down():
        early["down"] = mm_nt(g16_t, act)

    def add_up():
        early["up"] = mm_nt(jnp.concatenate([normed2_t, ones16], 0), d_inner)

    def add_bias():
        early["bias"] = mm_nt(ones16, jnp.concatenate([g16_t, d_branch], 0))

    def add_wo():
        early["wo"] = jnp.concatenate(
            [mm_nt(summed_t[h].astype(bf16), d_start[h].astype(bf16)) for h in hs], 0
        )

    def add_stay():
        stay_q, stay_k = stays(pulls_q[0], q_t), stays(pulls_q[1], k_t)
        dv = mm(d_summed_t.astype(bf16), near_k)
        early["stay"] = jnp.concatenate([stay_q, stay_k, dv], 0).astype(bf16)

    def add_qkv():
        early["qkv"] = mm_nt(normed_ones, early["stay"])

    def add_normed():
        early["normed"] = mm(wqkv, early["stay"])

    beside = [
        [partial(pull_some, 0), partial(pull_some, 1), partial(pull_some, 2), partial(pull_some, 3)],
        [add_tok_q, pull_rest],
        [add_tok_k],
        [add_stay],
        [add_up, add_down],
        [add_qkv, add_normed, add_bias, add_wo],
    ]
    b16 = [back[h].astype(bf16) for h in hs]
    last = NS_STEPS - 1
    d_rest = [mm(beside_rest[last][h][:, marks:], b16[h]) for h in hs]
    back = [back[h] + wide_mm(b16[h], wides[last][h][:marks]) for h in hs]
    for step in reversed(range(NS_STEPS)):
        if step < last:
            both16 = [
                jnp.concatenate([d_rest[h].astype(bf16), back[h].astype(bf16)], 0) for h in hs
            ]
            turned = [
                mm_wide(jnp.concatenate([d_rest[h], back[h]], 0), wides[step][h]) for h in hs
            ]
            back = [back[h] + turned[h][marks:] for h in hs]
            d_rest = [turned[h][:marks] + mm(beside_rest[step][h], both16[h]) for h in hs]
        for work in beside[last - step]:
            work()
    d16 = [d_rest[h].astype(bf16) for h in hs]
    d_gram = [
        mm(beside_gram[h], jnp.concatenate([back[h].astype(bf16), d16[h]], 0))
        - wide_mm(d16[h], gram_wide[h][:marks])
        for h in hs
    ]
    tok_both = (toks[0] + toks[1]).T
    tok_t, tok_sum = tok_both[:width], tok_both[width : width + 1]
    stay, d_normed_tok = early["stay"], early["normed"]
    gram_part = []
    for h in hs:
        d_widest = total_of(d_rest[h] * widest_a[h]) - total_of(back[h] * widest_b[h])
        weighted = ((d_gram[h] + d_gram[h].T) * kernel_inv[h]).astype(bf16)
        gram_part.append(mm(mark_ones[h], weighted) + d_widest * top_part[h])
    gram_part = jnp.concatenate(gram_part, 1)
    d_mark_t = (
        (tok_t + gram_part[:width] - mark_t * (tok_sum + gram_part[width : width + 1])) * own
    ).astype(bf16)
    g_bias, g_wo = early["bias"], early["wo"]
    g_down, g_up = early["down"], early["up"]
    by_mark = sharp * pair(
        mm_nt(normed_mark[:, :hm], d_mark_t), mm_nt(normed_mark[:, hm:], d_mark_t)
    )
    g_qkv = early["qkv"] + pair(by_mark, jnp.zeros((width + 16, width), f32))
    columns = [
        row_sum(d_norm2 * xhat2),
        row_sum(d_norm2),
    ]
    lane = iota((width, 128), 1)
    norms = sum(jnp.where(lane == i, col, 0.0) for i, col in enumerate(columns)).T[:8]
    g_bqkv = g_qkv[width : width + 1]
    blank = jnp.zeros((1, 2 * width), f32)
    grads = jnp.concatenate(
        [
            g_up[:width],
            g_down[:width],
            g_up[width : width + 1],
            pair(g_bias[:1, :width], g_bqkv[:, :width]),
            g_bqkv[:, width:],
        ]
        + [blank] * 5
        + [
            g_qkv[:width, : 2 * width],
            pair(g_qkv[:width, 2 * width :], g_wo),
            pair(g_bias[:1, width:], norms[0:1]),
            pair(norms[1:2], blank[:, :width]),
        ]
        + [blank] * 6,
        0,
    )
    later = (d_mark_t, d_normed_tok, d_hidden, xhat1, scale1, layer_out)
    return later, grads


def row_end(later, idx, par):
    gain1, wq, wk = par
    d_mark_t, d_normed_tok, d_hidden, xhat1, scale1, layer_out = later
    width, tokens = xhat1.shape
    heads, marks = idx.shape
    hm = heads * marks
    idx_row = jnp.concatenate([idx[h : h + 1] for h in range(heads)], 1)
    idx_col = jnp.broadcast_to(idx_row.astype(f32), (8, hm)).T[:, :1].astype(jnp.int32)
    tok_lane = iota((hm, tokens), 1)
    pick_m = jnp.concatenate([tok_lane == idx_col, tok_lane + tokens == idx_col], 0)
    pick_m = pick_m.astype(f32).astype(bf16)
    onto = mm(jnp.concatenate([wq, wk], 0), d_mark_t).astype(bf16)
    moved = mm(pair(onto[:width], onto[width:]), pick_m)
    d_normed = d_normed_tok + (width // heads) ** -0.5 * moved
    grad_in = d_hidden + norm_back(d_normed, xhat1, scale1, gain1)
    lane = iota((width, 128), 1)
    sums = jnp.where(lane == 0, row_sum(d_normed * xhat1), 0.0) + jnp.where(
        lane == 1, row_sum(d_normed), 0.0
    )
    sums = sums.T
    return jnp.concatenate([layer_out, grad_in], 0).T.astype(bf16), pair(sums[:1], sums[1:2])


MATRICES = (2, 4, 6, 8, 12, 14)
VECTORS = (0, 1, 3, 5, 7, 9, 10, 11, 13, 15)


def read_params(mats, vec_cols):
    par = [None] * 16
    for i, ref in zip(MATRICES, mats):
        par[i] = ref[...]
    for row, i in enumerate(VECTORS):
        wide = par[12].shape[1] if i == 13 else par[2].shape[0]
        par[i] = vec_cols[:wide, row : row + 1]
    return tuple(par)


def own_row(idx_ref):
    return idx_ref[jnp.clip(lax.axis_index("tok") - FIRST, 0, idx_ref.shape[0] - 1)]


def for_owners(idx_ref, work, zeroed):
    row = lax.axis_index("tok") - FIRST
    has_row = (row >= 0) & (row < idx_ref.shape[0])
    pl.when(has_row)(work)

    @pl.when(jnp.logical_not(has_row))
    def _():
        for ref in zeroed:
            ref[...] = jnp.zeros(ref.shape, ref.dtype)


def main_kernel(tok_block, blk_ref, idx_ref, vec_ref, *refs):
    mats, later_refs, (keep_ref, send_ref) = refs[:6], refs[6:-2], refs[-2:]

    def work():
        blocks = blk_ref.shape[0]
        tokens = blocks * tok_block
        xg = blk_ref[:, :tok_block, :].reshape(tokens, 128)
        ids = blk_ref[:, tok_block:, :].astype(f32)
        half = iota((SEG_ROWS, 128), 1) < tok_block
        onehot_t = jnp.concatenate(
            [jnp.where(half, ids[2 * j], ids[2 * j + 1]) for j in range(blocks // 2)], 1
        ).astype(bf16)
        later, grads = row_work(xg, onehot_t, own_row(idx_ref), read_params(mats, vec_ref[...].T))
        for ref, value in zip(later_refs, later):
            ref[...] = value
        first = lax.rem(lax.axis_index("rows"), 2) == 0
        h = GRAD_ROWS // 2
        keep_ref[...] = jnp.where(first, grads[:h], grads[h:])
        send_ref[...] = jnp.where(first, grads[h:], grads[:h])

    for_owners(idx_ref, work, (keep_ref, send_ref))


def end_kernel(idx_ref, vec_ref, wq_ref, wk_ref, *refs):
    later_refs, out_ref, norm_ref = refs[:-2], refs[-2], refs[-1]

    def work():
        later = [ref[...] for ref in later_refs]
        gain1 = vec_ref[...].T[: wq_ref.shape[0], :1]
        out, sums = row_end(later, own_row(idx_ref), (gain1, wq_ref[...], wk_ref[...]))
        out_ref[...] = out.reshape(out_ref.shape)
        norm_ref[...] = jnp.where(iota(norm_ref.shape, 0) == NORM_ROW, sums, 0.0)

    for_owners(idx_ref, work, (out_ref, norm_ref))


def pack_kernel(xg_ref, s_ref, *refs):
    vecs, (out_ref, vec_ref) = refs[:-2], refs[-2:]
    rows, tok, width = xg_ref.shape
    out_ref[:FIRST] = jnp.zeros((FIRST,) + out_ref.shape[1:], bf16)
    out_ref[FIRST : rows + FIRST, :tok, :] = xg_ref[...]
    unused = out_ref.shape[0] - rows - FIRST
    if unused:
        out_ref[rows + FIRST :] = jnp.zeros((unused,) + out_ref.shape[1:], bf16)
    seg = s_ref[...]
    seg = jnp.concatenate([seg, seg], 1)
    for r in range(rows):
        ids = jnp.broadcast_to(seg[r : r + 1], (SEG_ROWS, width))
        out_ref[FIRST + r, tok:, :] = (ids == iota((SEG_ROWS, width), 0)).astype(f32).astype(bf16)
    for i, ref in enumerate(vecs):
        vec_ref[i : i + 1, : ref.shape[0]] = ref[...].astype(f32).reshape(1, -1)


def sum_kernel(tok, got_ref, sum_ref):
    total = got_ref[0, tok:, :].astype(f32)
    for j in range(1, got_ref.shape[0]):
        total = total + got_ref[j, tok:, :].astype(f32)
    sum_ref[...] = total.astype(bf16)


def rows_kernel(got_ref, out_ref, grad_ref):
    rows, tok, width = out_ref.shape
    out_ref[...] = got_ref[FIRST : rows + FIRST, :tok, :width]
    grad_ref[...] = got_ref[FIRST : rows + FIRST, :tok, width:].astype(f32)


def unpack_kernel(n_parts, *refs):
    parts, outs = refs[:n_parts], refs[n_parts:]
    parts = [p[...].astype(f32) for p in parts]
    halves = [sum(parts[core + 2 :: 2], parts[core]) for core in range(2)]
    norms = halves[0][NORM_ROW] + halves[1][NORM_ROW]
    first = lax.rem(lax.axis_index("rows"), 2) == 0
    a = jnp.where(first, halves[0], halves[1])
    b = jnp.where(first, halves[1], halves[0])
    whole = jnp.concatenate([a, b], 0)
    (gain1, bias1, wq, bq, wk, bk, wv, bv, wo, bo, gain2, bias2, wup, bup, wdown_t, bdown) = outs
    wup[...] = whole[0:64]
    wdown_t[...] = whole[64:128]
    bup[...] = whole[128]
    bdown[...] = whole[129, :64]
    bq[...] = whole[129, 64:]
    bk[...] = whole[130, :64]
    bv[...] = whole[130, 64:]
    wq[...] = whole[136:200, :64]
    wk[...] = whole[136:200, 64:]
    wv[...] = whole[200:264, :64]
    wo[...] = whole[200:264, 64:]
    bo[...] = whole[264, :64]
    gain2[...] = whole[264, 64:]
    bias2[...] = whole[265, :64]
    gain1[...] = norms[:64]
    bias1[...] = norms[64:]


def call(kernel, outs, *args, mib=12):
    vmem = pl.BlockSpec(memory_space=pltpu.VMEM)
    return pl.pallas_call(
        kernel,
        out_shape=outs,
        in_specs=[vmem] * len(args),
        out_specs=jax.tree.map(lambda _: vmem, outs),
        compiler_params=pltpu.CompilerParams(vmem_limit_bytes=mib * 1024 * 1024),
    )(*args)


def shards(tokens_in, segments, landmark_index, *rest):
    params, grad_out = rest[:14] + (rest[14].T, rest[15]), rest[16]
    rows, tok, width = tokens_in.shape
    n_tok = lax.axis_size("tok")
    n_rows = lax.axis_size("rows")
    sds = jax.ShapeDtypeStruct
    sent, vecs = call(
        pack_kernel,
        (sds((n_tok, tok + SEG_ROWS, 128), bf16), sds((16, 128), f32)),
        jnp.concatenate([tokens_in, grad_out], 2),
        segments,
        *[params[i] for i in VECTORS],
        mib=4,
    )
    got = lax.all_to_all(sent, "tok", 0, 0, tiled=True)
    h = GRAD_ROWS // 2
    tokens = n_tok * tok
    mib = 12 * max(1, tokens // 512)
    by_token = sds((width, tokens), f32)
    marks = landmark_index.shape[1] * landmark_index.shape[2]
    *later, keep, send = call(
        partial(main_kernel, tok),
        (sds((width, marks), bf16),)
        + (by_token,) * 3
        + (sds((1, tokens), f32), by_token)
        + (sds((h, 128), f32),) * 2,
        got,
        landmark_index,
        vecs,
        *[params[i] for i in MATRICES],
        mib=mib,
    )
    send = lax.ppermute(send, "rows", [(i, i ^ 1) for i in range(n_rows)])
    out, norms = call(
        end_kernel,
        (sds((n_tok, tok, 128), bf16), sds((h, 128), f32)),
        landmark_index,
        vecs,
        params[2],
        params[4],
        *later,
        mib=mib,
    )
    def from_xor(array, m):
        return lax.ppermute(array, "rows", [(i, i ^ m) for i in range(n_rows)])

    total = (keep + send + norms).astype(bf16)
    back = jnp.concatenate([out, jnp.broadcast_to(total, (n_tok, h, 128))], 1)
    got = lax.all_to_all(back, "tok", 0, 0, tiled=True)
    mine = call(partial(sum_kernel, tok), sds((h, 128), bf16), got)
    parts = [mine] + [from_xor(mine, m) for m in range(1, n_rows)]
    layer_out, grad_input = call(
        rows_kernel, (sds((rows, tok, width), bf16), sds((rows, tok, width), f32)), got
    )
    sums = call(
        partial(unpack_kernel, n_rows), tuple(sds(p.shape, f32) for p in params), *parts
    )
    sums = sums[:14] + (sums[14].T,) + sums[15:]
    return (layer_out, grad_input) + tuple(sums)


def solution(mesh):
    split3 = P("rows", "tok", None)
    return jax.shard_map(
        shards,
        mesh=mesh,
        in_specs=(split3, P("rows", "tok"), P("rows", None, None)) + (P(),) * 16 + (split3,),
        out_specs=(split3, split3) + (P(),) * 16,
        check_vma=False,
    )
```

```python
from functools import partial

import jax
import jax.numpy as jnp
from jax import lax
from jax.experimental import pallas as pl
from jax.experimental.pallas import tpu as pltpu
from jax.sharding import PartitionSpec as P


NS_STEPS = 6
EPS = 1e-05
RIDGE = 0.1
FAR = 640.0
SEG_ROWS = 16
FIRST = 1
GRAD_ROWS = 272
NORM_ROW = 131

LOG2_E = 1.4426950408889634

f32 = jnp.float32
bf16 = jnp.bfloat16


def mm(a, b):
    return lax.dot_general(a, b, (((1,), (0,)), ((), ())), preferred_element_type=f32)


def mm_nt(a, b):
    return lax.dot_general(a, b, (((1,), (1,)), ((), ())), preferred_element_type=f32)


def mm_tn(a, b):
    return lax.dot_general(a, b, (((0,), (0,)), ((), ())), preferred_element_type=f32)


def split(a):
    hi = a.astype(bf16)
    return hi, (a - hi.astype(f32)).astype(bf16)


def wide_right(b):
    hi, lo = split(b)
    return jnp.concatenate(
        [jnp.concatenate([hi, lo], 1), jnp.concatenate([hi, jnp.zeros_like(hi)], 1)], 0
    )


def mm_wide(a, wide):
    n = wide.shape[1] // 2
    both = mm(jnp.concatenate(split(a), 1), wide)
    return both[:, :n] + both[:, n:]


def row_sum(a):
    return jnp.sum(a, axis=1, keepdims=True)


def col_sum(a):
    return jnp.sum(a, axis=0, keepdims=True)


def total_of(a):
    return col_sum(row_sum(a))


def both_parts(product, a, b):
    n = b.shape[1]
    both = product(a, jnp.concatenate(split(b), 1))
    return both[:, :n] + both[:, n:]


def pair(a, b):
    return jnp.concatenate([a, b], 1)


def wide_mm(a_pair, wide):
    n = wide.shape[1] // 2
    both = mm(a_pair, wide)
    return both[:, :n] + both[:, n:]


def both_parts_left(a, wide):
    n = wide.shape[1] // 2
    return wide_mm(a, wide[:n])


def norm_stats(values):
    n = 1.0 / values.shape[0]
    centre = values - col_sum(values) * n
    scale = lax.rsqrt(col_sum(centre * centre) * n + EPS)
    return centre * scale, scale


def norm_back(d_norm, xhat, scale, gain):
    scaled = d_norm * gain
    n = 1.0 / scaled.shape[0]
    return scale * (scaled - col_sum(scaled) * n - xhat * (col_sum(scaled * xhat) * n))


def iota(shape, dim):
    return lax.broadcasted_iota(jnp.int32, shape, dim)


def row_work(xg, onehot_t, idx, par):
    (gain1, bias1, wq, bq, wk, bk, wv, bv, wo, bo, gain2, bias2, wup, bup, wdown_t, bdown) = par
    tokens = xg.shape[0]
    width = wq.shape[0]
    heads, marks = idx.shape
    size = width // heads
    sharp = size**-0.5
    sharp2 = sharp * LOG2_E
    out_scale = tokens**-0.5
    hm = heads * marks
    hs = range(heads)
    at = [slice(h * marks, (h + 1) * marks) for h in hs]
    rows_of = [slice(h * size, (h + 1) * size) for h in hs]
    chunk = tokens // 4
    chunks = [slice(lo, lo + chunk) for lo in range(0, tokens, chunk)]

    xg_t = xg.astype(f32).T
    x_t, g_t = xg_t[:width], xg_t[width:]
    g16_t = g_t.astype(bf16)
    wqkv = jnp.concatenate([wq, wk, wv], 1)
    wqkv_t = wqkv.astype(f32).T.astype(bf16)
    xhat1, scale1 = norm_stats(x_t)
    normed_t = (xhat1 * gain1 + bias1).astype(bf16)
    qkv_t = mm(wqkv_t, normed_t) + jnp.concatenate([bq, bk, bv], 0)
    qkv16_t = qkv_t.astype(bf16)
    q_t, k_t, v_t = (qkv16_t[i * width : (i + 1) * width] for i in range(3))
    seg_rows = jnp.where(
        (iota(onehot_t.shape, 0) >= 4) & (iota(onehot_t.shape, 0) < 8), 1.0, onehot_t.astype(f32)
    )
    seg_rows = jnp.concatenate(
        [seg_rows, jnp.zeros((width - SEG_ROWS, tokens), f32)], 0
    ).astype(bf16)

    def features(p_t):
        p = p_t.astype(f32)
        sq = p * p
        hi = sq.astype(bf16)
        return jnp.concatenate([p_t, seg_rows, hi, (sq - hi.astype(f32)).astype(bf16)], 0)

    feats_q, feats_k = features(q_t), features(k_t)

    idx_row = jnp.concatenate([idx[h : h + 1] for h in hs], 1)
    pick_t = (iota((2 * tokens, hm), 0) == idx_row).astype(f32).astype(bf16)
    qk_t = jnp.concatenate([q_t, k_t], 1)
    ones16 = jnp.ones((16, tokens), bf16)
    normed_ones = jnp.concatenate([normed_t, ones16], 0)
    seg2 = jnp.concatenate([onehot_t, onehot_t], 1)
    picked = mm(jnp.concatenate([qk_t, seg2], 0), pick_t)
    own = ((iota((width, hm), 0) // size) == (iota((width, hm), 1) // marks)).astype(f32)
    mark_t = picked[:width] * own
    mark_seg = picked[width : width + 8]
    sq = mark_t * mark_t
    half = -0.5 * col_sum(sq)
    half_hi = half.astype(bf16).astype(f32)
    half_mid = (half - half_hi).astype(bf16).astype(f32)
    half_lo = half - half_hi - half_mid
    row8 = iota((8, hm), 0)
    extra = jnp.where(row8 < 4, mark_seg * FAR, 0.0)
    extra = jnp.where(row8 == 4, half_hi, extra)
    extra = jnp.where(row8 == 5, half_mid, extra)
    extra = jnp.where(row8 == 6, half_lo, extra)
    extra = jnp.where(row8 == 7, -FAR, extra)
    pad = jnp.zeros((width - 8, hm), f32)
    squares = iota((hm, 2 * width), 1) % width // size == iota((hm, 2 * width), 0) // marks
    right_m = pair(
        jnp.concatenate([mark_t, extra, pad], 0).T.astype(bf16),
        jnp.where(squares, -0.5, 0.0).astype(bf16),
    )
    sq_hi = sq.astype(bf16).astype(f32)
    left = jnp.concatenate(
        [mark_t, jnp.where(row8 < 4, mark_seg, 1.0), pad, sq_hi, sq - sq_hi], 0
    ).astype(bf16)
    mark16 = mark_t.astype(bf16)

    def near_of(points):
        return jnp.exp2(sharp2 * mm(right_m, points)).astype(bf16)

    eye = (iota((marks, marks), 0) == iota((marks, marks), 1)).astype(f32)
    kernel = [jnp.exp2(sharp2 * mm(right_m[at[h]], left[:, at[h]])) for h in hs]
    gram = [kernel[h] + RIDGE * eye for h in hs]
    sums = [col_sum(gram[h]) for h in hs]
    widest = [jnp.max(sums[h], axis=1, keepdims=True) for h in hs]
    inv2 = [1.0 / (widest[h] * widest[h]) for h in hs]
    gram_wide = [wide_right(gram[h]) for h in hs]
    wo_of = [wo[rows_of[h]] for h in hs]
    rest = [eye - mm_wide(gram[h] * inv2[h], gram_wide[h]) for h in hs]
    v_tok = v_t.astype(f32).T.astype(bf16)
    rests, wides = [rest], []
    near_k, near_q, near_q_tok, summed_t, sent_t, grown = [], [], [], [], [], []

    def add_near_k(i):
        half = tokens // 2
        near_k.append(near_of(feats_k[:, i * half : (i + 1) * half]))

    def add_near_q(i):
        near_q.append(near_of(feats_q[:, chunks[i]]))
        near_q_tok.append(near_q[-1].T)

    def add_sums():
        near_k[:] = [jnp.concatenate(near_k, 1)]
        both = mm(near_k[0], v_tok).T
        summed_t.extend(both[rows_of[h], at[h]] for h in hs)

    def add_sent():
        sent_t.extend(both_parts(mm_tn, wo_of[h], summed_t[h]) for h in hs)
        grown.append([mm_wide(sent_t[h], gram_wide[h]) * inv2[h] for h in hs])

    def two_steps(step):
        nxt = rests[step + 1]
        return [rests[step][h] + nxt[h] + mm_wide(rests[step][h], wides[step + 1][h]) for h in hs]

    def grown_by(now, wide):
        return [now[h] + mm_wide(now[h], wide[h]) for h in hs]

    def widen(both):
        return [wide_right(both[h]) for h in hs]

    def next_rest():
        wides.append(widen(rests[-1]))
        if len(rests) < NS_STEPS:
            rests.append([mm_wide(rests[-1][h], wides[-1][h]) for h in hs])

    add_near_k(0)
    next_rest()
    add_near_k(1)
    next_rest()
    twice = [widen(two_steps(0))]
    add_sums()
    next_rest()
    add_near_q(0)
    add_sent()
    next_rest()
    twice.append(widen(two_steps(2)))
    add_near_q(1)
    grown.extend([None] * NS_STEPS)
    grown[2] = grown_by(grown[0], twice[0])
    next_rest()
    add_near_q(2)
    grown[4] = grown_by(grown[2], twice[1])
    next_rest()
    grown[5] = grown_by(grown[4], wides[4])
    add_near_q(3)
    grown[6] = grown_by(grown[5], wides[5])
    near_k, now = near_k[0], grown[-1]
    near_q = jnp.concatenate(near_q, 1)
    near_q_tok = jnp.concatenate(near_q_tok, 0)
    mixed_t = jnp.concatenate(now, 1).astype(bf16)
    hidden = x_t + (mm(mixed_t, near_q) * out_scale + bo)
    twice.append(widen(two_steps(4)))
    inverse = [gram[h] * inv2[h] for h in hs]
    for wide in twice:
        inverse = grown_by(inverse, wide)
    inverse_wide = widen(inverse)
    grown[1] = grown_by(grown[0], wides[0])
    grown[3] = grown_by(grown[2], wides[2])
    beside_rest = [
        [pair(rests[step][h], grown[step][h].T).astype(bf16) for h in hs]
        for step in range(NS_STEPS)
    ]
    normed_mark = pair(mm(normed_ones, pick_t[:tokens]), mm(normed_ones, pick_t[tokens:])).astype(bf16)
    wup_t = wup.astype(f32).T.astype(bf16)
    d_act = mm_tn(wdown_t, g16_t)
    xhat2, scale2 = norm_stats(hidden)
    normed2_t = (xhat2 * gain2 + bias2).astype(bf16)
    inner = mm(wup_t, normed2_t) + bup
    c = (2.0 / jnp.pi) ** 0.5
    inner2 = inner * inner
    th = jnp.tanh(c * inner * (1.0 + 0.044715 * inner2))
    act = (0.5 * inner * (1.0 + th)).astype(bf16)

    slope = 0.5 * (1.0 + th) + 0.5 * inner * (1.0 - th * th) * (
        c * (1.0 + (3.0 * 0.044715) * inner2)
    )
    d_inner = (d_act * slope).astype(bf16)
    d_norm2 = mm(wup, d_inner)
    layer_out = hidden + (mm(wdown_t, act) + bdown)
    d_hidden = g_t + norm_back(d_norm2, xhat2, scale2, gain2)
    d_branch = d_hidden.astype(bf16)
    d_sent_t = mm(d_branch, near_q_tok) * out_scale
    back = [d_sent_t[:, at[h]] for h in hs]

    beside_gram = [pair(sent_t[h].T, -gram[h]).astype(bf16) for h in hs]
    kernel_inv = [kernel[h] * inv2[h] for h in hs]
    widest_a = [(2.0 / widest[h]) * (eye - rests[0][h]) for h in hs]
    widest_b = [(2.0 / widest[h]) * grown[0][h] for h in hs]
    mark_both = jnp.concatenate([mark16, own.astype(bf16)], 0)
    mark_ones = [
        jnp.concatenate([mark16[:, at[h]], jnp.ones((16, marks), bf16)], 0) for h in hs
    ]
    top_part = []
    for h in hs:
        top = (sums[h] == widest[h]).astype(f32)
        top = top * (1.0 / row_sum(top))
        seen = kernel[h].astype(bf16)
        along = jnp.broadcast_to(top, (16, marks)).astype(bf16)
        top_part.append(
            top * mm(mark_ones[h], seen)
            + mm_nt(mark_ones[h], along)[:, :1] * mm(along, seen)[:1]
        )
    mixed = [mm_wide(summed_t[h], inverse_wide[h]) for h in hs]
    blank_h = jnp.zeros((size, marks), f32)
    mixed_m = jnp.concatenate(
        [jnp.concatenate([mixed[h] if g == h else blank_h for g in hs], 1) for h in hs], 0
    ).T.astype(bf16)
    d_att = mm(wo, d_branch).astype(bf16)
    q_tok = q_t.astype(f32).T.astype(bf16)
    k_tok = k_t.astype(f32).T.astype(bf16)
    ones_tok = jnp.ones((tokens, width), bf16)
    d_start = [mm_wide(back[h], inverse_wide[h]) for h in hs]
    d_att_early = mm(wo, d_branch).astype(bf16)
    d_mixed = mm(d_att_early, near_q_tok) * out_scale
    d_mixed = [d_mixed[rows_of[h], at[h]].astype(bf16) for h in hs]
    d_summed = [both_parts_left(d_mixed[h], inverse_wide[h]) for h in hs]
    none = jnp.zeros((size, marks), f32)
    d_summed_t = jnp.concatenate(
        [jnp.concatenate([d_summed[h] if g == h else none for g in hs], 1) for h in hs], 0
    )
    d_summed_m = d_summed_t.T.astype(bf16)
    def stays(pull, p_t):
        both = mm(mark_both, pull)
        return sharp * (both[:width] - both[width:] * p_t.astype(f32))

    pulls_q, toks = [], []

    def pull_some(i):
        now_at = chunks[i]
        pull = (mm(mixed_m, d_att[:, now_at]) * out_scale).astype(bf16)
        pulls_q.append((pull.astype(f32) * near_q[:, now_at].astype(f32)).astype(bf16))

    def pull_rest():
        pull = mm(d_summed_m, v_t).astype(bf16)
        pulls_q.append((pull.astype(f32) * near_k.astype(f32)).astype(bf16))

    def add_tok(pull, tok):
        toks.append(mm(pull, pair(tok, ones_tok)))

    def add_tok_q():
        pulls_q[:4] = [jnp.concatenate(pulls_q[:4], 1)]
        add_tok(pulls_q[0], q_tok)

    def add_tok_k():
        add_tok(pulls_q[1], k_tok)

    early = {}

    def add_down():
        early["down"] = mm_nt(g16_t, act)

    def add_up():
        early["up"] = mm_nt(jnp.concatenate([normed2_t, ones16], 0), d_inner)

    def add_bias():
        early["bias"] = mm_nt(ones16, jnp.concatenate([g16_t, d_branch], 0))

    def add_wo():
        early["wo"] = jnp.concatenate(
            [mm_nt(summed_t[h].astype(bf16), d_start[h].astype(bf16)) for h in hs], 0
        )

    def add_stay():
        stay_q, stay_k = stays(pulls_q[0], q_t), stays(pulls_q[1], k_t)
        dv = mm(d_summed_t.astype(bf16), near_k)
        early["stay"] = jnp.concatenate([stay_q, stay_k, dv], 0).astype(bf16)

    def add_qkv():
        early["qkv"] = mm_nt(normed_ones, early["stay"])

    def add_normed():
        early["normed"] = mm(wqkv, early["stay"])

    beside = [
        [partial(pull_some, 0), partial(pull_some, 1), partial(pull_some, 2), partial(pull_some, 3)],
        [add_tok_q, pull_rest],
        [add_tok_k],
        [add_stay],
        [add_up, add_down],
        [add_qkv, add_normed, add_bias, add_wo],
    ]
    b16 = [back[h].astype(bf16) for h in hs]
    last = NS_STEPS - 1
    d_rest = [mm(beside_rest[last][h][:, marks:], b16[h]) for h in hs]
    back = [back[h] + wide_mm(b16[h], wides[last][h][:marks]) for h in hs]
    for step in reversed(range(NS_STEPS)):
        if step < last:
            both16 = [
                jnp.concatenate([d_rest[h].astype(bf16), back[h].astype(bf16)], 0) for h in hs
            ]
            turned = [
                mm_wide(jnp.concatenate([d_rest[h], back[h]], 0), wides[step][h]) for h in hs
            ]
            back = [back[h] + turned[h][marks:] for h in hs]
            d_rest = [turned[h][:marks] + mm(beside_rest[step][h], both16[h]) for h in hs]
        for work in beside[last - step]:
            work()
    d16 = [d_rest[h].astype(bf16) for h in hs]
    d_gram = [
        mm(beside_gram[h], jnp.concatenate([back[h].astype(bf16), d16[h]], 0))
        - wide_mm(d16[h], gram_wide[h][:marks])
        for h in hs
    ]
    tok_both = (toks[0] + toks[1]).T
    tok_t, tok_sum = tok_both[:width], tok_both[width : width + 1]
    stay, d_normed_tok = early["stay"], early["normed"]
    gram_part = []
    for h in hs:
        d_widest = total_of(d_rest[h] * widest_a[h]) - total_of(back[h] * widest_b[h])
        weighted = ((d_gram[h] + d_gram[h].T) * kernel_inv[h]).astype(bf16)
        gram_part.append(mm(mark_ones[h], weighted) + d_widest * top_part[h])
    gram_part = jnp.concatenate(gram_part, 1)
    d_mark_t = (
        (tok_t + gram_part[:width] - mark_t * (tok_sum + gram_part[width : width + 1])) * own
    ).astype(bf16)
    g_bias, g_wo = early["bias"], early["wo"]
    g_down, g_up = early["down"], early["up"]
    by_mark = sharp * pair(
        mm_nt(normed_mark[:, :hm], d_mark_t), mm_nt(normed_mark[:, hm:], d_mark_t)
    )
    g_qkv = early["qkv"] + pair(by_mark, jnp.zeros((width + 16, width), f32))
    columns = [
        row_sum(d_norm2 * xhat2),
        row_sum(d_norm2),
    ]
    lane = iota((width, 128), 1)
    norms = sum(jnp.where(lane == i, col, 0.0) for i, col in enumerate(columns)).T[:8]
    g_bqkv = g_qkv[width : width + 1]
    blank = jnp.zeros((1, 2 * width), f32)
    grads = jnp.concatenate(
        [
            g_up[:width],
            g_down[:width],
            g_up[width : width + 1],
            pair(g_bias[:1, :width], g_bqkv[:, :width]),
            g_bqkv[:, width:],
        ]
        + [blank] * 5
        + [
            g_qkv[:width, : 2 * width],
            pair(g_qkv[:width, 2 * width :], g_wo),
            pair(g_bias[:1, width:], norms[0:1]),
            pair(norms[1:2], blank[:, :width]),
        ]
        + [blank] * 6,
        0,
    )
    later = (d_mark_t, d_normed_tok, d_hidden, xhat1, scale1, layer_out)
    return later, grads


def row_end(later, idx, par):
    gain1, wq, wk = par
    d_mark_t, d_normed_tok, d_hidden, xhat1, scale1, layer_out = later
    width, tokens = xhat1.shape
    heads, marks = idx.shape
    hm = heads * marks
    idx_row = jnp.concatenate([idx[h : h + 1] for h in range(heads)], 1)
    idx_col = jnp.broadcast_to(idx_row.astype(f32), (8, hm)).T[:, :1].astype(jnp.int32)
    tok_lane = iota((hm, tokens), 1)
    pick_m = jnp.concatenate([tok_lane == idx_col, tok_lane + tokens == idx_col], 0)
    pick_m = pick_m.astype(f32).astype(bf16)
    onto = mm(jnp.concatenate([wq, wk], 0), d_mark_t).astype(bf16)
    moved = mm(pair(onto[:width], onto[width:]), pick_m)
    d_normed = d_normed_tok + (width // heads) ** -0.5 * moved
    grad_in = d_hidden + norm_back(d_normed, xhat1, scale1, gain1)
    lane = iota((width, 128), 1)
    sums = jnp.where(lane == 0, row_sum(d_normed * xhat1), 0.0) + jnp.where(
        lane == 1, row_sum(d_normed), 0.0
    )
    sums = sums.T
    return jnp.concatenate([layer_out, grad_in], 0).T.astype(bf16), pair(sums[:1], sums[1:2])


MATRICES = (2, 4, 6, 8, 12, 14)
VECTORS = (0, 1, 3, 5, 7, 9, 10, 11, 13, 15)


def read_params(mats, vec_cols):
    par = [None] * 16
    for i, ref in zip(MATRICES, mats):
        par[i] = ref[...]
    for row, i in enumerate(VECTORS):
        wide = par[12].shape[1] if i == 13 else par[2].shape[0]
        par[i] = vec_cols[:wide, row : row + 1]
    return tuple(par)


def own_row(idx_ref):
    return idx_ref[jnp.clip(lax.axis_index("tok") - FIRST, 0, idx_ref.shape[0] - 1)]


def for_owners(idx_ref, work, zeroed):
    row = lax.axis_index("tok") - FIRST
    has_row = (row >= 0) & (row < idx_ref.shape[0])
    pl.when(has_row)(work)

    @pl.when(jnp.logical_not(has_row))
    def _():
        for ref in zeroed:
            ref[...] = jnp.zeros(ref.shape, ref.dtype)


def main_kernel(tok_block, blk_ref, idx_ref, vec_ref, *refs):
    mats, later_refs, (keep_ref, send_ref) = refs[:6], refs[6:-2], refs[-2:]

    def work():
        blocks = blk_ref.shape[0]
        tokens = blocks * tok_block
        xg = blk_ref[:, :tok_block, :].reshape(tokens, 128)
        ids = blk_ref[:, tok_block:, :].astype(f32)
        half = iota((SEG_ROWS, 128), 1) < tok_block
        onehot_t = jnp.concatenate(
            [jnp.where(half, ids[2 * j], ids[2 * j + 1]) for j in range(blocks // 2)], 1
        ).astype(bf16)
        later, grads = row_work(xg, onehot_t, own_row(idx_ref), read_params(mats, vec_ref[...].T))
        for ref, value in zip(later_refs, later):
            ref[...] = value
        first = lax.rem(lax.axis_index("rows"), 2) == 0
        h = GRAD_ROWS // 2
        keep_ref[...] = jnp.where(first, grads[:h], grads[h:])
        send_ref[...] = jnp.where(first, grads[h:], grads[:h])

    for_owners(idx_ref, work, (keep_ref, send_ref))


def end_kernel(idx_ref, vec_ref, wq_ref, wk_ref, *refs):
    later_refs, out_ref, norm_ref = refs[:-2], refs[-2], refs[-1]

    def work():
        later = [ref[...] for ref in later_refs]
        gain1 = vec_ref[...].T[: wq_ref.shape[0], :1]
        out, sums = row_end(later, own_row(idx_ref), (gain1, wq_ref[...], wk_ref[...]))
        out_ref[...] = out.reshape(out_ref.shape)
        norm_ref[...] = jnp.where(iota(norm_ref.shape, 0) == NORM_ROW, sums, 0.0)

    for_owners(idx_ref, work, (out_ref, norm_ref))


def pack_kernel(xg_ref, s_ref, *refs):
    vecs, (out_ref, vec_ref) = refs[:-2], refs[-2:]
    rows, tok, width = xg_ref.shape
    out_ref[:FIRST] = jnp.zeros((FIRST,) + out_ref.shape[1:], bf16)
    out_ref[FIRST : rows + FIRST, :tok, :] = xg_ref[...]
    unused = out_ref.shape[0] - rows - FIRST
    if unused:
        out_ref[rows + FIRST :] = jnp.zeros((unused,) + out_ref.shape[1:], bf16)
    seg = s_ref[...]
    seg = jnp.concatenate([seg, seg], 1)
    for r in range(rows):
        ids = jnp.broadcast_to(seg[r : r + 1], (SEG_ROWS, width))
        out_ref[FIRST + r, tok:, :] = (ids == iota((SEG_ROWS, width), 0)).astype(f32).astype(bf16)
    for i, ref in enumerate(vecs):
        vec_ref[i : i + 1, : ref.shape[0]] = ref[...].astype(f32).reshape(1, -1)


def sum_kernel(tok, got_ref, sum_ref):
    total = got_ref[0, tok:, :].astype(f32)
    for j in range(1, got_ref.shape[0]):
        total = total + got_ref[j, tok:, :].astype(f32)
    sum_ref[...] = total.astype(bf16)


def rows_kernel(got_ref, out_ref, grad_ref):
    rows, tok, width = out_ref.shape
    out_ref[...] = got_ref[FIRST : rows + FIRST, :tok, :width]
    grad_ref[...] = got_ref[FIRST : rows + FIRST, :tok, width:].astype(f32)


def unpack_kernel(n_parts, *refs):
    parts, outs = refs[:n_parts], refs[n_parts:]
    parts = [p[...].astype(f32) for p in parts]
    halves = [sum(parts[core + 2 :: 2], parts[core]) for core in range(2)]
    norms = halves[0][NORM_ROW] + halves[1][NORM_ROW]
    first = lax.rem(lax.axis_index("rows"), 2) == 0
    a = jnp.where(first, halves[0], halves[1])
    b = jnp.where(first, halves[1], halves[0])
    whole = jnp.concatenate([a, b], 0)
    (gain1, bias1, wq, bq, wk, bk, wv, bv, wo, bo, gain2, bias2, wup, bup, wdown_t, bdown) = outs
    wup[...] = whole[0:64]
    wdown_t[...] = whole[64:128]
    bup[...] = whole[128]
    bdown[...] = whole[129, :64]
    bq[...] = whole[129, 64:]
    bk[...] = whole[130, :64]
    bv[...] = whole[130, 64:]
    wq[...] = whole[136:200, :64]
    wk[...] = whole[136:200, 64:]
    wv[...] = whole[200:264, :64]
    wo[...] = whole[200:264, 64:]
    bo[...] = whole[264, :64]
    gain2[...] = whole[264, 64:]
    bias2[...] = whole[265, :64]
    gain1[...] = norms[:64]
    bias1[...] = norms[64:]


def call(kernel, outs, *args, mib=12):
    vmem = pl.BlockSpec(memory_space=pltpu.VMEM)
    return pl.pallas_call(
        kernel,
        out_shape=outs,
        in_specs=[vmem] * len(args),
        out_specs=jax.tree.map(lambda _: vmem, outs),
        compiler_params=pltpu.CompilerParams(vmem_limit_bytes=mib * 1024 * 1024),
    )(*args)


def shards(tokens_in, segments, landmark_index, *rest):
    params, grad_out = rest[:14] + (rest[14].T, rest[15]), rest[16]
    rows, tok, width = tokens_in.shape
    n_tok = lax.axis_size("tok")
    n_rows = lax.axis_size("rows")
    sds = jax.ShapeDtypeStruct
    sent, vecs = call(
        pack_kernel,
        (sds((n_tok, tok + SEG_ROWS, 128), bf16), sds((16, 128), f32)),
        jnp.concatenate([tokens_in, grad_out], 2),
        segments,
        *[params[i] for i in VECTORS],
        mib=4,
    )
    got = lax.all_to_all(sent, "tok", 0, 0, tiled=True)
    h = GRAD_ROWS // 2
    tokens = n_tok * tok
    mib = 12 * max(1, tokens // 512)
    by_token = sds((width, tokens), f32)
    marks = landmark_index.shape[1] * landmark_index.shape[2]
    *later, keep, send = call(
        partial(main_kernel, tok),
        (sds((width, marks), bf16),)
        + (by_token,) * 3
        + (sds((1, tokens), f32), by_token)
        + (sds((h, 128), f32),) * 2,
        got,
        landmark_index,
        vecs,
        *[params[i] for i in MATRICES],
        mib=mib,
    )
    send = lax.ppermute(send, "rows", [(i, i ^ 1) for i in range(n_rows)])
    out, norms = call(
        end_kernel,
        (sds((n_tok, tok, 128), bf16), sds((h, 128), f32)),
        landmark_index,
        vecs,
        params[2],
        params[4],
        *later,
        mib=mib,
    )
    def from_xor(array, m):
        return lax.ppermute(array, "rows", [(i, i ^ m) for i in range(n_rows)])

    total = (keep + send + norms).astype(bf16)
    back = jnp.concatenate([out, jnp.broadcast_to(total, (n_tok, h, 128))], 1)
    got = lax.all_to_all(back, "tok", 0, 0, tiled=True)
    mine = call(partial(sum_kernel, tok), sds((h, 128), bf16), got)
    parts = [mine] + [from_xor(mine, m) for m in range(1, n_rows)]
    layer_out, grad_input = call(
        rows_kernel, (sds((rows, tok, width), bf16), sds((rows, tok, width), f32)), got
    )
    sums = call(
        partial(unpack_kernel, n_rows), tuple(sds(p.shape, f32) for p in params), *parts
    )
    sums = sums[:14] + (sums[14].T,) + sums[15:]
    return (layer_out, grad_input) + tuple(sums)


def solution(mesh):
    split3 = P("rows", "tok", None)
    return jax.shard_map(
        shards,
        mesh=mesh,
        in_specs=(split3, P("rows", "tok"), P("rows", None, None)) + (P(),) * 16 + (split3,),
        out_specs=(split3, split3) + (P(),) * 16,
        check_vma=False,
    )
```

```python
from functools import partial

import jax
import jax.numpy as jnp
from jax import lax
from jax.experimental import pallas as pl
from jax.experimental.pallas import tpu as pltpu
from jax.sharding import PartitionSpec as P


NS_STEPS = 6
EPS = 1e-05
RIDGE = 0.1
FAR = 640.0
SEG_ROWS = 8
FIRST = 1
GRAD_ROWS = 272
NORM_ROW = 131

LOG2_E = 1.4426950408889634

f32 = jnp.float32
bf16 = jnp.bfloat16


def mm(a, b):
    return lax.dot_general(a, b, (((1,), (0,)), ((), ())), preferred_element_type=f32)


def mm_nt(a, b):
    return lax.dot_general(a, b, (((1,), (1,)), ((), ())), preferred_element_type=f32)


def mm_tn(a, b):
    return lax.dot_general(a, b, (((0,), (0,)), ((), ())), preferred_element_type=f32)


def split(a):
    hi = a.astype(bf16)
    return hi, (a - hi.astype(f32)).astype(bf16)


def wide_right(b):
    hi, lo = split(b)
    return jnp.concatenate(
        [jnp.concatenate([hi, lo], 1), jnp.concatenate([hi, jnp.zeros_like(hi)], 1)], 0
    )


def mm_wide(a, wide):
    n = wide.shape[1] // 2
    both = mm(jnp.concatenate(split(a), 1), wide)
    return both[:, :n] + both[:, n:]


def row_sum(a):
    return jnp.sum(a, axis=1, keepdims=True)


def col_sum(a):
    return jnp.sum(a, axis=0, keepdims=True)


def total_of(a):
    return col_sum(row_sum(a))


def both_parts(product, a, b):
    n = b.shape[1]
    both = product(a, jnp.concatenate(split(b), 1))
    return both[:, :n] + both[:, n:]


def pair(a, b):
    return jnp.concatenate([a, b], 1)


def wide_mm(a_pair, wide):
    n = wide.shape[1] // 2
    both = mm(a_pair, wide)
    return both[:, :n] + both[:, n:]


def both_parts_left(a, wide):
    n = wide.shape[1] // 2
    return wide_mm(a, wide[:n])


def norm_stats(values):
    n = 1.0 / values.shape[0]
    centre = values - col_sum(values) * n
    scale = lax.rsqrt(col_sum(centre * centre) * n + EPS)
    return centre * scale, scale


def norm_back(d_norm, xhat, scale, gain):
    scaled = d_norm * gain
    n = 1.0 / scaled.shape[0]
    return scale * (scaled - col_sum(scaled) * n - xhat * (col_sum(scaled * xhat) * n))


def iota(shape, dim):
    return lax.broadcasted_iota(jnp.int32, shape, dim)


def row_work(xg, onehot_t, idx, par):
    (gain1, bias1, wq, bq, wk, bk, wv, bv, wo, bo, gain2, bias2, wup, bup, wdown_t, bdown) = par
    tokens = xg.shape[0]
    width = wq.shape[0]
    heads, marks = idx.shape
    size = width // heads
    sharp = size**-0.5
    sharp2 = sharp * LOG2_E
    out_scale = tokens**-0.5
    hm = heads * marks
    hs = range(heads)
    at = [slice(h * marks, (h + 1) * marks) for h in hs]
    rows_of = [slice(h * size, (h + 1) * size) for h in hs]
    chunk = tokens // 4
    chunks = [slice(lo, lo + chunk) for lo in range(0, tokens, chunk)]

    xg_t = xg.astype(f32).T
    x_t, g_t = xg_t[:width], xg_t[width:]
    g16_t = g_t.astype(bf16)
    wqkv = jnp.concatenate([wq, wk, wv], 1)
    wqkv_t = wqkv.astype(f32).T.astype(bf16)
    xhat1, scale1 = norm_stats(x_t)
    normed_t = (xhat1 * gain1 + bias1).astype(bf16)
    qkv_t = mm(wqkv_t, normed_t) + jnp.concatenate([bq, bk, bv], 0)
    qkv16_t = qkv_t.astype(bf16)
    q_t, k_t, v_t = (qkv16_t[i * width : (i + 1) * width] for i in range(3))
    seg_rows = jnp.where(
        (iota(onehot_t.shape, 0) >= 4) & (iota(onehot_t.shape, 0) < 8), 1.0, onehot_t.astype(f32)
    )
    seg_rows = jnp.concatenate(
        [seg_rows, jnp.zeros((width - SEG_ROWS, tokens), f32)], 0
    ).astype(bf16)

    def features(p_t):
        p = p_t.astype(f32)
        sq = p * p
        hi = sq.astype(bf16)
        return jnp.concatenate([p_t, seg_rows, hi, (sq - hi.astype(f32)).astype(bf16)], 0)

    feats_q, feats_k = features(q_t), features(k_t)

    idx_row = jnp.concatenate([idx[h : h + 1] for h in hs], 1)
    pick_t = (iota((2 * tokens, hm), 0) == idx_row).astype(f32).astype(bf16)
    qk_t = jnp.concatenate([q_t, k_t], 1)
    ones16 = jnp.ones((16, tokens), bf16)
    normed_ones = jnp.concatenate([normed_t, ones16], 0)
    seg2 = jnp.concatenate([onehot_t, onehot_t], 1)
    picked = mm(jnp.concatenate([qk_t, seg2], 0), pick_t)
    own = ((iota((width, hm), 0) // size) == (iota((width, hm), 1) // marks)).astype(f32)
    mark_t = picked[:width] * own
    mark_seg = picked[width : width + 8]
    sq = mark_t * mark_t
    half = -0.5 * col_sum(sq)
    half_hi = half.astype(bf16).astype(f32)
    half_mid = (half - half_hi).astype(bf16).astype(f32)
    half_lo = half - half_hi - half_mid
    row8 = iota((8, hm), 0)
    extra = jnp.where(row8 < 4, mark_seg * FAR, 0.0)
    extra = jnp.where(row8 == 4, half_hi, extra)
    extra = jnp.where(row8 == 5, half_mid, extra)
    extra = jnp.where(row8 == 6, half_lo, extra)
    extra = jnp.where(row8 == 7, -FAR, extra)
    pad = jnp.zeros((width - 8, hm), f32)
    squares = iota((hm, 2 * width), 1) % width // size == iota((hm, 2 * width), 0) // marks
    right_m = pair(
        jnp.concatenate([mark_t, extra, pad], 0).T.astype(bf16),
        jnp.where(squares, -0.5, 0.0).astype(bf16),
    )
    sq_hi = sq.astype(bf16).astype(f32)
    left = jnp.concatenate(
        [mark_t, jnp.where(row8 < 4, mark_seg, 1.0), pad, sq_hi, sq - sq_hi], 0
    ).astype(bf16)
    mark16 = mark_t.astype(bf16)

    def near_of(points):
        return jnp.exp2(sharp2 * mm(right_m, points)).astype(bf16)

    eye = (iota((marks, marks), 0) == iota((marks, marks), 1)).astype(f32)
    kernel = [jnp.exp2(sharp2 * mm(right_m[at[h]], left[:, at[h]])) for h in hs]
    gram = [kernel[h] + RIDGE * eye for h in hs]
    sums = [col_sum(gram[h]) for h in hs]
    widest = [jnp.max(sums[h], axis=1, keepdims=True) for h in hs]
    inv2 = [1.0 / (widest[h] * widest[h]) for h in hs]
    gram_wide = [wide_right(gram[h]) for h in hs]
    wo_of = [wo[rows_of[h]] for h in hs]
    rest = [eye - mm_wide(gram[h] * inv2[h], gram_wide[h]) for h in hs]
    v_tok = v_t.astype(f32).T.astype(bf16)
    rests, wides = [rest], []
    near_k, near_q, near_q_tok, summed_t, sent_t, grown = [], [], [], [], [], []

    def add_near_k(i):
        half = tokens // 2
        near_k.append(near_of(feats_k[:, i * half : (i + 1) * half]))

    def add_near_q(i):
        near_q.append(near_of(feats_q[:, chunks[i]]))
        near_q_tok.append(near_q[-1].T)

    def add_sums():
        near_k[:] = [jnp.concatenate(near_k, 1)]
        both = mm(near_k[0], v_tok).T
        summed_t.extend(both[rows_of[h], at[h]] for h in hs)

    def add_sent():
        sent_t.extend(both_parts(mm_tn, wo_of[h], summed_t[h]) for h in hs)
        grown.append([mm_wide(sent_t[h], gram_wide[h]) * inv2[h] for h in hs])

    def two_steps(step):
        nxt = rests[step + 1]
        return [rests[step][h] + nxt[h] + mm_wide(rests[step][h], wides[step + 1][h]) for h in hs]

    def grown_by(now, wide):
        return [now[h] + mm_wide(now[h], wide[h]) for h in hs]

    def widen(both):
        return [wide_right(both[h]) for h in hs]

    def next_rest():
        wides.append(widen(rests[-1]))
        if len(rests) < NS_STEPS:
            rests.append([mm_wide(rests[-1][h], wides[-1][h]) for h in hs])

    add_near_k(0)
    next_rest()
    add_near_k(1)
    next_rest()
    twice = [widen(two_steps(0))]
    add_sums()
    next_rest()
    add_near_q(0)
    add_sent()
    next_rest()
    twice.append(widen(two_steps(2)))
    add_near_q(1)
    grown.extend([None] * NS_STEPS)
    grown[2] = grown_by(grown[0], twice[0])
    next_rest()
    add_near_q(2)
    grown[4] = grown_by(grown[2], twice[1])
    next_rest()
    grown[5] = grown_by(grown[4], wides[4])
    add_near_q(3)
    grown[6] = grown_by(grown[5], wides[5])
    near_k, now = near_k[0], grown[-1]
    near_q = jnp.concatenate(near_q, 1)
    near_q_tok = jnp.concatenate(near_q_tok, 0)
    mixed_t = jnp.concatenate(now, 1).astype(bf16)
    hidden = x_t + (mm(mixed_t, near_q) * out_scale + bo)
    twice.append(widen(two_steps(4)))
    inverse = [gram[h] * inv2[h] for h in hs]
    for wide in twice:
        inverse = grown_by(inverse, wide)
    inverse_wide = widen(inverse)
    grown[1] = grown_by(grown[0], wides[0])
    grown[3] = grown_by(grown[2], wides[2])
    beside_rest = [
        [pair(rests[step][h], grown[step][h].T).astype(bf16) for h in hs]
        for step in range(NS_STEPS)
    ]
    normed_mark = pair(mm(normed_ones, pick_t[:tokens]), mm(normed_ones, pick_t[tokens:])).astype(bf16)
    wup_t = wup.astype(f32).T.astype(bf16)
    d_act = mm_tn(wdown_t, g16_t)
    xhat2, scale2 = norm_stats(hidden)
    normed2_t = (xhat2 * gain2 + bias2).astype(bf16)
    inner = mm(wup_t, normed2_t) + bup
    c = (2.0 / jnp.pi) ** 0.5
    inner2 = inner * inner
    th = jnp.tanh(c * inner * (1.0 + 0.044715 * inner2))
    act = (0.5 * inner * (1.0 + th)).astype(bf16)

    slope = 0.5 * (1.0 + th) + 0.5 * inner * (1.0 - th * th) * (
        c * (1.0 + (3.0 * 0.044715) * inner2)
    )
    d_inner = (d_act * slope).astype(bf16)
    d_norm2 = mm(wup, d_inner)
    layer_out = hidden + (mm(wdown_t, act) + bdown)
    d_hidden = g_t + norm_back(d_norm2, xhat2, scale2, gain2)
    d_branch = d_hidden.astype(bf16)
    d_sent_t = mm(d_branch, near_q_tok) * out_scale
    back = [d_sent_t[:, at[h]] for h in hs]

    mark_both = jnp.concatenate([mark16, own.astype(bf16)], 0)
    mixed = [mm_wide(summed_t[h], inverse_wide[h]) for h in hs]
    blank_h = jnp.zeros((size, marks), f32)
    mixed_m = jnp.concatenate(
        [jnp.concatenate([mixed[h] if g == h else blank_h for g in hs], 1) for h in hs], 0
    ).T.astype(bf16)
    d_att = mm(wo, d_branch).astype(bf16)
    q_tok = q_t.astype(f32).T.astype(bf16)
    k_tok = k_t.astype(f32).T.astype(bf16)
    ones_tok = jnp.ones((tokens, width), bf16)
    def stays(pull, p_t):
        both = mm(mark_both, pull)
        return sharp * (both[:width] - both[width:] * p_t.astype(f32))

    pulls_q, toks = [], []

    def pull_some(i):
        now_at = chunks[i]
        pull = (mm(mixed_m, d_att[:, now_at]) * out_scale).astype(bf16)
        pulls_q.append((pull.astype(f32) * near_q[:, now_at].astype(f32)).astype(bf16))

    def pull_rest():
        pull = mm(early["d_summed_m"], v_t).astype(bf16)
        pulls_q.append((pull.astype(f32) * near_k.astype(f32)).astype(bf16))

    def add_tok(pull, tok):
        toks.append(mm(pull, pair(tok, ones_tok)))

    def add_tok_q():
        pulls_q[:4] = [jnp.concatenate(pulls_q[:4], 1)]
        add_tok(pulls_q[0], q_tok)

    def add_tok_k():
        add_tok(pulls_q[1], k_tok)

    early = {}
    first_back = back

    def add_end():
        beside_gram = [pair(sent_t[h].T, -gram[h]).astype(bf16) for h in hs]
        kernel_inv = [kernel[h] * inv2[h] for h in hs]
        widest_a = [(2.0 / widest[h]) * (eye - rests[0][h]) for h in hs]
        widest_b = [(2.0 / widest[h]) * grown[0][h] for h in hs]
        mark_ones = [
            jnp.concatenate([mark16[:, at[h]], jnp.ones((16, marks), bf16)], 0) for h in hs
        ]
        top_part = []
        for h in hs:
            top = (sums[h] == widest[h]).astype(f32)
            top = top * (1.0 / row_sum(top))
            seen = kernel[h].astype(bf16)
            along = jnp.broadcast_to(top, (16, marks)).astype(bf16)
            top_part.append(
                top * mm(mark_ones[h], seen)
                + mm_nt(mark_ones[h], along)[:, :1] * mm(along, seen)[:1]
            )
        early.update(
            beside_gram=beside_gram,
            kernel_inv=kernel_inv,
            widest_a=widest_a,
            widest_b=widest_b,
            mark_ones=mark_ones,
            top_part=top_part,
        )

    def add_summed():
        d_start = [mm_wide(first_back[h], inverse_wide[h]) for h in hs]
        d_att_early = mm(wo, d_branch).astype(bf16)
        d_mixed = mm(d_att_early, near_q_tok) * out_scale
        d_mixed = [d_mixed[rows_of[h], at[h]].astype(bf16) for h in hs]
        d_summed = [both_parts_left(d_mixed[h], inverse_wide[h]) for h in hs]
        none = jnp.zeros((size, marks), f32)
        d_summed_t = jnp.concatenate(
            [jnp.concatenate([d_summed[h] if g == h else none for g in hs], 1) for h in hs], 0
        )
        d_summed_m = d_summed_t.T.astype(bf16)
        early.update(
            d_start=d_start,
            d_summed_t=d_summed_t,
            d_summed_m=d_summed_m,
        )


    def add_down():
        early["down"] = mm_nt(g16_t, act)

    def add_up():
        early["up"] = mm_nt(jnp.concatenate([normed2_t, ones16], 0), d_inner)

    def add_bias():
        early["bias"] = mm_nt(ones16, jnp.concatenate([g16_t, d_branch], 0))

    def add_wo():
        early["wo"] = jnp.concatenate(
            [mm_nt(summed_t[h].astype(bf16), early["d_start"][h].astype(bf16)) for h in hs], 0
        )

    def add_stay():
        stay_q, stay_k = stays(pulls_q[0], q_t), stays(pulls_q[1], k_t)
        dv = mm(early["d_summed_t"].astype(bf16), near_k)
        early["stay"] = jnp.concatenate([stay_q, stay_k, dv], 0).astype(bf16)

    def add_qkv():
        early["qkv"] = mm_nt(normed_ones, early["stay"])

    def add_normed():
        early["normed"] = mm(wqkv, early["stay"])

    beside = [
        [add_summed, partial(pull_some, 0), partial(pull_some, 1)],
        [partial(pull_some, 2), partial(pull_some, 3), pull_rest],
        [add_tok_q, add_tok_k],
        [add_stay],
        [add_up, add_down, add_end],
        [add_qkv, add_normed, add_bias, add_wo],
    ]
    b16 = [back[h].astype(bf16) for h in hs]
    last = NS_STEPS - 1
    d_rest = [mm(beside_rest[last][h][:, marks:], b16[h]) for h in hs]
    back = [back[h] + wide_mm(b16[h], wides[last][h][:marks]) for h in hs]
    for step in reversed(range(NS_STEPS)):
        if step < last:
            both16 = [
                jnp.concatenate([d_rest[h].astype(bf16), back[h].astype(bf16)], 0) for h in hs
            ]
            turned = [
                mm_wide(jnp.concatenate([d_rest[h], back[h]], 0), wides[step][h]) for h in hs
            ]
            back = [back[h] + turned[h][marks:] for h in hs]
            d_rest = [turned[h][:marks] + mm(beside_rest[step][h], both16[h]) for h in hs]
        for work in beside[last - step]:
            work()
    d16 = [d_rest[h].astype(bf16) for h in hs]
    d_gram = [
        mm(early["beside_gram"][h], jnp.concatenate([back[h].astype(bf16), d16[h]], 0))
        - wide_mm(d16[h], gram_wide[h][:marks])
        for h in hs
    ]
    tok_both = (toks[0] + toks[1]).T
    tok_t, tok_sum = tok_both[:width], tok_both[width : width + 1]
    stay, d_normed_tok = early["stay"], early["normed"]
    gram_part = []
    for h in hs:
        d_widest = total_of(d_rest[h] * early["widest_a"][h]) - total_of(back[h] * early["widest_b"][h])
        weighted = ((d_gram[h] + d_gram[h].T) * early["kernel_inv"][h]).astype(bf16)
        gram_part.append(mm(early["mark_ones"][h], weighted) + d_widest * early["top_part"][h])
    gram_part = jnp.concatenate(gram_part, 1)
    d_mark_t = (
        (tok_t + gram_part[:width] - mark_t * (tok_sum + gram_part[width : width + 1])) * own
    ).astype(bf16)
    g_bias, g_wo = early["bias"], early["wo"]
    g_down, g_up = early["down"], early["up"]
    by_mark = sharp * pair(
        mm_nt(normed_mark[:, :hm], d_mark_t), mm_nt(normed_mark[:, hm:], d_mark_t)
    )
    g_qkv = early["qkv"] + pair(by_mark, jnp.zeros((width + 16, width), f32))
    columns = [
        row_sum(d_norm2 * xhat2),
        row_sum(d_norm2),
    ]
    lane = iota((width, 128), 1)
    norms = sum(jnp.where(lane == i, col, 0.0) for i, col in enumerate(columns)).T[:8]
    g_bqkv = g_qkv[width : width + 1]
    blank = jnp.zeros((1, 2 * width), f32)
    grads = jnp.concatenate(
        [
            g_up[:width],
            g_down[:width],
            g_up[width : width + 1],
            pair(g_bias[:1, :width], g_bqkv[:, :width]),
            g_bqkv[:, width:],
        ]
        + [blank] * 5
        + [
            g_qkv[:width, : 2 * width],
            pair(g_qkv[:width, 2 * width :], g_wo),
            pair(g_bias[:1, width:], norms[0:1]),
            pair(norms[1:2], blank[:, :width]),
        ]
        + [blank] * 6,
        0,
    )
    later = (d_mark_t, d_normed_tok, d_hidden, xhat1, scale1, layer_out)
    return later, grads


def row_end(later, idx, par):
    gain1, wq, wk = par
    d_mark_t, d_normed_tok, d_hidden, xhat1, scale1, layer_out = later
    width, tokens = xhat1.shape
    heads, marks = idx.shape
    hm = heads * marks
    idx_row = jnp.concatenate([idx[h : h + 1] for h in range(heads)], 1)
    idx_col = jnp.broadcast_to(idx_row.astype(f32), (8, hm)).T[:, :1].astype(jnp.int32)
    tok_lane = iota((hm, tokens), 1)
    pick_m = jnp.concatenate([tok_lane == idx_col, tok_lane + tokens == idx_col], 0)
    pick_m = pick_m.astype(f32).astype(bf16)
    onto = mm(jnp.concatenate([wq, wk], 0), d_mark_t).astype(bf16)
    moved = mm(pair(onto[:width], onto[width:]), pick_m)
    d_normed = d_normed_tok + (width // heads) ** -0.5 * moved
    grad_in = d_hidden + norm_back(d_normed, xhat1, scale1, gain1)
    lane = iota((width, 128), 1)
    sums = jnp.where(lane == 0, row_sum(d_normed * xhat1), 0.0) + jnp.where(
        lane == 1, row_sum(d_normed), 0.0
    )
    sums = sums.T
    return jnp.concatenate([layer_out, grad_in], 0).T.astype(bf16), pair(sums[:1], sums[1:2])


MATRICES = (2, 4, 6, 8, 12, 14)
VECTORS = (0, 1, 3, 5, 7, 9, 10, 11, 13, 15)


def read_params(mats, vec_cols):
    par = [None] * 16
    for i, ref in zip(MATRICES, mats):
        par[i] = ref[...]
    for row, i in enumerate(VECTORS):
        wide = par[12].shape[1] if i == 13 else par[2].shape[0]
        par[i] = vec_cols[:wide, row : row + 1]
    return tuple(par)


def own_row(idx_ref):
    return idx_ref[jnp.clip(lax.axis_index("tok") - FIRST, 0, idx_ref.shape[0] - 1)]


def for_owners(idx_ref, work, zeroed):
    row = lax.axis_index("tok") - FIRST
    has_row = (row >= 0) & (row < idx_ref.shape[0])
    pl.when(has_row)(work)

    @pl.when(jnp.logical_not(has_row))
    def _():
        for ref in zeroed:
            ref[...] = jnp.zeros(ref.shape, ref.dtype)


def main_kernel(tok_block, blk_ref, idx_ref, vec_ref, *refs):
    mats, later_refs, (keep_ref, send_ref) = refs[:6], refs[6:-2], refs[-2:]

    def work():
        blocks = blk_ref.shape[0]
        tokens = blocks * tok_block
        xg = blk_ref[:, :tok_block, :].reshape(tokens, 128)
        ids = blk_ref[:, tok_block:, :].astype(f32)
        half = iota((SEG_ROWS, 128), 1) < tok_block
        onehot_t = jnp.concatenate(
            [jnp.where(half, ids[2 * j], ids[2 * j + 1]) for j in range(blocks // 2)], 1
        ).astype(bf16)
        later, grads = row_work(xg, onehot_t, own_row(idx_ref), read_params(mats, vec_ref[...].T))
        for ref, value in zip(later_refs, later):
            ref[...] = value
        first = lax.rem(lax.axis_index("rows"), 2) == 0
        h = GRAD_ROWS // 2
        keep_ref[...] = jnp.where(first, grads[:h], grads[h:])
        send_ref[...] = jnp.where(first, grads[h:], grads[:h])

    for_owners(idx_ref, work, (keep_ref, send_ref))


def end_kernel(idx_ref, vec_ref, wq_ref, wk_ref, *refs):
    later_refs, out_ref, norm_ref = refs[:-2], refs[-2], refs[-1]

    def work():
        later = [ref[...] for ref in later_refs]
        gain1 = vec_ref[...].T[: wq_ref.shape[0], :1]
        out, sums = row_end(later, own_row(idx_ref), (gain1, wq_ref[...], wk_ref[...]))
        out_ref[...] = out.reshape(out_ref.shape)
        norm_ref[...] = jnp.where(iota(norm_ref.shape, 0) == NORM_ROW, sums, 0.0)

    for_owners(idx_ref, work, (out_ref, norm_ref))


def pack_kernel(xg_ref, s_ref, *refs):
    vecs, (out_ref, vec_ref) = refs[:-2], refs[-2:]
    rows, tok, width = xg_ref.shape
    out_ref[:FIRST] = jnp.zeros((FIRST,) + out_ref.shape[1:], bf16)
    out_ref[FIRST : rows + FIRST, :tok, :] = xg_ref[...]
    unused = out_ref.shape[0] - rows - FIRST
    if unused:
        out_ref[rows + FIRST :] = jnp.zeros((unused,) + out_ref.shape[1:], bf16)
    seg = s_ref[...]
    seg = jnp.concatenate([seg, seg], 1)
    for r in range(rows):
        ids = jnp.broadcast_to(seg[r : r + 1], (SEG_ROWS, width))
        out_ref[FIRST + r, tok:, :] = (ids == iota((SEG_ROWS, width), 0)).astype(f32).astype(bf16)
    for i, ref in enumerate(vecs):
        vec_ref[i : i + 1, : ref.shape[0]] = ref[...].astype(f32).reshape(1, -1)


def sum_kernel(tok, got_ref, sum_ref):
    total = got_ref[0, tok:, :].astype(f32)
    for j in range(1, got_ref.shape[0]):
        total = total + got_ref[j, tok:, :].astype(f32)
    sum_ref[...] = total.astype(bf16)


def rows_kernel(got_ref, out_ref, grad_ref):
    rows, tok, width = out_ref.shape
    out_ref[...] = got_ref[FIRST : rows + FIRST, :tok, :width]
    grad_ref[...] = got_ref[FIRST : rows + FIRST, :tok, width:].astype(f32)


def unpack_kernel(n_parts, *refs):
    parts, outs = refs[:n_parts], refs[n_parts:]
    parts = [p[...].astype(f32) for p in parts]
    halves = [sum(parts[core + 2 :: 2], parts[core]) for core in range(2)]
    norms = halves[0][NORM_ROW] + halves[1][NORM_ROW]
    first = lax.rem(lax.axis_index("rows"), 2) == 0
    a = jnp.where(first, halves[0], halves[1])
    b = jnp.where(first, halves[1], halves[0])
    whole = jnp.concatenate([a, b], 0)
    (gain1, bias1, wq, bq, wk, bk, wv, bv, wo, bo, gain2, bias2, wup, bup, wdown_t, bdown) = outs
    wup[...] = whole[0:64]
    wdown_t[...] = whole[64:128]
    bup[...] = whole[128]
    bdown[...] = whole[129, :64]
    bq[...] = whole[129, 64:]
    bk[...] = whole[130, :64]
    bv[...] = whole[130, 64:]
    wq[...] = whole[136:200, :64]
    wk[...] = whole[136:200, 64:]
    wv[...] = whole[200:264, :64]
    wo[...] = whole[200:264, 64:]
    bo[...] = whole[264, :64]
    gain2[...] = whole[264, 64:]
    bias2[...] = whole[265, :64]
    gain1[...] = norms[:64]
    bias1[...] = norms[64:]


def call(kernel, outs, *args, mib=12):
    vmem = pl.BlockSpec(memory_space=pltpu.VMEM)
    return pl.pallas_call(
        kernel,
        out_shape=outs,
        in_specs=[vmem] * len(args),
        out_specs=jax.tree.map(lambda _: vmem, outs),
        compiler_params=pltpu.CompilerParams(vmem_limit_bytes=mib * 1024 * 1024),
    )(*args)


def shards(tokens_in, segments, landmark_index, *rest):
    params, grad_out = rest[:14] + (rest[14].T, rest[15]), rest[16]
    rows, tok, width = tokens_in.shape
    n_tok = lax.axis_size("tok")
    n_rows = lax.axis_size("rows")
    sds = jax.ShapeDtypeStruct
    sent, vecs = call(
        pack_kernel,
        (sds((n_tok, tok + SEG_ROWS, 128), bf16), sds((16, 128), f32)),
        jnp.concatenate([tokens_in, grad_out], 2),
        segments,
        *[params[i] for i in VECTORS],
        mib=4,
    )
    got = lax.all_to_all(sent, "tok", 0, 0, tiled=True)
    h = GRAD_ROWS // 2
    tokens = n_tok * tok
    mib = 12 * max(1, tokens // 512)
    by_token = sds((width, tokens), f32)
    marks = landmark_index.shape[1] * landmark_index.shape[2]
    *later, keep, send = call(
        partial(main_kernel, tok),
        (sds((width, marks), bf16),)
        + (by_token,) * 3
        + (sds((1, tokens), f32), by_token)
        + (sds((h, 128), f32),) * 2,
        got,
        landmark_index,
        vecs,
        *[params[i] for i in MATRICES],
        mib=mib,
    )
    send = lax.ppermute(send, "rows", [(i, i ^ 1) for i in range(n_rows)])
    out, norms = call(
        end_kernel,
        (sds((n_tok, tok, 128), bf16), sds((h, 128), f32)),
        landmark_index,
        vecs,
        params[2],
        params[4],
        *later,
        mib=mib,
    )
    def from_xor(array, m):
        return lax.ppermute(array, "rows", [(i, i ^ m) for i in range(n_rows)])

    total = (keep + send + norms).astype(bf16)
    back = jnp.concatenate([out, jnp.broadcast_to(total, (n_tok, h, 128))], 1)
    got = lax.all_to_all(back, "tok", 0, 0, tiled=True)
    mine = call(partial(sum_kernel, tok), sds((h, 128), bf16), got)
    parts = [mine] + [from_xor(mine, m) for m in range(1, n_rows)]
    layer_out, grad_input = call(
        rows_kernel, (sds((rows, tok, width), bf16), sds((rows, tok, width), f32)), got
    )
    sums = call(
        partial(unpack_kernel, n_rows), tuple(sds(p.shape, f32) for p in params), *parts
    )
    sums = sums[:14] + (sums[14].T,) + sums[15:]
    return (layer_out, grad_input) + tuple(sums)


def solution(mesh):
    split3 = P("rows", "tok", None)
    return jax.shard_map(
        shards,
        mesh=mesh,
        in_specs=(split3, P("rows", "tok"), P("rows", None, None)) + (P(),) * 16 + (split3,),
        out_specs=(split3, split3) + (P(),) * 16,
        check_vma=False,
    )
```

```python
from functools import partial

import jax
import jax.numpy as jnp
from jax import lax
from jax.experimental import pallas as pl
from jax.experimental.pallas import tpu as pltpu
from jax.sharding import PartitionSpec as P


NS_STEPS = 6
EPS = 1e-05
RIDGE = 0.1
FAR = 640.0
SEG_ROWS = 8
FIRST = 1
GRAD_ROWS = 272
NORM_ROW = 131

LOG2_E = 1.4426950408889634

f32 = jnp.float32
bf16 = jnp.bfloat16


def mm(a, b):
    return lax.dot_general(a, b, (((1,), (0,)), ((), ())), preferred_element_type=f32)


def mm_nt(a, b):
    return lax.dot_general(a, b, (((1,), (1,)), ((), ())), preferred_element_type=f32)


def mm_tn(a, b):
    return lax.dot_general(a, b, (((0,), (0,)), ((), ())), preferred_element_type=f32)


def split(a):
    hi = a.astype(bf16)
    return hi, (a - hi.astype(f32)).astype(bf16)


def wide_right(b):
    hi, lo = split(b)
    return jnp.concatenate(
        [jnp.concatenate([hi, lo], 1), jnp.concatenate([hi, jnp.zeros_like(hi)], 1)], 0
    )


def mm_wide(a, wide):
    n = wide.shape[1] // 2
    both = mm(jnp.concatenate(split(a), 1), wide)
    return both[:, :n] + both[:, n:]


def row_sum(a):
    return jnp.sum(a, axis=1, keepdims=True)


def col_sum(a):
    return jnp.sum(a, axis=0, keepdims=True)


def total_of(a):
    return col_sum(row_sum(a))


def both_parts(product, a, b):
    n = b.shape[1]
    both = product(a, jnp.concatenate(split(b), 1))
    return both[:, :n] + both[:, n:]


def pair(a, b):
    return jnp.concatenate([a, b], 1)


def wide_mm(a_pair, wide):
    n = wide.shape[1] // 2
    both = mm(a_pair, wide)
    return both[:, :n] + both[:, n:]


def both_parts_left(a, wide):
    n = wide.shape[1] // 2
    return wide_mm(a, wide[:n])


def norm_stats(values):
    n = 1.0 / values.shape[0]
    centre = values - col_sum(values) * n
    scale = lax.rsqrt(col_sum(centre * centre) * n + EPS)
    return centre * scale, scale


def norm_back(d_norm, xhat, scale, gain):
    scaled = d_norm * gain
    n = 1.0 / scaled.shape[0]
    return scale * (scaled - col_sum(scaled) * n - xhat * (col_sum(scaled * xhat) * n))


def iota(shape, dim):
    return lax.broadcasted_iota(jnp.int32, shape, dim)


def row_work(xg, onehot_t, idx, par):
    (gain1, bias1, wq, bq, wk, bk, wv, bv, wo, bo, gain2, bias2, wup, bup, wdown_t, bdown) = par
    tokens = xg.shape[0]
    width = wq.shape[0]
    heads, marks = idx.shape
    size = width // heads
    sharp = size**-0.5
    sharp2 = sharp * LOG2_E
    out_scale = tokens**-0.5
    hm = heads * marks
    hs = range(heads)
    at = [slice(h * marks, (h + 1) * marks) for h in hs]
    rows_of = [slice(h * size, (h + 1) * size) for h in hs]
    chunk = tokens // 4
    chunks = [slice(lo, lo + chunk) for lo in range(0, tokens, chunk)]

    xg_t = xg.astype(f32).T
    x_t, g_t = xg_t[:width], xg_t[width:]
    g16_t = g_t.astype(bf16)
    wqkv = jnp.concatenate([wq, wk, wv], 1)
    wqkv_t = wqkv.astype(f32).T.astype(bf16)
    xhat1, scale1 = norm_stats(x_t)
    normed_t = (xhat1 * gain1 + bias1).astype(bf16)
    qkv_t = mm(wqkv_t, normed_t) + jnp.concatenate([bq, bk, bv], 0)
    qkv16_t = qkv_t.astype(bf16)
    q_t, k_t, v_t = (qkv16_t[i * width : (i + 1) * width] for i in range(3))
    seg_rows = jnp.where(
        (iota(onehot_t.shape, 0) >= 4) & (iota(onehot_t.shape, 0) < 8), 1.0, onehot_t.astype(f32)
    )
    seg_rows = jnp.concatenate(
        [seg_rows, jnp.zeros((width - SEG_ROWS, tokens), f32)], 0
    ).astype(bf16)

    def features(p_t):
        p = p_t.astype(f32)
        sq = p * p
        hi = sq.astype(bf16)
        return jnp.concatenate([p_t, seg_rows, hi, (sq - hi.astype(f32)).astype(bf16)], 0)

    feats_q, feats_k = features(q_t), features(k_t)

    idx_row = jnp.concatenate([idx[h : h + 1] for h in hs], 1)
    pick_t = (iota((2 * tokens, hm), 0) == idx_row).astype(f32).astype(bf16)
    qk_t = jnp.concatenate([q_t, k_t], 1)
    ones16 = jnp.ones((16, tokens), bf16)
    normed_ones = jnp.concatenate([normed_t, ones16], 0)
    seg2 = jnp.concatenate([onehot_t, onehot_t], 1)
    picked = mm(jnp.concatenate([qk_t, seg2], 0), pick_t)
    own = ((iota((width, hm), 0) // size) == (iota((width, hm), 1) // marks)).astype(f32)
    mark_t = picked[:width] * own
    mark_seg = picked[width : width + 8]
    sq = mark_t * mark_t
    half = -0.5 * col_sum(sq)
    half_hi = half.astype(bf16).astype(f32)
    half_mid = (half - half_hi).astype(bf16).astype(f32)
    half_lo = half - half_hi - half_mid
    row8 = iota((8, hm), 0)
    extra = jnp.where(row8 < 4, mark_seg * FAR, 0.0)
    extra = jnp.where(row8 == 4, half_hi, extra)
    extra = jnp.where(row8 == 5, half_mid, extra)
    extra = jnp.where(row8 == 6, half_lo, extra)
    extra = jnp.where(row8 == 7, -FAR, extra)
    pad = jnp.zeros((width - 8, hm), f32)
    squares = iota((hm, 2 * width), 1) % width // size == iota((hm, 2 * width), 0) // marks
    right_m = pair(
        jnp.concatenate([mark_t, extra, pad], 0).T.astype(bf16),
        jnp.where(squares, -0.5, 0.0).astype(bf16),
    )
    sq_hi = sq.astype(bf16).astype(f32)
    left = jnp.concatenate(
        [mark_t, jnp.where(row8 < 4, mark_seg, 1.0), pad, sq_hi, sq - sq_hi], 0
    ).astype(bf16)
    mark16 = mark_t.astype(bf16)

    def near_of(points):
        return jnp.exp2(sharp2 * mm(right_m, points)).astype(bf16)

    eye = (iota((marks, marks), 0) == iota((marks, marks), 1)).astype(f32)
    kernel = [jnp.exp2(sharp2 * mm(right_m[at[h]], left[:, at[h]])) for h in hs]
    gram = [kernel[h] + RIDGE * eye for h in hs]
    sums = [col_sum(gram[h]) for h in hs]
    widest = [jnp.max(sums[h], axis=1, keepdims=True) for h in hs]
    inv2 = [1.0 / (widest[h] * widest[h]) for h in hs]
    gram_wide = [wide_right(gram[h]) for h in hs]
    wo_of = [wo[rows_of[h]] for h in hs]
    rest = [eye - mm_wide(gram[h] * inv2[h], gram_wide[h]) for h in hs]
    v_tok = v_t.astype(f32).T.astype(bf16)
    rests, wides = [rest], []
    near_k, near_q, near_q_tok, summed_t, sent_t, grown = [], [], [], [], [], []

    def add_near_k(i):
        half = tokens // 2
        near_k.append(near_of(feats_k[:, i * half : (i + 1) * half]))

    def add_near_q(i):
        near_q.append(near_of(feats_q[:, chunks[i]]))
        near_q_tok.append(near_q[-1].T)

    def add_sums():
        near_k[:] = [jnp.concatenate(near_k, 1)]
        both = mm(near_k[0], v_tok).T
        summed_t.extend(both[rows_of[h], at[h]] for h in hs)

    def add_sent():
        sent_t.extend(both_parts(mm_tn, wo_of[h], summed_t[h]) for h in hs)
        grown.append([mm_wide(sent_t[h], gram_wide[h]) * inv2[h] for h in hs])

    def two_steps(step):
        nxt = rests[step + 1]
        return [rests[step][h] + nxt[h] + mm_wide(rests[step][h], wides[step + 1][h]) for h in hs]

    def grown_by(now, wide):
        return [now[h] + mm_wide(now[h], wide[h]) for h in hs]

    def widen(both):
        return [wide_right(both[h]) for h in hs]

    def next_rest():
        wides.append(widen(rests[-1]))
        if len(rests) < NS_STEPS:
            rests.append([mm_wide(rests[-1][h], wides[-1][h]) for h in hs])

    add_near_k(0)
    next_rest()
    add_near_k(1)
    next_rest()
    twice = [widen(two_steps(0))]
    add_sums()
    next_rest()
    add_near_q(0)
    add_sent()
    next_rest()
    twice.append(widen(two_steps(2)))
    add_near_q(1)
    grown.extend([None] * NS_STEPS)
    grown[2] = grown_by(grown[0], twice[0])
    next_rest()
    add_near_q(2)
    grown[4] = grown_by(grown[2], twice[1])
    next_rest()
    grown[5] = grown_by(grown[4], wides[4])
    add_near_q(3)
    grown[6] = grown_by(grown[5], wides[5])
    near_k, now = near_k[0], grown[-1]
    near_q = jnp.concatenate(near_q, 1)
    near_q_tok = jnp.concatenate(near_q_tok, 0)
    mixed_t = jnp.concatenate(now, 1).astype(bf16)
    hidden = x_t + (mm(mixed_t, near_q) * out_scale + bo)
    twice.append(widen(two_steps(4)))
    inverse = [gram[h] * inv2[h] for h in hs]
    for wide in twice:
        inverse = grown_by(inverse, wide)
    inverse_wide = widen(inverse)
    grown[1] = grown_by(grown[0], wides[0])
    grown[3] = grown_by(grown[2], wides[2])
    beside_rest = [
        [pair(rests[step][h], grown[step][h].T).astype(bf16) for h in hs]
        for step in range(NS_STEPS)
    ]
    normed_mark = pair(mm(normed_ones, pick_t[:tokens]), mm(normed_ones, pick_t[tokens:])).astype(bf16)
    wup_t = wup.astype(f32).T.astype(bf16)
    d_act = mm_tn(wdown_t, g16_t)
    xhat2, scale2 = norm_stats(hidden)
    normed2_t = (xhat2 * gain2 + bias2).astype(bf16)
    inner = mm(wup_t, normed2_t) + bup
    c = (2.0 / jnp.pi) ** 0.5
    inner2 = inner * inner
    th = jnp.tanh(c * inner * (1.0 + 0.044715 * inner2))
    act = (0.5 * inner * (1.0 + th)).astype(bf16)

    slope = 0.5 * (1.0 + th) + 0.5 * inner * (1.0 - th * th) * (
        c * (1.0 + (3.0 * 0.044715) * inner2)
    )
    d_inner = (d_act * slope).astype(bf16)
    d_norm2 = mm(wup, d_inner)
    layer_out = hidden + (mm(wdown_t, act) + bdown)
    d_hidden = g_t + norm_back(d_norm2, xhat2, scale2, gain2)
    d_branch = d_hidden.astype(bf16)
    d_sent_t = mm(d_branch, near_q_tok) * out_scale
    back = [d_sent_t[:, at[h]] for h in hs]

    mark_both = jnp.concatenate([mark16, own.astype(bf16)], 0)
    mixed = [mm_wide(summed_t[h], inverse_wide[h]) for h in hs]
    blank_h = jnp.zeros((size, marks), f32)
    mixed_m = jnp.concatenate(
        [jnp.concatenate([mixed[h] if g == h else blank_h for g in hs], 1) for h in hs], 0
    ).T.astype(bf16)
    d_att = mm(wo, d_branch).astype(bf16)
    q_tok = q_t.astype(f32).T.astype(bf16)
    k_tok = k_t.astype(f32).T.astype(bf16)
    ones_tok = jnp.ones((tokens, width), bf16)
    def stays(pull, p_t):
        both = mm(mark_both, pull)
        return sharp * (both[:width] - both[width:] * p_t.astype(f32))

    pulls_q, toks = [], []

    def pull_some(i):
        now_at = chunks[i]
        pull = (mm(mixed_m, d_att[:, now_at]) * out_scale).astype(bf16)
        pulls_q.append((pull.astype(f32) * near_q[:, now_at].astype(f32)).astype(bf16))

    def pull_rest():
        pull = mm(early["d_summed_m"], v_t).astype(bf16)
        pulls_q.append((pull.astype(f32) * near_k.astype(f32)).astype(bf16))

    def add_tok(pull, tok):
        toks.append(mm(pull, pair(tok, ones_tok)))

    def add_tok_q():
        pulls_q[:4] = [jnp.concatenate(pulls_q[:4], 1)]
        add_tok(pulls_q[0], q_tok)

    def add_tok_k():
        add_tok(pulls_q[1], k_tok)

    early = {}
    first_back = back

    def add_end():
        beside_gram = [pair(sent_t[h].T, -gram[h]).astype(bf16) for h in hs]
        kernel_inv = [kernel[h] * inv2[h] for h in hs]
        widest_a = [(2.0 / widest[h]) * (eye - rests[0][h]) for h in hs]
        widest_b = [(2.0 / widest[h]) * grown[0][h] for h in hs]
        mark_ones = [
            jnp.concatenate([mark16[:, at[h]], jnp.ones((16, marks), bf16)], 0) for h in hs
        ]
        top_part = []
        for h in hs:
            top = (sums[h] == widest[h]).astype(f32)
            top = top * (1.0 / row_sum(top))
            seen = kernel[h].astype(bf16)
            along = jnp.broadcast_to(top, (16, marks)).astype(bf16)
            top_part.append(
                top * mm(mark_ones[h], seen)
                + mm_nt(mark_ones[h], along)[:, :1] * mm(along, seen)[:1]
            )
        early.update(
            beside_gram=beside_gram,
            kernel_inv=kernel_inv,
            widest_a=widest_a,
            widest_b=widest_b,
            mark_ones=mark_ones,
            top_part=top_part,
        )

    def add_summed():
        d_start = [mm_wide(first_back[h], inverse_wide[h]) for h in hs]
        d_att_early = mm(wo, d_branch).astype(bf16)
        d_mixed = mm(d_att_early, near_q_tok) * out_scale
        d_mixed = [d_mixed[rows_of[h], at[h]].astype(bf16) for h in hs]
        d_summed = [both_parts_left(d_mixed[h], inverse_wide[h]) for h in hs]
        none = jnp.zeros((size, marks), f32)
        d_summed_t = jnp.concatenate(
            [jnp.concatenate([d_summed[h] if g == h else none for g in hs], 1) for h in hs], 0
        )
        d_summed_m = d_summed_t.T.astype(bf16)
        early.update(
            d_start=d_start,
            d_summed_t=d_summed_t,
            d_summed_m=d_summed_m,
        )


    def add_down():
        early["down"] = mm_nt(g16_t, act)

    def add_up():
        early["up"] = mm_nt(jnp.concatenate([normed2_t, ones16], 0), d_inner)

    def add_bias():
        early["bias"] = mm_nt(ones16, jnp.concatenate([g16_t, d_branch], 0))

    def add_wo():
        early["wo"] = jnp.concatenate(
            [mm_nt(summed_t[h].astype(bf16), early["d_start"][h].astype(bf16)) for h in hs], 0
        )

    def add_stay():
        stay_q, stay_k = stays(pulls_q[0], q_t), stays(pulls_q[1], k_t)
        dv = mm(early["d_summed_t"].astype(bf16), near_k)
        early["stay"] = jnp.concatenate([stay_q, stay_k, dv], 0).astype(bf16)

    def add_qkv():
        early["qkv"] = mm_nt(normed_ones, early["stay"])

    def add_normed():
        early["normed"] = mm(wqkv, early["stay"])

    beside = [
        [add_summed, partial(pull_some, 0), partial(pull_some, 1)],
        [partial(pull_some, 2), partial(pull_some, 3), pull_rest],
        [add_tok_q, add_tok_k],
        [add_stay],
        [add_up, add_down, add_end],
        [add_qkv, add_normed, add_bias, add_wo],
    ]
    b16 = [back[h].astype(bf16) for h in hs]
    last = NS_STEPS - 1
    d_rest = [mm(beside_rest[last][h][:, marks:], b16[h]) for h in hs]
    back = [back[h] + wide_mm(b16[h], wides[last][h][:marks]) for h in hs]
    for step in reversed(range(NS_STEPS)):
        if step < last:
            both16 = [
                jnp.concatenate([d_rest[h].astype(bf16), back[h].astype(bf16)], 0) for h in hs
            ]
            turned = [
                mm_wide(jnp.concatenate([d_rest[h], back[h]], 0), wides[step][h]) for h in hs
            ]
            back = [back[h] + turned[h][marks:] for h in hs]
            d_rest = [turned[h][:marks] + mm(beside_rest[step][h], both16[h]) for h in hs]
        for work in beside[last - step]:
            work()
    d16 = [d_rest[h].astype(bf16) for h in hs]
    d_gram = [
        mm(early["beside_gram"][h], jnp.concatenate([back[h].astype(bf16), d16[h]], 0))
        - wide_mm(d16[h], gram_wide[h][:marks])
        for h in hs
    ]
    tok_both = (toks[0] + toks[1]).T
    tok_t, tok_sum = tok_both[:width], tok_both[width : width + 1]
    stay, d_normed_tok = early["stay"], early["normed"]
    gram_part = []
    for h in hs:
        d_widest = total_of(d_rest[h] * early["widest_a"][h]) - total_of(back[h] * early["widest_b"][h])
        weighted = ((d_gram[h] + d_gram[h].T) * early["kernel_inv"][h]).astype(bf16)
        gram_part.append(mm(early["mark_ones"][h], weighted) + d_widest * early["top_part"][h])
    gram_part = jnp.concatenate(gram_part, 1)
    d_mark_t = (
        (tok_t + gram_part[:width] - mark_t * (tok_sum + gram_part[width : width + 1])) * own
    ).astype(bf16)
    g_bias, g_wo = early["bias"], early["wo"]
    g_down, g_up = early["down"], early["up"]
    by_mark = sharp * pair(
        mm_nt(normed_mark[:, :hm], d_mark_t), mm_nt(normed_mark[:, hm:], d_mark_t)
    )
    g_qkv = early["qkv"] + pair(by_mark, jnp.zeros((width + 16, width), f32))
    columns = [
        row_sum(d_norm2 * xhat2),
        row_sum(d_norm2),
    ]
    lane = iota((width, 128), 1)
    norms = sum(jnp.where(lane == i, col, 0.0) for i, col in enumerate(columns)).T[:8]
    g_bqkv = g_qkv[width : width + 1]
    blank = jnp.zeros((1, 2 * width), f32)
    grads = jnp.concatenate(
        [
            g_up[:width],
            g_down[:width],
            g_up[width : width + 1],
            pair(g_bias[:1, :width], g_bqkv[:, :width]),
            g_bqkv[:, width:],
        ]
        + [blank] * 5
        + [
            g_qkv[:width, : 2 * width],
            pair(g_qkv[:width, 2 * width :], g_wo),
            pair(g_bias[:1, width:], norms[0:1]),
            pair(norms[1:2], blank[:, :width]),
        ]
        + [blank] * 6,
        0,
    )
    later = (d_mark_t, d_normed_tok, d_hidden, xhat1, scale1, layer_out)
    return later, grads


def row_end(later, idx, par):
    gain1, wq, wk = par
    d_mark_t, d_normed_tok, d_hidden, xhat1, scale1, layer_out = later
    width, tokens = xhat1.shape
    heads, marks = idx.shape
    hm = heads * marks
    idx_row = jnp.concatenate([idx[h : h + 1] for h in range(heads)], 1)
    idx_col = jnp.broadcast_to(idx_row.astype(f32), (8, hm)).T[:, :1].astype(jnp.int32)
    tok_lane = iota((hm, tokens), 1)
    pick_m = jnp.concatenate([tok_lane == idx_col, tok_lane + tokens == idx_col], 0)
    pick_m = pick_m.astype(f32).astype(bf16)
    onto = mm(jnp.concatenate([wq, wk], 0), d_mark_t).astype(bf16)
    moved = mm(pair(onto[:width], onto[width:]), pick_m)
    d_normed = d_normed_tok + (width // heads) ** -0.5 * moved
    grad_in = d_hidden + norm_back(d_normed, xhat1, scale1, gain1)
    lane = iota((width, 128), 1)
    sums = jnp.where(lane == 0, row_sum(d_normed * xhat1), 0.0) + jnp.where(
        lane == 1, row_sum(d_normed), 0.0
    )
    sums = sums.T
    return jnp.concatenate([layer_out, grad_in], 0).T.astype(bf16), pair(sums[:1], sums[1:2])


MATRICES = (2, 4, 6, 8, 12, 14)
VECTORS = (0, 1, 3, 5, 7, 9, 10, 11, 13, 15)


def read_params(mats, vec_cols):
    par = [None] * 16
    for i, ref in zip(MATRICES, mats):
        par[i] = ref[...]
    for row, i in enumerate(VECTORS):
        wide = par[12].shape[1] if i == 13 else par[2].shape[0]
        par[i] = vec_cols[:wide, row : row + 1]
    return tuple(par)


def own_row(idx_ref):
    return idx_ref[jnp.clip(lax.axis_index("tok") - FIRST, 0, idx_ref.shape[0] - 1)]


def for_owners(idx_ref, work, zeroed):
    row = lax.axis_index("tok") - FIRST
    has_row = (row >= 0) & (row < idx_ref.shape[0])
    pl.when(has_row)(work)

    @pl.when(jnp.logical_not(has_row))
    def _():
        for ref in zeroed:
            ref[...] = jnp.zeros(ref.shape, ref.dtype)


def main_kernel(tok_block, blk_ref, idx_ref, vec_ref, *refs):
    mats, later_refs, (keep_ref, send_ref) = refs[:6], refs[6:-2], refs[-2:]

    def work():
        blocks = blk_ref.shape[0]
        tokens = blocks * tok_block
        xg = blk_ref[:, :tok_block, :].reshape(tokens, 128)
        ids = blk_ref[:, tok_block:, :].astype(f32)
        half = iota((SEG_ROWS, 128), 1) < tok_block
        onehot_t = jnp.concatenate(
            [jnp.where(half, ids[2 * j], ids[2 * j + 1]) for j in range(blocks // 2)], 1
        ).astype(bf16)
        later, grads = row_work(xg, onehot_t, own_row(idx_ref), read_params(mats, vec_ref[...].T))
        for ref, value in zip(later_refs, later):
            ref[...] = value
        first = lax.rem(lax.axis_index("rows"), 2) == 0
        h = GRAD_ROWS // 2
        keep_ref[...] = jnp.where(first, grads[:h], grads[h:])
        send_ref[...] = jnp.where(first, grads[h:], grads[:h])

    for_owners(idx_ref, work, (keep_ref, send_ref))


def end_kernel(idx_ref, vec_ref, wq_ref, wk_ref, *refs):
    later_refs, out_ref, norm_ref = refs[:-2], refs[-2], refs[-1]

    def work():
        later = [ref[...] for ref in later_refs]
        gain1 = vec_ref[...].T[: wq_ref.shape[0], :1]
        out, sums = row_end(later, own_row(idx_ref), (gain1, wq_ref[...], wk_ref[...]))
        out_ref[...] = out.reshape(out_ref.shape)
        norm_ref[...] = jnp.where(iota(norm_ref.shape, 0) == NORM_ROW, sums, 0.0)

    for_owners(idx_ref, work, (out_ref, norm_ref))


def pack_kernel(xg_ref, s_ref, *refs):
    vecs, (out_ref, vec_ref) = refs[:-2], refs[-2:]
    rows, tok, width = xg_ref.shape
    out_ref[:FIRST] = jnp.zeros((FIRST,) + out_ref.shape[1:], bf16)
    out_ref[FIRST : rows + FIRST, :tok, :] = xg_ref[...]
    unused = out_ref.shape[0] - rows - FIRST
    if unused:
        out_ref[rows + FIRST :] = jnp.zeros((unused,) + out_ref.shape[1:], bf16)
    seg = s_ref[...]
    seg = jnp.concatenate([seg, seg], 1)
    for r in range(rows):
        ids = jnp.broadcast_to(seg[r : r + 1], (SEG_ROWS, width))
        out_ref[FIRST + r, tok:, :] = (ids == iota((SEG_ROWS, width), 0)).astype(f32).astype(bf16)
    for i, ref in enumerate(vecs):
        vec_ref[i : i + 1, : ref.shape[0]] = ref[...].astype(f32).reshape(1, -1)


def sum_kernel(tok, got_ref, sum_ref):
    total = got_ref[0, tok:, :].astype(f32)
    for j in range(1, got_ref.shape[0]):
        total = total + got_ref[j, tok:, :].astype(f32)
    sum_ref[...] = total.astype(bf16)


def rows_kernel(got_ref, out_ref, grad_ref):
    rows, tok, width = out_ref.shape
    out_ref[...] = got_ref[FIRST : rows + FIRST, :tok, :width]
    grad_ref[...] = got_ref[FIRST : rows + FIRST, :tok, width:].astype(f32)


def unpack_kernel(n_parts, *refs):
    parts, outs = refs[:n_parts], refs[n_parts:]
    parts = [p[...].astype(f32) for p in parts]
    halves = [sum(parts[core + 2 :: 2], parts[core]) for core in range(2)]
    norms = halves[0][NORM_ROW] + halves[1][NORM_ROW]
    first = lax.rem(lax.axis_index("rows"), 2) == 0
    a = jnp.where(first, halves[0], halves[1])
    b = jnp.where(first, halves[1], halves[0])
    whole = jnp.concatenate([a, b], 0)
    (gain1, bias1, wq, bq, wk, bk, wv, bv, wo, bo, gain2, bias2, wup, bup, wdown_t, bdown) = outs
    wup[...] = whole[0:64]
    wdown_t[...] = whole[64:128]
    bup[...] = whole[128]
    bdown[...] = whole[129, :64]
    bq[...] = whole[129, 64:]
    bk[...] = whole[130, :64]
    bv[...] = whole[130, 64:]
    wq[...] = whole[136:200, :64]
    wk[...] = whole[136:200, 64:]
    wv[...] = whole[200:264, :64]
    wo[...] = whole[200:264, 64:]
    bo[...] = whole[264, :64]
    gain2[...] = whole[264, 64:]
    bias2[...] = whole[265, :64]
    gain1[...] = norms[:64]
    bias1[...] = norms[64:]


def call(kernel, outs, *args, mib=12):
    vmem = pl.BlockSpec(memory_space=pltpu.VMEM)
    return pl.pallas_call(
        kernel,
        out_shape=outs,
        in_specs=[vmem] * len(args),
        out_specs=jax.tree.map(lambda _: vmem, outs),
        compiler_params=pltpu.CompilerParams(vmem_limit_bytes=mib * 1024 * 1024),
    )(*args)


def shards(tokens_in, segments, landmark_index, *rest):
    params, grad_out = rest[:14] + (rest[14].T, rest[15]), rest[16]
    rows, tok, width = tokens_in.shape
    n_tok = lax.axis_size("tok")
    n_rows = lax.axis_size("rows")
    sds = jax.ShapeDtypeStruct
    sent, vecs = call(
        pack_kernel,
        (sds((n_tok, tok + SEG_ROWS, 128), bf16), sds((16, 128), f32)),
        jnp.concatenate([tokens_in, grad_out], 2),
        segments,
        *[params[i] for i in VECTORS],
        mib=4,
    )
    got = lax.all_to_all(sent, "tok", 0, 0, tiled=True)
    h = GRAD_ROWS // 2
    tokens = n_tok * tok
    mib = 12 * max(1, tokens // 512)
    by_token = sds((width, tokens), f32)
    marks = landmark_index.shape[1] * landmark_index.shape[2]
    *later, keep, send = call(
        partial(main_kernel, tok),
        (sds((width, marks), bf16),)
        + (by_token,) * 3
        + (sds((1, tokens), f32), by_token)
        + (sds((h, 128), f32),) * 2,
        got,
        landmark_index,
        vecs,
        *[params[i] for i in MATRICES],
        mib=mib,
    )
    send = lax.ppermute(send, "rows", [(i, i ^ 1) for i in range(n_rows)])
    out, norms = call(
        end_kernel,
        (sds((n_tok, tok, 128), bf16), sds((h, 128), f32)),
        landmark_index,
        vecs,
        params[2],
        params[4],
        *later,
        mib=mib,
    )
    def from_xor(array, m):
        return lax.ppermute(array, "rows", [(i, i ^ m) for i in range(n_rows)])

    total = (keep + send + norms).astype(bf16)
    back = jnp.concatenate([out, jnp.broadcast_to(total, (n_tok, h, 128))], 1)
    got = lax.all_to_all(back, "tok", 0, 0, tiled=True)
    mine = call(partial(sum_kernel, tok), sds((h, 128), bf16), got)
    parts = [mine] + [from_xor(mine, m) for m in reversed(range(1, n_rows))][::-1]
    layer_out, grad_input = call(
        rows_kernel, (sds((rows, tok, width), bf16), sds((rows, tok, width), f32)), got
    )
    sums = call(
        partial(unpack_kernel, n_rows), tuple(sds(p.shape, f32) for p in params), *parts
    )
    sums = sums[:14] + (sums[14].T,) + sums[15:]
    return (layer_out, grad_input) + tuple(sums)


def solution(mesh):
    split3 = P("rows", "tok", None)
    return jax.shard_map(
        shards,
        mesh=mesh,
        in_specs=(split3, P("rows", "tok"), P("rows", None, None)) + (P(),) * 16 + (split3,),
        out_specs=(split3, split3) + (P(),) * 16,
        check_vma=False,
    )
```
